128 devices in a mesh: row: 8 (over x, core), col: 16 (over y, z).
Axes of the slice: x: 4, y: 4, z: 4, core: 2. Of those that a mesh axis runs over, the one named last changes fastest.
Arguments:
- features: bfloat16 [256, 256, 1280], P('row', 'col'), may hold values from -6 to 6
- known: bfloat16 [256, 256, 1280], P('row', 'col'), may hold values from -6 to 6
- known_mask: int32 [256, 256], P('row', 'col'), may hold values 0 or 1
- w_query: bfloat16 [1280, 1024], replicated, may hold values from -2 to 2
- w_keyval: bfloat16 [1280, 2048], replicated, may hold values from -2 to 2
- w_out: bfloat16 [1024, 1280], replicated, may hold values from -0.75 to 0.75
- win_anchor: int32 [8, 16, 6, 2], P('row', 'col'), may hold values from -8 to 24, as said below
- win_weight: int32 [8, 16, 6], P('row', 'col'), may hold values from 0 to 3, as said below
Outputs:
- output: bfloat16 [256, 256, 1280], P('row', 'col')
The draws below stay inside these ranges and needn't reach their ends.
Inputs may be any that keep to these rules, and one draw needn't show every extreme that they name: `win_anchor`: A window of 16 x 16 cells starting at its anchor lies inside the canvas and within 8 cells of its tile on every side. `win_weight`: in each tile's list the slots of nonzero weight come first; every tile has 1 to 6 of them, and some tile has all 6.
All inputs are finite; a program needn't handle non-finite values. No bound on the sum of `known_mask` on one device may be relied on, other than what follows from the above.
Results may differ from the reference program's by a relative error of at most 0.012.
Values may be sent and summed in bfloat16 or wider, within the bound.
No kernel may reach another device: no remote copies, remote signals or barrier semaphores. Data moves between devices by JAX's collectives and lax.ppermute only.
A program may use at most 128 MiB of HBM per device.

```python
import math
import jax
import jax.numpy as jnp
from jax import lax

C = 1280
HEADS = 16
HD = 64
STRIDE = 4
WIN = 16
HALO = 8
TH = 32
TW = 16
MAXW = 6
MAP_H = 256
MAP_W = 256


def shared_normal(key):
    return jnp.clip(jax.random.normal(key, (C, HEADS * HD), jnp.float32), -4.0, 4.0)


def draw_features(key, part):
    key = jax.random.fold_in(key, 15)
    key_noise = jax.random.fold_in(key, 0)
    noise = jnp.clip(jax.random.normal(key_noise, (MAP_H, MAP_W, C), jnp.float32), -6.0, 6.0)
    result = noise
    return result.astype(jnp.bfloat16)


def draw_w_query(key, part):
    base = shared_normal(key)
    return (base * (C // 4) ** (-0.5)).astype(jnp.bfloat16)


def draw_w_keyval(key, part):
    key = jax.random.fold_in(key, 14)
    key_keys, key_values = jax.random.split(key)
    own = jnp.clip(jax.random.normal(key_keys, (C, HEADS * HD), jnp.float32), -4.0, 4.0)
    key_part = own
    value_part = jnp.clip(jax.random.normal(key_values, (C, HEADS * HD), jnp.float32), -4.0, 4.0)
    return (jnp.concatenate([key_part, value_part], 1) * C ** (-0.5)).astype(jnp.bfloat16)


def draw_win_anchor(key, part):
    key = jax.random.fold_in(key, 11)
    tile_count_rows = MAP_H // TH
    tile_count_cols = MAP_W // TW
    shape_all = (tile_count_rows, tile_count_cols, MAXW)
    row_index = jnp.broadcast_to(jnp.arange(tile_count_rows).reshape(tile_count_rows, 1, 1), shape_all)
    col_index = jnp.broadcast_to(jnp.arange(tile_count_cols).reshape(1, tile_count_cols, 1), shape_all)
    low_rows = jnp.where(row_index > 0, 0 - HALO, 0)
    high_rows = jnp.where(row_index < tile_count_rows - 1, TH - WIN + HALO, TH - WIN)
    low_cols = jnp.where(col_index > 0, 0 - HALO, 0)
    high_cols = jnp.where(col_index < tile_count_cols - 1, TW - WIN + HALO, TW - WIN)
    key_rows, key_cols = jax.random.split(key)
    anchor_rows = jax.random.randint(key_rows, shape_all, low_rows, high_rows + 1)
    anchor_cols = jax.random.randint(key_cols, shape_all, low_cols, high_cols + 1)
    return jnp.stack([anchor_rows, anchor_cols], -1).astype(jnp.int32)


def draw_win_weight(key, part):
    key = jax.random.fold_in(key, 12)
    tile_count_rows = MAP_H // TH
    tile_count_cols = MAP_W // TW
    key_small, key_heavy, key_forced, key_levels = jax.random.split(key, 4)
    smaller = jax.random.randint(key_small, (tile_count_rows, tile_count_cols), 1, max(MAXW // 2, 1) + 1)
    heavy = jax.random.randint(key_heavy, (tile_count_rows, tile_count_cols), 0, 8) == 0
    forced = jax.random.randint(key_forced, (), 0, tile_count_rows * tile_count_cols)
    tile_ids = jnp.arange(tile_count_rows * tile_count_cols).reshape(tile_count_rows, tile_count_cols)
    live_count = jnp.where(heavy | (tile_ids == forced), MAXW, smaller)
    levels = jax.random.randint(key_levels, (tile_count_rows, tile_count_cols, MAXW), 1, 4)
    slot_ids = jnp.arange(MAXW).reshape(1, 1, MAXW)
    return jnp.where(slot_ids < live_count[..., None], levels, 0).astype(jnp.int32)


def plant(values, rng, smallest, high):
    longest = values.shape.index(max(values.shape))
    spots = []
    for shift in (0, 1):
        where = [jax.random.randint(jax.random.fold_in(rng, axis), (), 0, length) for axis, length in enumerate(values.shape)]
        where[longest] = (where[longest] + shift) % values.shape[longest]
        spots.append(tuple(where))
    return values.at[spots[0]].set(smallest).at[spots[1]].set(high)


def block_scale(own_key, dims, cuts, low, high):
    factor_of = 1.0
    for position, blocks in cuts:
        draws = jax.random.uniform(jax.random.fold_in(jax.random.fold_in(own_key, 6), position), (blocks,), jnp.float32, low / len(cuts), high / len(cuts))
        factor_of = factor_of * jnp.repeat(jnp.exp(draws), dims[position] // blocks).reshape((-1,) + (1,) * (len(dims) - 1 - position))
    return factor_of


def scatter_about(own_key, extent, scale, limit, cuts=(), kind=jnp.bfloat16):
    entries = jax.random.normal(own_key, extent, jnp.float32) * scale
    if len(cuts) > 0:
        entries = block_scale(own_key, extent, cuts, -0.22, 0.18) * entries
    return jnp.clip(entries, min=-limit, max=limit).astype(kind)


def setup_inputs(seed: int = 0) -> dict:
    arg_keys = jax.random.split(jax.random.key(seed), 9)
    return {
        "features": draw_features(jax.random.fold_in(arg_keys[8], 71), 0),
        "known": scatter_about(arg_keys[1], (MAP_H, MAP_W, C), 1.0, 6.0, ((0, 8), (1, 16))),
        "known_mask": plant((jax.random.randint(arg_keys[2], (MAP_H, MAP_W), 0, 3) < 1).astype(jnp.int32), jax.random.fold_in(arg_keys[2], 1), 0, 1),
        "w_query": draw_w_query(jax.random.fold_in(arg_keys[8], 71), 0),
        "w_keyval": draw_w_keyval(jax.random.fold_in(arg_keys[8], 71), 0),
        "w_out": scatter_about(arg_keys[5], (HEADS * HD, C), (HEADS * HD // 16) ** -0.5, 0.75),
        "win_anchor": draw_win_anchor(jax.random.fold_in(arg_keys[8], 71), 0),
        "win_weight": draw_win_weight(jax.random.fold_in(arg_keys[8], 71), 0),
    }


def softmax_mix(queries, keys, values):
    scores = jnp.einsum("qhd,khd->hqk", queries.astype(jnp.float32), keys.astype(jnp.float32)) * (HD ** -0.5)
    highest = jnp.max(scores, axis=-1, keepdims=True)
    expsum = jnp.exp(scores - highest)
    weights_bf = (expsum / jnp.sum(expsum, axis=-1, keepdims=True)).astype(jnp.bfloat16)
    return jnp.einsum("hqk,khd->qhd", weights_bf.astype(jnp.float32), values.astype(jnp.float32))


def lattice_branch(queries, keys, values):
    row_count = queries.shape[0]
    block_rows = math.gcd(row_count, 512)
    grouped = queries.reshape(row_count // block_rows, block_rows, HEADS, HD)

    def one_block(query_block):
        return softmax_mix(query_block, keys, values).astype(jnp.bfloat16)

    return lax.map(one_block, grouped).reshape(row_count, HEADS, HD)


def to_lattice(field):
    trailing = field.shape[2:]
    shaped = field.reshape((MAP_H // STRIDE, STRIDE, MAP_W // STRIDE, STRIDE) + trailing)
    axes_order = (1, 3, 0, 2) + tuple(range(4, 4 + len(trailing)))
    return jnp.transpose(shaped, axes_order).reshape((STRIDE * STRIDE, (MAP_H // STRIDE) * (MAP_W // STRIDE)) + trailing)


def from_lattice(lattice):
    trailing = lattice.shape[2:]
    shaped = lattice.reshape((STRIDE, STRIDE, MAP_H // STRIDE, MAP_W // STRIDE) + trailing)
    axes_order = (2, 0, 3, 1) + tuple(range(4, 4 + len(trailing)))
    return jnp.transpose(shaped, axes_order).reshape((MAP_H, MAP_W) + trailing)


def reference(features, known, known_mask, w_query, w_keyval, w_out, win_anchor, win_weight):
    inner = HEADS * HD
    flat = features.reshape(MAP_H * MAP_W, C)
    queries = jnp.dot(flat, w_query, preferred_element_type=jnp.float32).astype(jnp.bfloat16)
    keyvals = jnp.dot(flat, w_keyval, preferred_element_type=jnp.float32).astype(jnp.bfloat16)
    queries = queries.reshape(MAP_H, MAP_W, HEADS, HD)
    keys = keyvals[:, :inner].reshape(MAP_H, MAP_W, HEADS, HD)
    values = keyvals[:, inner:].reshape(MAP_H, MAP_W, HEADS, HD)

    def lattice_one(triple):
        return lattice_branch(triple[0], triple[1], triple[2])

    lattice = lax.map(lattice_one, (to_lattice(queries), to_lattice(keys), to_lattice(values)))
    dilated = from_lattice(lattice).reshape(MAP_H, MAP_W, inner)

    tile_count_rows = MAP_H // TH
    tile_count_cols = MAP_W // TW
    base_rows = (jnp.arange(tile_count_rows) * TH).astype(jnp.int32).reshape(tile_count_rows, 1, 1)
    base_cols = (jnp.arange(tile_count_cols) * TW).astype(jnp.int32).reshape(1, tile_count_cols, 1)
    top_rows = (win_anchor[..., 0] + base_rows).astype(jnp.int32).reshape(-1)
    left_cols = (win_anchor[..., 1] + base_cols).astype(jnp.int32).reshape(-1)
    factors = win_weight.reshape(-1).astype(jnp.float32)
    zero_index = jnp.zeros((), jnp.int32)

    def add_window(carry, item):
        summed, coverage = carry
        top_row, left_col, factor = item
        corner = (top_row, left_col, zero_index, zero_index)
        window_q = lax.dynamic_slice(queries, corner, (WIN, WIN, HEADS, HD)).reshape(WIN * WIN, HEADS, HD)
        window_k = lax.dynamic_slice(keys, corner, (WIN, WIN, HEADS, HD)).reshape(WIN * WIN, HEADS, HD)
        window_v = lax.dynamic_slice(values, corner, (WIN, WIN, HEADS, HD)).reshape(WIN * WIN, HEADS, HD)
        result = softmax_mix(window_q, window_k, window_v).reshape(WIN, WIN, inner)
        current = lax.dynamic_slice(summed, (top_row, left_col, zero_index), (WIN, WIN, inner))
        summed = lax.dynamic_update_slice(summed, current + factor * result, (top_row, left_col, zero_index))
        cover_now = lax.dynamic_slice(coverage, (top_row, left_col), (WIN, WIN))
        coverage = lax.dynamic_update_slice(coverage, cover_now + factor, (top_row, left_col))
        return (summed, coverage), None

    start_sum = jnp.zeros((MAP_H, MAP_W, inner), jnp.float32)
    start_cover = jnp.zeros((MAP_H, MAP_W), jnp.float32)
    (accum, coverage), unused = lax.scan(add_window, (start_sum, start_cover), (top_rows, left_cols, factors))
    blended = ((dilated.astype(jnp.float32) + accum) / (1.0 + coverage)[..., None]).astype(jnp.bfloat16)
    projected = jnp.dot(blended.reshape(MAP_H * MAP_W, inner), w_out, preferred_element_type=jnp.float32)
    computed = (features.astype(jnp.float32) + projected.reshape(MAP_H, MAP_W, C)).astype(jnp.bfloat16)
    return jnp.where(known_mask[..., None] == 1, known, computed)
```

```python
import functools
import math

import jax
import jax.numpy as jnp
from jax import lax
from jax.experimental import pallas as pl
from jax.experimental.pallas import tpu as pltpu
from jax.sharding import PartitionSpec as P

HD = 64
STRIDE = 4
WIN = 16
HALO = 8
SUBS = STRIDE * STRIDE
LANES = 128
SCALE = HD**-0.5 * math.log2(math.e)
FREE_RANGE = 100.0
VROWS = 80
QBLOCK = 1024
KBLOCK = 256
BF16 = jnp.bfloat16
F32 = jnp.float32
VMEM_LIMIT = 58 * 2**20


def dot(a, b):
    return jnp.dot(a, b, preferred_element_type=F32)


def dot_nt(a, b):
    return lax.dot_general(a, b, (((1,), (1,)), ((), ())), preferred_element_type=F32)


def whole(shape):
    return pl.BlockSpec(shape, lambda *_: (0,) * len(shape))


def lattice_order(count, by_row):
    lattice = lax.broadcasted_iota(jnp.int32, (count, count), 0 if by_row else 1)
    cell = lax.broadcasted_iota(jnp.int32, (count, count), 1 if by_row else 0)
    per_sub = count // SUBS
    tile_cols = 16
    sub, place = lattice // per_sub, lattice % per_sub
    across = tile_cols // STRIDE
    row = (place // across) * STRIDE + sub // STRIDE
    col = (place % across) * STRIDE + sub % STRIDE
    return jnp.where(cell == row * tile_cols + col, 1.0, 0.0).astype(BF16)


def project_kernel(x_ref, wq_ref, wk_ref, wv_ref, out_ref, ordered):
    count = x_ref.shape[0]

    @pl.when(pl.program_id(0) == 0)
    def _():
        ordered[...] = dot(lattice_order(count, True), x_ref[...]).astype(BF16)

    x = ordered[...]
    for part, w_ref in enumerate((wq_ref, wk_ref, wv_ref)):
        y = dot(x, w_ref[...]).astype(BF16)
        for g in range(2):
            out_ref[:, g, :, part * LANES : (part + 1) * LANES] = y[
                :, g * LANES : (g + 1) * LANES
            ].reshape(SUBS, count // SUBS, LANES)


def project(x, w_query, w_keyval):
    count, channels = x.shape
    inner = w_query.shape[1]
    groups = inner // LANES
    steps = groups // 2
    per_sub = count // SUBS
    return pl.pallas_call(
        project_kernel,
        grid=(steps,),
        in_specs=[
            whole(x.shape),
            pl.BlockSpec((channels, 2 * LANES), lambda g: (0, g)),
            pl.BlockSpec((channels, 2 * LANES), lambda g: (0, g)),
            pl.BlockSpec((channels, 2 * LANES), lambda g: (0, g + steps)),
        ],
        out_specs=pl.BlockSpec((SUBS, 2, per_sub, 3 * LANES), lambda g: (0, g, 0, 0)),
        out_shape=jax.ShapeDtypeStruct((SUBS, groups, per_sub, 3 * LANES), BF16),
        scratch_shapes=[pltpu.VMEM((count, channels), BF16)],
        compiler_params=pltpu.CompilerParams(vmem_limit_bytes=VMEM_LIMIT),
        cost_estimate=pl.CostEstimate(
            flops=2 * count * channels * 3 * inner,
            bytes_accessed=2 * (3 * channels * inner + count * channels + 3 * count * inner),
            transcendentals=0,
        ),
        name="project",
    )(x, w_query, w_keyval, w_keyval)


def lattice_kernel(x_ref, o_ref, keys, queries_t, values_t, free):
    count = x_ref.shape[0]
    step = pl.program_id(0)
    block = o_ref.shape[0]

    @pl.when(step == 0)
    def _():
        q_t = x_ref[:, 0:LANES].astype(F32).T
        k_all = x_ref[:, LANES : 2 * LANES].astype(F32)
        v_t = x_ref[:, 2 * LANES : 3 * LANES].astype(F32).T.astype(BF16)
        worst = jnp.float32(0)
        for h in range(2):
            head = slice(h * HD, (h + 1) * HD)
            q, k = q_t[head, :], k_all[:, head]
            bound = jnp.max(jnp.sum(q * q, axis=0)) * jnp.max(jnp.sum(k * k, axis=1))
            worst = jnp.maximum(worst, bound)
            queries_t[h] = q.astype(BF16)
            keys[h] = k.astype(BF16)
            values_t[h, 0:HD] = v_t[head, :]
            values_t[h, HD:VROWS] = jnp.ones((VROWS - HD, count), BF16)
        free[0] = (worst * (SCALE * SCALE) <= FREE_RANGE * FREE_RANGE).astype(jnp.int32)

    cols = pl.ds(pl.multiple_of(step * block, block), block)

    def finish(sums):
        out = jnp.concatenate([s[:HD] / s[HD : HD + 1] for s in sums], 0)
        o_ref[...] = out.T.astype(BF16)

    @pl.when(free[0] == 1)
    def _():
        items = [(h, c) for h in range(2) for c in range(0, count, KBLOCK)]

        def score(i):
            h, c = items[i]
            return dot(keys[h, c : c + KBLOCK, :], queries_t[h, :, cols])

        sums = [None, None]
        later = score(0)
        for i, (h, c) in enumerate(items):
            now = later
            if i + 1 < len(items):
                later = score(i + 1)
            weights = jnp.exp2(now * SCALE).astype(BF16)
            part = dot(values_t[h, :, c : c + KBLOCK], weights)
            sums[h] = part if sums[h] is None else sums[h] + part
        finish(sums)

    @pl.when(free[0] == 0)
    def _():
        chunks = count // KBLOCK
        sums = []
        for h in range(2):
            q = queries_t[h, :, cols]

            def score(c, h=h, q=q):
                return dot(keys[h, pl.ds(pl.multiple_of(c * KBLOCK, KBLOCK), KBLOCK), :], q)

            def top(c, m, score=score):
                return jnp.maximum(m, jnp.max(score(c), axis=0, keepdims=True))

            m = lax.fori_loop(0, chunks, top, jnp.full((1, block), -jnp.inf, F32))

            def add(c, total, score=score, m=m, h=h):
                weights = jnp.exp2((score(c) - m) * SCALE).astype(BF16)
                rows = pl.ds(pl.multiple_of(c * KBLOCK, KBLOCK), KBLOCK)
                return total + dot(values_t[h, :, rows], weights)

            sums.append(lax.fori_loop(0, chunks, add, jnp.zeros((VROWS, block), F32)))
        finish(sums)


def lattice_attend(x):
    count = x.shape[0]
    return pl.pallas_call(
        lattice_kernel,
        grid=(count // QBLOCK,),
        in_specs=[whole(x.shape)],
        out_specs=pl.BlockSpec((QBLOCK, LANES), lambda i: (i, 0)),
        out_shape=jax.ShapeDtypeStruct((count, LANES), BF16),
        scratch_shapes=[
            pltpu.VMEM((2, count, HD), BF16),
            pltpu.VMEM((2, HD, count), BF16),
            pltpu.VMEM((2, VROWS, count), BF16),
            pltpu.SMEM((1,), jnp.int32),
        ],
        compiler_params=pltpu.CompilerParams(vmem_limit_bytes=VMEM_LIMIT),
        cost_estimate=pl.CostEstimate(
            flops=8 * 4 * count * count * HD,
            bytes_accessed=8 * count * LANES,
            transcendentals=2 * count * count,
        ),
        name="lattice_attend",
    )(x)


def windows_kernel(
    anchor, weight, mid_ref, side_ref, wq_ref, wkv_ref, top_out, bottom_out, mid_out, side_out,
    mid_sum, side_sum, results,
):
    inner = wq_ref.shape[1]
    channels = wq_ref.shape[0]
    cells = WIN * WIN
    wide = inner + LANES
    tile_rows = mid_out.shape[0]
    mid_sum[...] = jnp.zeros(mid_sum.shape, F32)
    side_sum[...] = jnp.zeros(side_sum.shape, F32)
    results[:, inner:wide] = jnp.ones((cells, LANES), BF16)
    slots = weight.shape[0]
    live = sum((weight[s] > 0).astype(jnp.int32) for s in range(slots))
    first = lax.broadcasted_iota(jnp.int32, (cells, LANES), 1) < HD
    ones = jnp.ones((cells, LANES), BF16)

    def one_hot(window_dim, left, offset):
        window = lax.broadcasted_iota(jnp.int32, (cells, cells), window_dim)
        source = lax.broadcasted_iota(jnp.int32, (cells, cells), 1 - window_dim)
        place = ((window & (WIN - 1)) + left) & (2 * WIN - 1)
        same = ((window >> 4) == (source >> 4)) & (place == (source & (WIN - 1)) + offset)
        return jnp.where(same, 1.0, 0.0)

    def one_window(slot, carry):
        top = anchor[slot, 0] + HALO
        left = anchor[slot, 1]
        factor = weight[slot].astype(F32)
        rows = pl.ds(top, WIN)
        mid = mid_ref[rows].reshape(cells, channels)
        side = side_ref[rows].reshape(cells, channels)
        x = dot(one_hot(0, left, 0).astype(BF16), mid) + dot(one_hot(0, left, WIN).astype(BF16), side)
        x = x.astype(BF16)
        for g in range(0, inner, 2 * LANES):
            q2 = dot(x, wq_ref[:, g : g + 2 * LANES]).astype(BF16)
            k2 = dot(x, wkv_ref[:, g : g + 2 * LANES]).astype(BF16)
            v2 = dot(x, wkv_ref[:, inner + g : inner + g + 2 * LANES]).astype(BF16)
            for pair in range(2):
                lanes = slice(pair * LANES, (pair + 1) * LANES)
                q, k, v = q2[:, lanes], k2[:, lanes], v2[:, lanes]
                v = jnp.concatenate([v, ones], 1)
                mixed = []
                for h in range(2):
                    own = jnp.where(first if h == 0 else ~first, q, jnp.zeros_like(q))
                    s = dot_nt(own, k)
                    e = jnp.exp2((s - jnp.max(s, axis=1, keepdims=True)) * SCALE).astype(BF16)
                    o = dot(e, v)
                    mixed.append(o[:, :LANES] / o[:, LANES:])
                results[:, g + pair * LANES : g + (pair + 1) * LANES] = jnp.where(
                    first, mixed[0], mixed[1]
                ).astype(BF16)
        r = results[...]
        to_mid = (one_hot(1, left, 0) * factor).astype(BF16)
        to_side = (one_hot(1, left, WIN) * factor).astype(BF16)
        mid_sum[rows] += dot(to_mid, r).reshape(WIN, WIN, wide)
        side_sum[rows] += dot(to_side, r).reshape(WIN, WIN, wide)
        return carry

    lax.fori_loop(0, live, one_window, 0)
    end = tile_rows + HALO
    top_out[:, 0:WIN] = mid_sum[0:HALO].astype(BF16)
    top_out[:, WIN : 2 * WIN] = side_sum[0:HALO].astype(BF16)
    bottom_out[:, 0:WIN] = mid_sum[end : end + HALO].astype(BF16)
    bottom_out[:, WIN : 2 * WIN] = side_sum[end : end + HALO].astype(BF16)
    mid_out[...] = mid_sum[HALO:end]
    side_out[...] = side_sum[HALO:end]


def windows(mid, side, w_query, w_keyval, anchor, weight):
    high, tile_cols, channels = mid.shape
    inner = w_query.shape[1]
    wide = inner + LANES
    tile_rows = high - 2 * HALO
    vmem = pl.BlockSpec(memory_space=pltpu.VMEM)
    smem = pl.BlockSpec(memory_space=pltpu.SMEM)
    rim = jax.ShapeDtypeStruct((HALO, 2 * WIN, wide), BF16)
    inside = jax.ShapeDtypeStruct((tile_rows, WIN, wide), F32)
    slots = weight.shape[0]
    cells = WIN * WIN
    return pl.pallas_call(
        windows_kernel,
        in_specs=[smem, smem, vmem, vmem, vmem, vmem],
        out_specs=[vmem] * 4,
        out_shape=[rim, rim, inside, inside],
        scratch_shapes=[
            pltpu.VMEM((high, WIN, wide), F32),
            pltpu.VMEM((high, WIN, wide), F32),
            pltpu.VMEM((cells, wide), BF16),
        ],
        compiler_params=pltpu.CompilerParams(vmem_limit_bytes=VMEM_LIMIT),
        cost_estimate=pl.CostEstimate(
            flops=slots * 2 * cells * 3 * inner * (channels + 2 * cells),
            bytes_accessed=6 * channels * inner + 4 * high * tile_cols * channels,
            transcendentals=slots * cells * cells * inner // HD,
        ),
        name="windows",
    )(anchor, weight, mid, side, w_query, w_keyval)


def blend_kernel(
    x_ref, known_ref, mask_ref, mixed_ref, mid_ref, above_ref, below_ref, beside_ref, w_ref, out_ref,
    blended,
):
    count = x_ref.shape[0]
    inner = blended.shape[1]
    wide = inner + LANES

    @pl.when(pl.program_id(0) == 0)
    def _():
        groups = mixed_ref.shape[1]
        tile_rows = mid_ref.shape[0]
        back = lattice_order(count, False)

        def total(lanes):
            upper = above_ref[:, 0:WIN, lanes].astype(F32)
            lower = below_ref[:, 0:WIN, lanes].astype(F32)
            middle = mid_ref[:, :, lanes] + beside_ref[:, :, lanes].astype(F32)
            parts = [
                middle[:HALO] + upper,
                middle[HALO : tile_rows - HALO],
                middle[tile_rows - HALO :] + lower,
            ]
            return jnp.concatenate(parts, 0).reshape(count, -1)

        share = 1.0 / (1.0 + total(slice(inner, wide)))
        share = jnp.concatenate([share, share], 1)
        for g in range(0, groups, 2):
            lanes = slice(g * LANES, (g + 2) * LANES)
            mixed = jnp.concatenate(
                [mixed_ref[:, g + j].reshape(count, LANES) for j in range(2)], 1
            )
            blended[:, lanes] = ((dot(back, mixed) + total(lanes)) * share).astype(BF16)

    width = out_ref.shape[1]
    y = (x_ref[...].astype(F32) + dot(blended[...], w_ref[...])).astype(BF16)
    mask = jnp.concatenate([mask_ref[...]] * (width // LANES), 1)
    out_ref[...] = jnp.where(mask == 1, known_ref[...], y)


def blend(x, known, mask, mixed, mid, above, below, beside, w_out):
    count, channels = x.shape
    inner = w_out.shape[0]
    width = 2 * LANES
    by_cols = pl.BlockSpec((count, width), lambda i: (0, i))
    return pl.pallas_call(
        blend_kernel,
        grid=(channels // width,),
        in_specs=[by_cols, by_cols]
        + [whole(a.shape) for a in (mask, mixed, mid, above, below, beside)]
        + [pl.BlockSpec((inner, width), lambda i: (0, i))],
        out_specs=by_cols,
        out_shape=jax.ShapeDtypeStruct((count, channels), BF16),
        scratch_shapes=[pltpu.VMEM((count, inner), BF16)],
        compiler_params=pltpu.CompilerParams(vmem_limit_bytes=VMEM_LIMIT),
        cost_estimate=pl.CostEstimate(
            flops=2 * count * inner * (channels + count),
            bytes_accessed=2 * inner * channels + 6 * count * channels,
            transcendentals=0,
        ),
        name="blend",
    )(x, known, mask, mixed, mid, above, below, beside, w_out)


def exchange(pieces):
    return lax.all_to_all(pieces, ("row", "col"), split_axis=0, concat_axis=0, tiled=True)


def neighbours(axis):
    peers = lax.axis_size(axis)
    onward = [(i, i + 1) for i in range(peers - 1)]
    return onward, [(j, i) for i, j in onward]


def on_device(features, known, known_mask, w_query, w_keyval, w_out, win_anchor, win_weight):
    tile_rows, tile_cols, channels = features.shape
    count = tile_rows * tile_cols
    per_sub = count // SUBS
    inner = w_query.shape[1]
    devices = lax.axis_size("row") * lax.axis_size("col")
    down, up = neighbours("row")
    right, left = neighbours("col")
    x = features.reshape(count, channels)

    before = lax.ppermute(features[tile_rows - HALO :], "row", down)
    after = lax.ppermute(features[:HALO], "row", up)
    pieces = project(x, w_query, w_keyval).reshape(devices, per_sub, 3 * LANES)
    mid = jnp.concatenate([before, features, after], 0)
    from_right = lax.ppermute(mid[:, :HALO], "col", left)
    from_left = lax.ppermute(mid[:, tile_cols - HALO :], "col", right)
    side = jnp.concatenate([from_right, from_left], 1)

    gathered = exchange(pieces).reshape(devices * per_sub, 3 * LANES)

    top, bottom, inside, beside = windows(
        mid, side, w_query, w_keyval, win_anchor.reshape(-1, 2), win_weight.reshape(-1)
    )
    above = lax.ppermute(bottom, "row", down)
    below = lax.ppermute(top, "row", up)
    beside = jnp.concatenate(
        [
            beside[:HALO] + above[:, WIN:].astype(F32),
            beside[HALO : tile_rows - HALO],
            beside[tile_rows - HALO :] + below[:, WIN:].astype(F32),
        ],
        0,
    ).astype(BF16)
    on_first = lax.ppermute(beside[:, :HALO], "col", right)
    on_last = lax.ppermute(beside[:, HALO:], "col", left)
    arrived = jnp.concatenate([on_first, on_last], 1)

    mixed = lattice_attend(gathered)
    returned = exchange(mixed.reshape(devices, per_sub, LANES))
    returned = returned.reshape(SUBS, devices // SUBS, per_sub, LANES)
    mask = jnp.broadcast_to(known_mask.reshape(count, 1), (count, LANES))
    out = blend(
        x, known.reshape(count, channels), mask, returned, inside, above, below, arrived, w_out
    )
    return out.reshape(tile_rows, tile_cols, channels)


def solution(mesh):
    in_specs = (
        P("row", "col", None),
        P("row", "col", None),
        P("row", "col"),
        P(),
        P(),
        P(),
        P("row", "col", None, None),
        P("row", "col", None),
    )
    out_specs = P("row", "col", None)
    return jax.shard_map(
        on_device, mesh=mesh, in_specs=in_specs, out_specs=out_specs, check_vma=False
    )
```

```python
import functools
import math

import jax
import jax.numpy as jnp
from jax import lax
from jax.experimental import pallas as pl
from jax.experimental.pallas import tpu as pltpu
from jax.sharding import PartitionSpec as P

HD = 64
STRIDE = 4
WIN = 16
HALO = 8
SUBS = STRIDE * STRIDE
LANES = 128
SCALE = HD**-0.5 * math.log2(math.e)
FREE_RANGE = 100.0
VROWS = 80
QBLOCK = 1024
KBLOCK = 256
BF16 = jnp.bfloat16
F32 = jnp.float32


def dot(a, b):
    return jnp.dot(a, b, preferred_element_type=F32)


def dot_nt(a, b):
    return lax.dot_general(a, b, (((1,), (1,)), ((), ())), preferred_element_type=F32)


def whole(shape):
    return pl.BlockSpec(shape, lambda *_: (0,) * len(shape), pipeline_mode=pl.Buffered(1))


PARAMS = pltpu.CompilerParams(vmem_limit_bytes=58 * 2**20)


def lattice_order(count, by_row):
    lattice = lax.broadcasted_iota(jnp.int32, (count, count), 0 if by_row else 1)
    cell = lax.broadcasted_iota(jnp.int32, (count, count), 1 if by_row else 0)
    per_sub = count // SUBS
    tile_cols = 16
    sub, place = lattice // per_sub, lattice % per_sub
    across = tile_cols // STRIDE
    row = (place // across) * STRIDE + sub // STRIDE
    col = (place % across) * STRIDE + sub % STRIDE
    return jnp.where(cell == row * tile_cols + col, 1.0, 0.0).astype(BF16)


def project_kernel(x_ref, wq_ref, wk_ref, wv_ref, out_ref, ordered):
    count = x_ref.shape[0]

    @pl.when(pl.program_id(0) == 0)
    def _():
        ordered[...] = dot(lattice_order(count, True), x_ref[...]).astype(BF16)

    x = ordered[...]
    for part, w_ref in enumerate((wq_ref, wk_ref, wv_ref)):
        y = dot(x, w_ref[...]).astype(BF16)
        for g in range(2):
            out_ref[:, g, :, part * LANES : (part + 1) * LANES] = y[
                :, g * LANES : (g + 1) * LANES
            ].reshape(SUBS, count // SUBS, LANES)


def project(x, w_query, w_keyval):
    count, channels = x.shape
    inner = w_query.shape[1]
    groups = inner // LANES
    steps = groups // 2
    per_sub = count // SUBS
    return pl.pallas_call(
        project_kernel,
        grid=(steps,),
        in_specs=[
            whole(x.shape),
            pl.BlockSpec((channels, 2 * LANES), lambda g: (0, g)),
            pl.BlockSpec((channels, 2 * LANES), lambda g: (0, g)),
            pl.BlockSpec((channels, 2 * LANES), lambda g: (0, g + steps)),
        ],
        out_specs=pl.BlockSpec((SUBS, 2, per_sub, 3 * LANES), lambda g: (0, g, 0, 0)),
        out_shape=jax.ShapeDtypeStruct((SUBS, groups, per_sub, 3 * LANES), BF16),
        scratch_shapes=[pltpu.VMEM((count, channels), BF16)],
        compiler_params=PARAMS,
        cost_estimate=pl.CostEstimate(
            flops=2 * count * channels * 3 * inner,
            bytes_accessed=2 * (3 * channels * inner + count * channels + 3 * count * inner),
            transcendentals=0,
        ),
        name="project",
    )(x, w_query, w_keyval, w_keyval)


def lattice_kernel(x_ref, o_ref, keys, queries_t, values_t, free):
    count = x_ref.shape[0]
    step = pl.program_id(0)
    block = o_ref.shape[0]

    @pl.when(step == 0)
    def _():
        q_t = x_ref[:, 0:LANES].astype(F32).T
        k_all = x_ref[:, LANES : 2 * LANES].astype(F32)
        v_t = x_ref[:, 2 * LANES : 3 * LANES].astype(F32).T.astype(BF16)
        worst = jnp.float32(0)
        for h in range(2):
            head = slice(h * HD, (h + 1) * HD)
            q, k = q_t[head, :], k_all[:, head]
            bound = jnp.max(jnp.sum(q * q, axis=0)) * jnp.max(jnp.sum(k * k, axis=1))
            worst = jnp.maximum(worst, bound)
            queries_t[h] = q.astype(BF16)
            keys[h] = k.astype(BF16)
            values_t[h, 0:HD] = v_t[head, :]
            values_t[h, HD:VROWS] = jnp.ones((VROWS - HD, count), BF16)
        free[0] = (worst * (SCALE * SCALE) <= FREE_RANGE * FREE_RANGE).astype(jnp.int32)

    cols = pl.ds(pl.multiple_of(step * block, block), block)

    def finish(sums):
        out = jnp.concatenate([s[:HD] / s[HD : HD + 1] for s in sums], 0)
        o_ref[...] = out.T.astype(BF16)

    @pl.when(free[0] == 1)
    def _():
        items = [(h, c) for h in range(2) for c in range(0, count, KBLOCK)]

        def score(i):
            h, c = items[i]
            return dot(keys[h, c : c + KBLOCK, :], queries_t[h, :, cols])

        sums = [None, None]
        later = score(0)
        for i, (h, c) in enumerate(items):
            now = later
            if i + 1 < len(items):
                later = score(i + 1)
            weights = jnp.exp2(now * SCALE).astype(BF16)
            part = dot(values_t[h, :, c : c + KBLOCK], weights)
            sums[h] = part if sums[h] is None else sums[h] + part
        finish(sums)

    @pl.when(free[0] == 0)
    def _():
        chunks = count // KBLOCK
        sums = []
        for h in range(2):
            q = queries_t[h, :, cols]

            def score(c, h=h, q=q):
                return dot(keys[h, pl.ds(pl.multiple_of(c * KBLOCK, KBLOCK), KBLOCK), :], q)

            def top(c, m, score=score):
                return jnp.maximum(m, jnp.max(score(c), axis=0, keepdims=True))

            m = lax.fori_loop(0, chunks, top, jnp.full((1, block), -jnp.inf, F32))

            def add(c, total, score=score, m=m, h=h):
                weights = jnp.exp2((score(c) - m) * SCALE).astype(BF16)
                rows = pl.ds(pl.multiple_of(c * KBLOCK, KBLOCK), KBLOCK)
                return total + dot(values_t[h, :, rows], weights)

            sums.append(lax.fori_loop(0, chunks, add, jnp.zeros((VROWS, block), F32)))
        finish(sums)


def lattice_attend(x):
    count = x.shape[0]
    return pl.pallas_call(
        lattice_kernel,
        grid=(count // QBLOCK,),
        in_specs=[whole(x.shape)],
        out_specs=pl.BlockSpec((QBLOCK, LANES), lambda i: (i, 0)),
        out_shape=jax.ShapeDtypeStruct((count, LANES), BF16),
        scratch_shapes=[
            pltpu.VMEM((2, count, HD), BF16),
            pltpu.VMEM((2, HD, count), BF16),
            pltpu.VMEM((2, VROWS, count), BF16),
            pltpu.SMEM((1,), jnp.int32),
        ],
        compiler_params=PARAMS,
        cost_estimate=pl.CostEstimate(
            flops=8 * 4 * count * count * HD,
            bytes_accessed=8 * count * LANES,
            transcendentals=2 * count * count,
        ),
        name="lattice_attend",
    )(x)


def windows_kernel(
    anchor, weight, before_ref, ext_ref, after_ref, wq_ref, wkv_ref, top_out, bottom_out, mid_out,
    side_out, held, mid_sum, side_sum, results_t,
):
    inner = wq_ref.shape[1]
    channels = wq_ref.shape[0]
    cells = WIN * WIN
    wide = inner + LANES
    tile_rows = mid_out.shape[0]
    end = tile_rows + HALO
    held[0:HALO] = before_ref[...]
    held[HALO:end] = ext_ref[...]
    held[end:] = after_ref[...]
    mid_sum[...] = jnp.zeros(mid_sum.shape, F32)
    side_sum[...] = jnp.zeros(side_sum.shape, F32)
    results_t[inner:wide] = jnp.ones((LANES, cells), BF16)
    slots = weight.shape[0]
    live = sum((weight[s] > 0).astype(jnp.int32) for s in range(slots))
    first = lax.broadcasted_iota(jnp.int32, (cells, LANES), 1) < HD
    ones = jnp.ones((VROWS - HD, cells), BF16)

    def one_hot(window_dim, left):
        shape = (cells, 2 * cells) if window_dim == 0 else (2 * cells, cells)
        window = lax.broadcasted_iota(jnp.int32, shape, window_dim)
        source = lax.broadcasted_iota(jnp.int32, shape, 1 - window_dim)
        place = ((window & (WIN - 1)) + left) & (2 * WIN - 1)
        held = (source & (WIN - 1)) + ((source >> 8) << 4)
        same = (((window ^ source) & (cells - WIN)) == 0) & (place == held)
        return jnp.where(same, 1.0, 0.0)

    def one_window(slot, carry):
        top = anchor[slot, 0] + HALO
        left = anchor[slot, 1]
        factor = weight[slot].astype(F32)
        rows = pl.ds(top, WIN)
        source = jnp.concatenate(
            [
                held[rows, 0:WIN].reshape(cells, channels),
                held[rows, WIN : 2 * WIN].reshape(cells, channels),
            ],
            0,
        )
        x = dot(one_hot(0, left).astype(BF16), source).astype(BF16)

        def project(g):
            q = dot(x, wq_ref[:, g : g + 2 * LANES]).astype(BF16)
            k = dot(x, wkv_ref[:, g : g + 2 * LANES]).astype(BF16)
            v = dot(x, wkv_ref[:, inner + g : inner + g + 2 * LANES])
            return q, k, v.T.astype(BF16)

        def scores(q, k, j):
            lanes = slice(j // 2 * LANES, (j // 2 + 1) * LANES)
            own = jnp.where(first if j % 2 == 0 else ~first, q[:, lanes], jnp.zeros((), BF16))
            return dot_nt(k[:, lanes], own)

        def mix(s, v_t, g, j):
            e = jnp.exp2((s - jnp.max(s, axis=0, keepdims=True)) * SCALE).astype(BF16)
            o = dot(jnp.concatenate([v_t[j * HD : (j + 1) * HD], ones], 0), e)
            at = g + j * HD
            results_t[at : at + HD] = (o[:HD] / o[HD : HD + 1]).astype(BF16)

        later = project(0)
        for g in range(0, inner, 2 * LANES):
            q, k, v_t = later
            now = [scores(q, k, j) for j in range(4)]
            if g + 2 * LANES < inner:
                later = project(g + 2 * LANES)
            for j in range(4):
                mix(now[j], v_t, g, j)
        placed = dot_nt((one_hot(1, left) * factor).astype(BF16), results_t[...])
        mid_sum[rows] += placed[:cells].reshape(WIN, WIN, wide)
        side_sum[rows] += placed[cells:].reshape(WIN, WIN, wide)
        return carry

    lax.fori_loop(0, live, one_window, 0)
    top_out[:, 0:WIN] = mid_sum[0:HALO].astype(BF16)
    top_out[:, WIN : 2 * WIN] = side_sum[0:HALO].astype(BF16)
    bottom_out[:, 0:WIN] = mid_sum[end : end + HALO].astype(BF16)
    bottom_out[:, WIN : 2 * WIN] = side_sum[end : end + HALO].astype(BF16)
    mid_out[...] = mid_sum[HALO:end]
    side_out[...] = side_sum[HALO:end]


def windows(before, ext, after, w_query, w_keyval, anchor, weight):
    tile_rows, _, channels = ext.shape
    high = tile_rows + 2 * HALO
    inner = w_query.shape[1]
    wide = inner + LANES
    vmem = pl.BlockSpec(memory_space=pltpu.VMEM)
    smem = pl.BlockSpec(memory_space=pltpu.SMEM)
    rim = jax.ShapeDtypeStruct((HALO, 2 * WIN, wide), BF16)
    inside = jax.ShapeDtypeStruct((tile_rows, WIN, wide), F32)
    slots = weight.shape[0]
    cells = WIN * WIN
    return pl.pallas_call(
        windows_kernel,
        in_specs=[smem, smem] + [vmem] * 5,
        out_specs=[vmem] * 4,
        out_shape=[rim, rim, inside, inside],
        scratch_shapes=[
            pltpu.VMEM((high, 2 * WIN, channels), BF16),
            pltpu.VMEM((high, WIN, wide), F32),
            pltpu.VMEM((high, WIN, wide), F32),
            pltpu.VMEM((wide, cells), BF16),
        ],
        compiler_params=PARAMS,
        cost_estimate=pl.CostEstimate(
            flops=8 * slots * 2 * cells * 3 * inner * (channels + 2 * cells),
            bytes_accessed=6 * channels * inner + 4 * high * WIN * channels,
            transcendentals=slots * cells * cells * inner // HD,
        ),
        name="windows",
    )(anchor, weight, before, ext, after, w_query, w_keyval)


def settle_kernel(mid_ref, above_ref, below_ref, beside_ref, sum_ref, share_ref):
    count, inner = sum_ref.shape
    tile_rows = mid_ref.shape[0]

    def total(lanes):
        upper = above_ref[:, 0:WIN, lanes].astype(F32)
        lower = below_ref[:, 0:WIN, lanes].astype(F32)
        middle = mid_ref[:, :, lanes] + beside_ref[:, :, lanes].astype(F32)
        parts = [
            middle[:HALO] + upper,
            middle[HALO : tile_rows - HALO],
            middle[tile_rows - HALO :] + lower,
        ]
        return jnp.concatenate(parts, 0).reshape(count, LANES)

    share = 1.0 / (1.0 + total(slice(inner, inner + LANES)))
    share_ref[...] = share
    for g in range(0, inner, LANES):
        lanes = slice(g, g + LANES)
        sum_ref[:, lanes] = total(lanes) * share


def settle(mid, above, below, beside):
    tile_rows, tile_cols, wide = mid.shape
    count = tile_rows * tile_cols
    vmem = pl.BlockSpec(memory_space=pltpu.VMEM)
    return pl.pallas_call(
        settle_kernel,
        in_specs=[vmem] * 4,
        out_specs=[vmem] * 2,
        out_shape=[
            jax.ShapeDtypeStruct((count, wide - LANES), F32),
            jax.ShapeDtypeStruct((count, LANES), F32),
        ],
        compiler_params=PARAMS,
        cost_estimate=pl.CostEstimate(
            flops=4 * count * wide, bytes_accessed=12 * count * wide, transcendentals=0
        ),
        name="settle",
    )(mid, above, below, beside)


def blend_kernel(x_ref, known_ref, mask_ref, mixed_ref, sum_ref, share_ref, w_ref, out_ref, blended):
    count = x_ref.shape[0]

    @pl.when(pl.program_id(0) == 0)
    def _():
        groups = mixed_ref.shape[1]
        back = lattice_order(count, False)
        share = jnp.concatenate([share_ref[...]] * 2, 1)
        for g in range(0, groups, 2):
            lanes = slice(g * LANES, (g + 2) * LANES)
            mixed = jnp.concatenate(
                [mixed_ref[:, g + j].reshape(count, LANES) for j in range(2)], 1
            )
            blended[:, lanes] = (dot(back, mixed) * share + sum_ref[:, lanes]).astype(BF16)

    width = out_ref.shape[1]
    y = (x_ref[...].astype(F32) + dot(blended[...], w_ref[...])).astype(BF16)
    mask = jnp.concatenate([mask_ref[...]] * (width // LANES), 1)
    out_ref[...] = jnp.where(mask == 1, known_ref[...], y)


def blend(x, known, mask, mixed, windowed, share, w_out):
    count, channels = x.shape
    inner = w_out.shape[0]
    width = 2 * LANES
    by_cols = pl.BlockSpec((count, width), lambda i: (0, i))
    return pl.pallas_call(
        blend_kernel,
        grid=(channels // width,),
        in_specs=[by_cols, by_cols]
        + [whole(a.shape) for a in (mask, mixed, windowed, share)]
        + [pl.BlockSpec((inner, width), lambda i: (0, i))],
        out_specs=by_cols,
        out_shape=jax.ShapeDtypeStruct((count, channels), BF16),
        scratch_shapes=[pltpu.VMEM((count, inner), BF16)],
        compiler_params=PARAMS,
        cost_estimate=pl.CostEstimate(
            flops=2 * count * inner * (channels + count),
            bytes_accessed=2 * inner * channels + 6 * count * channels,
            transcendentals=0,
        ),
        name="blend",
    )(x, known, mask, mixed, windowed, share, w_out)


def exchange(pieces):
    return lax.all_to_all(pieces, ("row", "col"), split_axis=0, concat_axis=0, tiled=True)


def neighbours(axis):
    peers = lax.axis_size(axis)
    onward = [(i, i + 1) for i in range(peers - 1)]
    return onward, [(j, i) for i, j in onward]


def on_device(features, known, known_mask, w_query, w_keyval, w_out, win_anchor, win_weight):
    tile_rows, tile_cols, channels = features.shape
    count = tile_rows * tile_cols
    per_sub = count // SUBS
    inner = w_query.shape[1]
    devices = lax.axis_size("row") * lax.axis_size("col")
    down, up = neighbours("row")
    right, left = neighbours("col")
    x = features.reshape(count, channels)

    from_right = lax.ppermute(features[:, :HALO], "col", left)
    from_left = lax.ppermute(features[:, tile_cols - HALO :], "col", right)
    pieces = project(x, w_query, w_keyval).reshape(devices, per_sub, 3 * LANES)
    from_right, from_left, _ = lax.optimization_barrier((from_right, from_left, pieces))

    def rows_of_halo(rows):
        return jnp.concatenate([features[rows], from_right[rows], from_left[rows]], 1)

    before = lax.ppermute(rows_of_halo(slice(tile_rows - HALO, None)), "row", down)
    after = lax.ppermute(rows_of_halo(slice(0, HALO)), "row", up)
    ext = rows_of_halo(slice(None))

    gathered = exchange(pieces).reshape(devices * per_sub, 3 * LANES)

    top, bottom, inside, beside = windows(
        before, ext, after, w_query, w_keyval, win_anchor.reshape(-1, 2), win_weight.reshape(-1)
    )
    above = lax.ppermute(bottom, "row", down)
    below = lax.ppermute(top, "row", up)
    beside = jnp.concatenate(
        [
            beside[:HALO] + above[:, WIN:].astype(F32),
            beside[HALO : tile_rows - HALO],
            beside[tile_rows - HALO :] + below[:, WIN:].astype(F32),
        ],
        0,
    ).astype(BF16)
    gathered, beside = lax.optimization_barrier((gathered, beside))
    on_first = lax.ppermute(beside[:, :HALO], "col", right)
    on_last = lax.ppermute(beside[:, HALO:], "col", left)
    mixed = lattice_attend(gathered)
    mixed, on_first, on_last = lax.optimization_barrier((mixed, on_first, on_last))
    returned = exchange(mixed.reshape(devices, per_sub, LANES))
    arrived = jnp.concatenate([on_first, on_last], 1)
    windowed, share = settle(inside, above, below, arrived)
    mask = jnp.broadcast_to(known_mask.reshape(count, 1), (count, LANES))
    returned = returned.reshape(SUBS, devices // SUBS, per_sub, LANES)
    out = blend(x, known.reshape(count, channels), mask, returned, windowed, share, w_out)
    return out.reshape(tile_rows, tile_cols, channels)


def solution(mesh):
    in_specs = (
        P("row", "col", None),
        P("row", "col", None),
        P("row", "col"),
        P(),
        P(),
        P(),
        P("row", "col", None, None),
        P("row", "col", None),
    )
    out_specs = P("row", "col", None)
    return jax.shard_map(
        on_device, mesh=mesh, in_specs=in_specs, out_specs=out_specs, check_vma=False
    )
```

```python
import functools
import math

import jax
import jax.numpy as jnp
from jax import lax
from jax.experimental import pallas as pl
from jax.experimental.pallas import tpu as pltpu
from jax.sharding import PartitionSpec as P

HD = 64
STRIDE = 4
WIN = 16
HALO = 8
SUBS = STRIDE * STRIDE
LANES = 128
SCALE = HD**-0.5 * math.log2(math.e)
FREE_RANGE = 100.0
VROWS = 80
QBLOCK = 2048
KBLOCK = 256
QPART = 256
AHEAD = 8
BF16 = jnp.bfloat16
F32 = jnp.float32


def dot(a, b):
    return jnp.dot(a, b, preferred_element_type=F32)


def dot_nt(a, b):
    return lax.dot_general(a, b, (((1,), (1,)), ((), ())), preferred_element_type=F32)


def whole(shape):
    return pl.BlockSpec(shape, lambda *_: (0,) * len(shape), pipeline_mode=pl.Buffered(1))


PARAMS = pltpu.CompilerParams(vmem_limit_bytes=60 * 2**20)


def lattice_order(count, by_row):
    lattice = lax.broadcasted_iota(jnp.int32, (count, count), 0 if by_row else 1)
    cell = lax.broadcasted_iota(jnp.int32, (count, count), 1 if by_row else 0)
    per_sub = count // SUBS
    tile_cols = 16
    sub, place = lattice // per_sub, lattice % per_sub
    across = tile_cols // STRIDE
    row = (place // across) * STRIDE + sub // STRIDE
    col = (place % across) * STRIDE + sub % STRIDE
    return jnp.where(cell == row * tile_cols + col, 1.0, 0.0).astype(BF16)


def project_kernel(x_ref, wq_ref, wk_ref, wv_ref, out_ref, ordered):
    count = x_ref.shape[0]

    @pl.when(pl.program_id(0) == 0)
    def _():
        ordered[...] = dot(lattice_order(count, True), x_ref[...]).astype(BF16)

    x = ordered[...]
    q, k, v = (dot(x, w_ref[...]) for w_ref in (wq_ref, wk_ref, wv_ref))
    for g in range(2):
        at = g * LANES
        parts = [
            jnp.concatenate([q[:, at : at + HD], k[:, at : at + HD]], 1),
            v[:, at : at + LANES],
            jnp.concatenate([q[:, at + HD : at + LANES], k[:, at + HD : at + LANES]], 1),
        ]
        for j, part in enumerate(parts):
            out_ref[:, g, :, j * LANES : (j + 1) * LANES] = part.astype(BF16).reshape(
                SUBS, count // SUBS, LANES
            )


def project(x, w_query, w_keyval):
    count, channels = x.shape
    inner = w_query.shape[1]
    groups = inner // LANES
    steps = groups // 2
    per_sub = count // SUBS
    return pl.pallas_call(
        project_kernel,
        grid=(steps,),
        in_specs=[
            whole(x.shape),
            pl.BlockSpec((channels, 2 * LANES), lambda g: (0, g)),
            pl.BlockSpec((channels, 2 * LANES), lambda g: (0, g)),
            pl.BlockSpec((channels, 2 * LANES), lambda g: (0, g + steps)),
        ],
        out_specs=pl.BlockSpec((SUBS, 2, per_sub, 3 * LANES), lambda g: (0, g, 0, 0)),
        out_shape=jax.ShapeDtypeStruct((SUBS, groups, per_sub, 3 * LANES), BF16),
        scratch_shapes=[pltpu.VMEM((count, channels), BF16)],
        compiler_params=PARAMS,
        cost_estimate=pl.CostEstimate(
            flops=2 * count * channels * 3 * inner,
            bytes_accessed=2 * (3 * channels * inner + count * channels + 3 * count * inner),
            transcendentals=0,
        ),
        name="project",
    )(x, w_query, w_keyval, w_keyval)


def lattice_kernel(head, qk_ref, v_ref, *refs):
    if head == 0:
        o_ref, queries_t, values_t, free = refs
    else:
        other_ref, o_ref, queries_t, values_t, free = refs
    count = qk_ref.shape[0]
    block = o_ref.shape[1 - head]
    step = pl.program_id(0)

    @pl.when(step == 0)
    def _():
        both = qk_ref[...].astype(F32)
        q_t = both.T[:HD]
        lane = lax.broadcasted_iota(jnp.int32, both.shape, 1)
        k_norms = jnp.sum(jnp.where(lane < HD, 0.0, both * both), axis=1)
        bound = jnp.max(jnp.sum(q_t * q_t, axis=0)) * jnp.max(k_norms)
        free[0] = (bound * (SCALE * SCALE) <= FREE_RANGE * FREE_RANGE).astype(jnp.int32)
        queries_t[0:HD] = jnp.zeros((HD, count), BF16)
        queries_t[HD:LANES] = q_t.astype(BF16)
        v_t = v_ref[...].astype(F32).T
        values_t[0:HD] = v_t[head * HD : (head + 1) * HD].astype(BF16)
        values_t[HD:VROWS] = jnp.ones((VROWS - HD, count), BF16)

    cols = pl.ds(pl.multiple_of(step * block, block), block)

    def finish(total):
        out = total[:HD] / total[HD : HD + 1]
        if head == 0:
            o_ref[...] = out.astype(BF16)
        else:
            o_ref[...] = jnp.concatenate([other_ref[...].astype(F32), out], 0).T.astype(BF16)

    @pl.when(free[0] == 1)
    def _():
        parts = block // QPART
        items = [(c, j) for c in range(0, count, KBLOCK) for j in range(parts)]
        queries = [
            queries_t[:, pl.ds(pl.multiple_of(step * block + j * QPART, QPART), QPART)]
            for j in range(parts)
        ]

        def score(i):
            c, j = items[i]
            return dot(qk_ref[c : c + KBLOCK, :], queries[j])

        totals = [None] * parts
        ahead = [score(i) for i in range(AHEAD)]
        for i, (c, j) in enumerate(items):
            now = ahead.pop(0)
            if i + AHEAD < len(items):
                ahead.append(score(i + AHEAD))
            weights = jnp.exp2(now * SCALE).astype(BF16)
            part = dot(values_t[:, c : c + KBLOCK], weights)
            totals[j] = part if totals[j] is None else totals[j] + part
        finish(jnp.concatenate(totals, 1))

    @pl.when(free[0] == 0)
    def _():
        chunks = count // KBLOCK
        q = queries_t[:, cols]

        def score(c):
            return dot(qk_ref[pl.ds(pl.multiple_of(c * KBLOCK, KBLOCK), KBLOCK), :], q)

        def top(c, m):
            return jnp.maximum(m, jnp.max(score(c), axis=0, keepdims=True))

        m = lax.fori_loop(0, chunks, top, jnp.full((1, block), -jnp.inf, F32))

        def add(c, total):
            weights = jnp.exp2((score(c) - m) * SCALE).astype(BF16)
            rows = pl.ds(pl.multiple_of(c * KBLOCK, KBLOCK), KBLOCK)
            return total + dot(values_t[:, rows], weights)

        finish(lax.fori_loop(0, chunks, add, jnp.zeros((VROWS, block), F32)))


def lattice_attend(head, x, other=None):
    count = x.shape[0]
    in_specs = [
        pl.BlockSpec((count, LANES), lambda i: (0, 2 * head), pipeline_mode=pl.Buffered(1)),
        pl.BlockSpec((count, LANES), lambda i: (0, 1), pipeline_mode=pl.Buffered(1)),
    ]
    args = [x, x]
    if head == 0:
        out_spec = pl.BlockSpec((HD, QBLOCK), lambda i: (0, i))
        out_shape = (HD, count)
    else:
        in_specs.append(pl.BlockSpec((HD, QBLOCK), lambda i: (0, i)))
        args.append(other)
        out_spec = pl.BlockSpec((QBLOCK, LANES), lambda i: (i, 0))
        out_shape = (count, LANES)
    return pl.pallas_call(
        functools.partial(lattice_kernel, head),
        grid=(count // QBLOCK,),
        in_specs=in_specs,
        out_specs=out_spec,
        out_shape=jax.ShapeDtypeStruct(out_shape, BF16),
        scratch_shapes=[
            pltpu.VMEM((LANES, count), BF16),
            pltpu.VMEM((VROWS, count), BF16),
            pltpu.SMEM((1,), jnp.int32),
        ],
        compiler_params=PARAMS,
        cost_estimate=pl.CostEstimate(
            flops=4 * 4 * count * count * HD,
            bytes_accessed=6 * count * LANES,
            transcendentals=count * count,
        ),
        name="lattice_attend_" + str(head),
    )(*args)


def windows_kernel(
    anchor, weight, mid_hbm, before_hbm, after_hbm, side_before_hbm, side_after_hbm, right_ref, left_ref,
    wq_hbm, wkv_hbm, top_out, bottom_out, mid_out, right_out, left_out, held, wq_ref, wkv_ref, mid_sum, side_sum, results_t, sems,
):
    channels, inner = wq_ref.shape
    cells = WIN * WIN
    wide = inner + LANES
    tile_rows = mid_hbm.shape[0]
    end = tile_rows + HALO
    pair_lanes = 2 * LANES
    copies = [
        pltpu.make_async_copy(source, target, sems.at[i])
        for i, (source, target) in enumerate(
            (
                (mid_hbm, held.at[HALO:end, 0:WIN]),
                (before_hbm, held.at[0:HALO, 0:WIN]),
                (after_hbm, held.at[end : end + HALO, 0:WIN]),
                (side_before_hbm, held.at[0:HALO, WIN : 2 * WIN]),
                (side_after_hbm, held.at[end : end + HALO, WIN : 2 * WIN]),
            )
        )
    ]
    weight_copies = {}
    for g in range(0, inner, pair_lanes):
        for part, (source, target, at) in enumerate(
            ((wq_hbm, wq_ref, g), (wkv_hbm, wkv_ref, g), (wkv_hbm, wkv_ref, inner + g))
        ):
            cols = slice(at, at + pair_lanes)
            sem = sems.at[len(copies) + 3 * (g // pair_lanes) + part]
            weight_copies.setdefault(g, []).append(
                pltpu.make_async_copy(source.at[:, cols], target.at[:, cols], sem)
            )
    for copy in copies + sum(weight_copies.values(), []):
        copy.start()
    mid_sum[...] = jnp.zeros(mid_sum.shape, F32)
    side_sum[...] = jnp.zeros(side_sum.shape, F32)
    results_t[inner:wide] = jnp.ones((LANES, cells), BF16)
    for row in range(0, tile_rows, HALO):
        rows = slice(row, row + HALO)
        pair = (right_ref[rows].astype(F32), left_ref[rows].astype(F32))
        held[HALO + row : 2 * HALO + row, WIN : 2 * WIN] = jnp.concatenate(pair, 1).astype(BF16)
    for copy in copies:
        copy.wait()
    slots = weight.shape[0]
    live = sum((weight[s] > 0).astype(jnp.int32) for s in range(slots))
    first = lax.broadcasted_iota(jnp.int32, (cells, LANES), 1) < HD
    ones = jnp.ones((VROWS - HD, cells), BF16)

    def one_hot(window_dim, left):
        shape = (cells, 2 * cells) if window_dim == 0 else (2 * cells, cells)
        window = lax.broadcasted_iota(jnp.int32, shape, window_dim)
        source = lax.broadcasted_iota(jnp.int32, shape, 1 - window_dim)
        place = ((window & (WIN - 1)) + left) & (2 * WIN - 1)
        held = (source & (WIN - 1)) + ((source >> 8) << 4)
        same = (((window ^ source) & (cells - WIN)) == 0) & (place == held)
        return jnp.where(same, 1.0, 0.0)

    def one_window(slot, arriving):
        top = anchor[slot, 0] + HALO
        left = anchor[slot, 1]
        factor = weight[slot].astype(F32)
        rows = pl.ds(top, WIN)
        source = jnp.concatenate(
            [
                held[rows, 0:WIN].reshape(cells, channels),
                held[rows, WIN : 2 * WIN].reshape(cells, channels),
            ],
            0,
        )
        x = dot(one_hot(0, left).astype(BF16), source).astype(BF16)

        def project(g):
            for copy in arriving.get(g, ()):
                copy.wait()
            q = dot(x, wq_ref[:, g : g + 2 * LANES]).astype(BF16)
            k = dot(x, wkv_ref[:, g : g + 2 * LANES]).astype(BF16)
            v = dot(x, wkv_ref[:, inner + g : inner + g + 2 * LANES])
            return q, k, v.T.astype(BF16)

        def scores(q, k, j):
            lanes = slice(j // 2 * LANES, (j // 2 + 1) * LANES)
            own = jnp.where(first if j % 2 == 0 else ~first, q[:, lanes], jnp.zeros((), BF16))
            return dot_nt(k[:, lanes], own)

        def mix(s, v_t, g, j):
            e = jnp.exp2((s - jnp.max(s, axis=0, keepdims=True)) * SCALE).astype(BF16)
            o = dot(jnp.concatenate([v_t[j * HD : (j + 1) * HD], ones], 0), e)
            at = g + j * HD
            results_t[at : at + HD] = (o[:HD] / o[HD : HD + 1]).astype(BF16)

        later = project(0)
        for g in range(0, inner, 2 * LANES):
            q, k, v_t = later
            now = [scores(q, k, j) for j in range(4)]
            if g + 2 * LANES < inner:
                later = project(g + 2 * LANES)
            for j in range(4):
                mix(now[j], v_t, g, j)
        placed = dot_nt((one_hot(1, left) * factor).astype(BF16), results_t[...])
        mid_sum[rows] += placed[:cells].reshape(WIN, WIN, wide)
        side_sum[rows] += placed[cells:].reshape(WIN, WIN, wide)

    def later_window(slot, carry):
        one_window(slot, {})
        return carry

    one_window(0, weight_copies)
    lax.fori_loop(1, live, later_window, 0)
    top_out[:, 0:WIN] = mid_sum[0:HALO].astype(BF16)
    top_out[:, WIN : 2 * WIN] = side_sum[0:HALO].astype(BF16)
    bottom_out[:, 0:WIN] = mid_sum[end : end + HALO].astype(BF16)
    bottom_out[:, WIN : 2 * WIN] = side_sum[end : end + HALO].astype(BF16)
    mid_out[...] = mid_sum[HALO:end].astype(BF16)
    right_out[...] = side_sum[HALO:end, 0:HALO].astype(BF16)
    left_out[...] = side_sum[HALO:end, HALO : 2 * HALO].astype(BF16)


def windows(
    mid, before, after, side_before, side_after, from_right, from_left, w_query, w_keyval, anchor, weight
):
    tile_rows, _, channels = mid.shape
    high = tile_rows + 2 * HALO
    inner = w_query.shape[1]
    wide = inner + LANES
    vmem = pl.BlockSpec(memory_space=pltpu.VMEM)
    smem = pl.BlockSpec(memory_space=pltpu.SMEM)
    free = pl.BlockSpec(memory_space=pl.ANY)
    rim = jax.ShapeDtypeStruct((HALO, 2 * WIN, wide), BF16)
    inside = jax.ShapeDtypeStruct((tile_rows, WIN, wide), BF16)
    edge = jax.ShapeDtypeStruct((tile_rows, HALO, wide), BF16)
    slots = weight.shape[0]
    cells = WIN * WIN
    return pl.pallas_call(
        windows_kernel,
        in_specs=[smem, smem] + [free] * 5 + [vmem] * 2 + [free] * 2,
        out_specs=[vmem] * 5,
        out_shape=[rim, rim, inside, edge, edge],
        scratch_shapes=[
            pltpu.VMEM((high, 2 * WIN, channels), BF16),
            pltpu.VMEM(w_query.shape, BF16),
            pltpu.VMEM(w_keyval.shape, BF16),
            pltpu.VMEM((high, WIN, wide), F32),
            pltpu.VMEM((high, WIN, wide), F32),
            pltpu.VMEM((wide, cells), BF16),
            pltpu.SemaphoreType.DMA((5 + 3 * (inner // (2 * LANES)),)),
        ],
        compiler_params=PARAMS,
        cost_estimate=pl.CostEstimate(
            flops=8 * slots * 2 * cells * 3 * inner * (channels + 2 * cells),
            bytes_accessed=6 * channels * inner + 4 * high * WIN * channels,
            transcendentals=slots * cells * cells * inner // HD,
        ),
        name="windows",
    )(
        anchor, weight, mid, before, after, side_before, side_after, from_right, from_left,
        w_query, w_keyval,
    )


def fold_kernel(right_ref, left_ref, above_ref, below_ref, right_out, left_out):
    tile_rows = right_ref.shape[0]
    sides = [ref[:, WIN : 2 * WIN].astype(F32) for ref in (above_ref, below_ref)]
    for j, (source, target) in enumerate(((right_ref, right_out), (left_ref, left_out))):
        upper, lower = [side[:, j * HALO : (j + 1) * HALO] for side in sides]
        target[0:HALO] = (source[0:HALO].astype(F32) + upper).astype(BF16)
        target[HALO : tile_rows - HALO] = source[HALO : tile_rows - HALO]
        last = slice(tile_rows - HALO, tile_rows)
        target[last] = (source[last].astype(F32) + lower).astype(BF16)


def fold(on_right, on_left, above, below):
    vmem = pl.BlockSpec(memory_space=pltpu.VMEM)
    return pl.pallas_call(
        fold_kernel,
        in_specs=[vmem] * 4,
        out_specs=[vmem] * 2,
        out_shape=[jax.ShapeDtypeStruct(a.shape, a.dtype) for a in (on_right, on_left)],
        compiler_params=PARAMS,
        cost_estimate=pl.CostEstimate(
            flops=on_right.size, bytes_accessed=12 * on_right.size, transcendentals=0
        ),
        name="fold",
    )(on_right, on_left, above, below)


def settle_kernel(
    mid_ref, above_ref, below_ref, beside_ref, mask_ref, sum_ref, share_ref, wide_mask_ref
):
    count, inner = sum_ref.shape
    tile_rows, tile_cols = mask_ref.shape
    cell = lax.broadcasted_iota(jnp.int32, (count, tile_rows), 0)
    row = lax.broadcasted_iota(jnp.int32, (count, tile_rows), 1)
    pick_row = jnp.where(cell // tile_cols == row, 1.0, 0.0).astype(BF16)
    in_row = dot(pick_row, mask_ref[...].astype(BF16))
    cell = lax.broadcasted_iota(jnp.int32, (count, tile_cols), 0)
    col = lax.broadcasted_iota(jnp.int32, (count, tile_cols), 1)
    own = jnp.sum(jnp.where(cell % tile_cols == col, in_row, 0.0), axis=1, keepdims=True)
    wide_mask_ref[...] = jnp.broadcast_to(own, wide_mask_ref.shape)

    def total(lanes):
        upper = above_ref[:, 0:WIN, lanes].astype(F32)
        lower = below_ref[:, 0:WIN, lanes].astype(F32)
        middle = mid_ref[:, :, lanes].astype(F32) + beside_ref[:, :, lanes].astype(F32)
        parts = [
            middle[:HALO] + upper,
            middle[HALO : tile_rows - HALO],
            middle[tile_rows - HALO :] + lower,
        ]
        return jnp.concatenate(parts, 0).reshape(count, LANES)

    share = 1.0 / (1.0 + total(slice(inner, inner + LANES)))
    share_ref[...] = share
    for g in range(0, inner, LANES):
        lanes = slice(g, g + LANES)
        sum_ref[:, lanes] = total(lanes) * share


def settle(mid, above, below, beside, mask):
    tile_rows, tile_cols, wide = mid.shape
    count = tile_rows * tile_cols
    vmem = pl.BlockSpec(memory_space=pltpu.VMEM)
    return pl.pallas_call(
        settle_kernel,
        in_specs=[vmem] * 5,
        out_specs=[vmem] * 3,
        out_shape=[
            jax.ShapeDtypeStruct((count, wide - LANES), F32),
            jax.ShapeDtypeStruct((count, LANES), F32),
            jax.ShapeDtypeStruct((count, LANES), F32),
        ],
        compiler_params=PARAMS,
        cost_estimate=pl.CostEstimate(
            flops=2**17 * count * wide, bytes_accessed=12 * count * wide, transcendentals=0
        ),
        name="settle",
    )(mid, above, below, beside, mask)


def blend_kernel(
    x_hbm, known_hbm, mask_hbm, mixed_hbm, sum_hbm, share_hbm, w_hbm, out_hbm,
    x_ref, known_ref, mask_ref, mixed_ref, sum_ref, share_ref, w_ref, out_ref, blended, sems, out_sems,
):
    count, channels = x_ref.shape
    groups = mixed_ref.shape[1]
    width = 2 * LANES
    blocks = [slice(c, c + width) for c in range(0, channels, width)]
    whole_copies = [
        pltpu.make_async_copy(source, target, sems.at[i])
        for i, (source, target) in enumerate(
            (
                (mixed_hbm, mixed_ref),
                (share_hbm, share_ref),
                (sum_hbm, sum_ref),
                (mask_hbm, mask_ref),
            )
        )
    ]
    block_copies = [
        [
            pltpu.make_async_copy(source.at[:, cols], target.at[:, cols], sems.at[4 + 3 * i + j])
            for j, (source, target) in enumerate(
                ((w_hbm, w_ref), (x_hbm, x_ref), (known_hbm, known_ref))
            )
        ]
        for i, cols in enumerate(blocks)
    ]
    for copy in whole_copies + sum(block_copies, []):
        copy.start()
    back = lattice_order(count, False)
    for copy in whole_copies:
        copy.wait()
    share = jnp.concatenate([share_ref[...]] * 2, 1)
    for g in range(0, groups, 2):
        lanes = slice(g * LANES, (g + 2) * LANES)
        mixed = jnp.concatenate([mixed_ref[:, g + j].reshape(count, LANES) for j in range(2)], 1)
        blended[:, lanes] = (dot(back, mixed) * share + sum_ref[:, lanes]).astype(BF16)
    known_cell = jnp.concatenate([mask_ref[...]] * 2, 1) == 1
    outs = []
    for i, cols in enumerate(blocks):
        for copy in block_copies[i]:
            copy.wait()
        y = (x_ref[:, cols].astype(F32) + dot(blended[...], w_ref[:, cols])).astype(BF16)
        out_ref[:, cols] = jnp.where(known_cell, known_ref[:, cols], y)
        outs.append(
            pltpu.make_async_copy(out_ref.at[:, cols], out_hbm.at[:, cols], out_sems.at[i])
        )
        outs[-1].start()
    for copy in outs:
        copy.wait()


def blend(x, known, mask, mixed, windowed, share, w_out):
    count, channels = x.shape
    inner = w_out.shape[0]
    arrays = (x, known, mask, mixed, windowed, share, w_out)
    free = pl.BlockSpec(memory_space=pl.ANY)
    blocks = channels // (2 * LANES)
    return pl.pallas_call(
        blend_kernel,
        in_specs=[free] * len(arrays),
        out_specs=free,
        out_shape=jax.ShapeDtypeStruct((count, channels), BF16),
        scratch_shapes=[pltpu.VMEM(a.shape, a.dtype) for a in arrays]
        + [
            pltpu.VMEM((count, channels), BF16),
            pltpu.VMEM((count, inner), BF16),
            pltpu.SemaphoreType.DMA((4 + 3 * blocks,)),
            pltpu.SemaphoreType.DMA((blocks,)),
        ],
        compiler_params=PARAMS,
        cost_estimate=pl.CostEstimate(
            flops=2 * count * inner * (channels + count),
            bytes_accessed=2 * inner * channels + 6 * count * channels,
            transcendentals=0,
        ),
        name="blend",
    )(*arrays)


def exchange(pieces):
    return lax.all_to_all(pieces, ("row", "col"), split_axis=0, concat_axis=0, tiled=True)


def neighbours(axis):
    peers = lax.axis_size(axis)
    onward = [(i, i + 1) for i in range(peers - 1)]
    return onward, [(j, i) for i, j in onward]


def on_device(features, known, known_mask, w_query, w_keyval, w_out, win_anchor, win_weight):
    tile_rows, tile_cols, channels = features.shape
    count = tile_rows * tile_cols
    per_sub = count // SUBS
    inner = w_query.shape[1]
    devices = lax.axis_size("row") * lax.axis_size("col")
    down, up = neighbours("row")
    right, left = neighbours("col")
    x = features.reshape(count, channels)

    from_right = lax.ppermute(features[:, :HALO], "col", left)
    from_left = lax.ppermute(features[:, tile_cols - HALO :], "col", right)
    before = lax.ppermute(features[tile_rows - HALO :], "row", down)
    after = lax.ppermute(features[:HALO], "row", up)
    pieces = project(x, w_query, w_keyval).reshape(devices, per_sub, 3 * LANES)
    from_right, from_left, mask, anchors, _ = lax.optimization_barrier(
        (from_right, from_left, known_mask.astype(F32), win_anchor.reshape(-1, 2), pieces)
    )

    def corners(rows):
        return jnp.concatenate([from_right[rows], from_left[rows]], 1)

    side_before = lax.ppermute(corners(slice(tile_rows - HALO, None)), "row", down)
    side_after = lax.ppermute(corners(slice(0, HALO)), "row", up)

    gathered = exchange(pieces).reshape(devices * per_sub, 3 * LANES)

    top, bottom, inside, on_right, on_left = windows(
        features,
        before,
        after,
        side_before,
        side_after,
        from_right,
        from_left,
        w_query,
        w_keyval,
        anchors,
        win_weight.reshape(-1),
    )
    above = lax.ppermute(bottom, "row", down)
    below = lax.ppermute(top, "row", up)
    half = lattice_attend(0, gathered)
    half, above, below = lax.optimization_barrier((half, above, below))
    on_right, on_left = fold(on_right, on_left, above, below)
    gathered, half, on_right, on_left = lax.optimization_barrier((gathered, half, on_right, on_left))
    on_first = lax.ppermute(on_right, "col", right)
    on_last = lax.ppermute(on_left, "col", left)
    mixed = lattice_attend(1, gathered, half)
    mixed, on_first, on_last = lax.optimization_barrier((mixed, on_first, on_last))
    returned = exchange(mixed.reshape(devices, per_sub, LANES))
    arrived = jnp.concatenate([on_first, on_last], 1)
    windowed, share, mask = settle(inside, above, below, arrived, mask)
    returned = returned.reshape(SUBS, devices // SUBS, per_sub, LANES)
    out = blend(x, known.reshape(count, channels), mask, returned, windowed, share, w_out)
    return out.reshape(tile_rows, tile_cols, channels)


def solution(mesh):
    in_specs = (
        P("row", "col", None),
        P("row", "col", None),
        P("row", "col"),
        P(),
        P(),
        P(),
        P("row", "col", None, None),
        P("row", "col", None),
    )
    out_specs = P("row", "col", None)
    return jax.shard_map(
        on_device, mesh=mesh, in_specs=in_specs, out_specs=out_specs, check_vma=False
    )
```

```python
import functools
import math

import jax
import jax.numpy as jnp
from jax import lax
from jax.experimental import pallas as pl
from jax.experimental.pallas import tpu as pltpu
from jax.sharding import PartitionSpec as P

HD = 64
STRIDE = 4
WIN = 16
HALO = 8
SUBS = STRIDE * STRIDE
LANES = 128
SCALE = HD**-0.5 * math.log2(math.e)
FREE_RANGE = 100.0
VROWS = 80
QBLOCK = 2048
KBLOCK = 256
QPART = 256
AHEAD = 8
BF16 = jnp.bfloat16
F32 = jnp.float32


def dot(a, b):
    return jnp.dot(a, b, preferred_element_type=F32)


def dot_nt(a, b):
    return lax.dot_general(a, b, (((1,), (1,)), ((), ())), preferred_element_type=F32)


def whole(shape):
    return pl.BlockSpec(shape, lambda *_: (0,) * len(shape), pipeline_mode=pl.Buffered(1))


def params(mebibytes=63):
    return pltpu.CompilerParams(vmem_limit_bytes=mebibytes * 2**20)


def lattice_order(count, by_row):
    lattice = lax.broadcasted_iota(jnp.int32, (count, count), 0 if by_row else 1)
    cell = lax.broadcasted_iota(jnp.int32, (count, count), 1 if by_row else 0)
    per_sub = count // SUBS
    tile_cols = 16
    sub, place = lattice // per_sub, lattice % per_sub
    across = tile_cols // STRIDE
    row = (place // across) * STRIDE + sub // STRIDE
    col = (place % across) * STRIDE + sub % STRIDE
    return jnp.where(cell == row * tile_cols + col, 1.0, 0.0).astype(BF16)


def project_kernel(
    x_hbm, wq_hbm, wkv_hbm, out_hbm, x_ref, wq_ref, wkv_ref, ordered, queries, out_ref, sems,
    out_sems,
):
    count, channels = x_ref.shape
    inner = wq_ref.shape[1]
    width = 2 * LANES
    x_copy = pltpu.make_async_copy(x_hbm, x_ref, sems.at[0])
    x_copy.start()
    weight_copies = [
        pltpu.make_async_copy(source, target, sems.at[1 + i])
        for i, (source, target) in enumerate(((wq_hbm, wq_ref), (wkv_hbm, wkv_ref)))
    ]
    for copy in weight_copies:
        copy.start()
    order = lattice_order(count, True)
    x_copy.wait()
    ordered[...] = dot(order, x_ref[...]).astype(BF16)
    weight_copies[0].wait()
    for c in range(0, inner, width):
        queries[:, c : c + width] = dot(ordered[...], wq_ref[:, c : c + width])
    weight_copies[1].wait()
    leaving = []
    for i, c in enumerate(range(0, inner, width)):
        q = queries[:, c : c + width]
        k = dot(ordered[...], wkv_ref[:, c : c + width])
        v = dot(ordered[...], wkv_ref[:, inner + c : inner + c + width])
        for g in range(2):
            at = g * LANES
            parts = [
                jnp.concatenate([q[:, at : at + HD], k[:, at : at + HD]], 1),
                v[:, at : at + LANES],
                jnp.concatenate([q[:, at + HD : at + LANES], k[:, at + HD : at + LANES]], 1),
            ]
            for j, part in enumerate(parts):
                out_ref[:, 2 * i + g, :, j * LANES : (j + 1) * LANES] = part.astype(BF16).reshape(
                    SUBS, count // SUBS, LANES
                )
        groups = slice(2 * i, 2 * i + 2)
        leaving.append(
            pltpu.make_async_copy(out_ref.at[:, groups], out_hbm.at[:, groups], out_sems.at[i])
        )
        leaving[-1].start()
    for copy in leaving:
        copy.wait()


def project(x, w_query, w_keyval):
    count, channels = x.shape
    inner = w_query.shape[1]
    groups = inner // LANES
    shape = (SUBS, groups, count // SUBS, 3 * LANES)
    free = pl.BlockSpec(memory_space=pl.ANY)
    return pl.pallas_call(
        project_kernel,
        in_specs=[free] * 3,
        out_specs=free,
        out_shape=jax.ShapeDtypeStruct(shape, BF16),
        scratch_shapes=[
            pltpu.VMEM(x.shape, BF16),
            pltpu.VMEM(w_query.shape, BF16),
            pltpu.VMEM(w_keyval.shape, BF16),
            pltpu.VMEM(x.shape, BF16),
            pltpu.VMEM((count, inner), F32),
            pltpu.VMEM(shape, BF16),
            pltpu.SemaphoreType.DMA((3,)),
            pltpu.SemaphoreType.DMA((groups // 2,)),
        ],
        compiler_params=params(61),
        cost_estimate=pl.CostEstimate(
            flops=2 * count * channels * 3 * inner,
            bytes_accessed=2 * (3 * channels * inner + count * channels + 3 * count * inner),
            transcendentals=0,
        ),
        name="project",
    )(x, w_query, w_keyval)


def lattice_kernel(head, qk_ref, v_ref, *refs):
    if head == 0:
        o_ref, queries_t, values_t, free = refs
    else:
        other_ref, o_ref, queries_t, values_t, free = refs
    count = qk_ref.shape[0]
    block = o_ref.shape[1 - head]
    step = pl.program_id(0)

    @pl.when(step == 0)
    def _():
        row = lax.broadcasted_iota(jnp.int32, (LANES, LANES), 0)
        lane = lax.broadcasted_iota(jnp.int32, (LANES, LANES), 1)
        to_keys = jnp.where(row == lane + HD, 1.0, 0.0).astype(BF16)
        queries_t[...] = dot_nt(to_keys, qk_ref[...]).astype(BF16)
        own = (row[:HD] + head * HD == lane[:HD]).astype(F32).astype(BF16)
        values_t[0:HD] = dot_nt(own, v_ref[...]).astype(BF16)
        squares = qk_ref[...].astype(F32)
        squares = (squares * squares).astype(BF16)
        halves = ((row[:VROWS - HD] < 8) == (lane[:VROWS - HD] < HD)).astype(F32).astype(BF16)
        norms = dot_nt(halves, squares)
        bound = jnp.max(norms[:8]) * jnp.max(norms[8:]) * 1.02
        free[0] = (bound * (SCALE * SCALE) <= FREE_RANGE * FREE_RANGE).astype(jnp.int32)
        values_t[HD:VROWS] = jnp.ones((VROWS - HD, count), BF16)

    cols = pl.ds(pl.multiple_of(step * block, block), block)

    def finish(total):
        out = total[:HD] / total[HD : HD + 1]
        if head == 0:
            o_ref[...] = out.astype(BF16)
        else:
            o_ref[...] = jnp.concatenate([other_ref[...].astype(F32), out], 0).T.astype(BF16)

    @pl.when(free[0] == 1)
    def _():
        parts = block // QPART
        items = [(c, j) for c in range(0, count, KBLOCK) for j in range(parts)]
        queries = [
            queries_t[:, pl.ds(pl.multiple_of(step * block + j * QPART, QPART), QPART)]
            for j in range(parts)
        ]

        def score(i):
            c, j = items[i]
            return dot(qk_ref[c : c + KBLOCK, :], queries[j])

        totals = [None] * parts
        ahead = [score(i) for i in range(AHEAD)]
        for i, (c, j) in enumerate(items):
            now = ahead.pop(0)
            if i + AHEAD < len(items):
                ahead.append(score(i + AHEAD))
            weights = jnp.exp2(now * SCALE).astype(BF16)
            part = dot(values_t[:, c : c + KBLOCK], weights)
            totals[j] = part if totals[j] is None else totals[j] + part
        finish(jnp.concatenate(totals, 1))

    @pl.when(free[0] == 0)
    def _():
        chunks = count // KBLOCK
        q = queries_t[:, cols]

        def score(c):
            return dot(qk_ref[pl.ds(pl.multiple_of(c * KBLOCK, KBLOCK), KBLOCK), :], q)

        def top(c, m):
            return jnp.maximum(m, jnp.max(score(c), axis=0, keepdims=True))

        m = lax.fori_loop(0, chunks, top, jnp.full((1, block), -jnp.inf, F32))

        def add(c, total):
            weights = jnp.exp2((score(c) - m) * SCALE).astype(BF16)
            rows = pl.ds(pl.multiple_of(c * KBLOCK, KBLOCK), KBLOCK)
            return total + dot(values_t[:, rows], weights)

        finish(lax.fori_loop(0, chunks, add, jnp.zeros((VROWS, block), F32)))


def lattice_attend(head, x, other=None):
    count = x.shape[0]
    in_specs = [
        pl.BlockSpec((count, LANES), lambda i: (0, 2 * head), pipeline_mode=pl.Buffered(1)),
        pl.BlockSpec((count, LANES), lambda i: (0, 1), pipeline_mode=pl.Buffered(1)),
    ]
    args = [x, x]
    if head == 0:
        out_spec = pl.BlockSpec((HD, QBLOCK), lambda i: (0, i))
        out_shape = (HD, count)
    else:
        in_specs.append(pl.BlockSpec((HD, QBLOCK), lambda i: (0, i)))
        args.append(other)
        out_spec = pl.BlockSpec((QBLOCK, LANES), lambda i: (i, 0))
        out_shape = (count, LANES)
    return pl.pallas_call(
        functools.partial(lattice_kernel, head),
        grid=(count // QBLOCK,),
        in_specs=in_specs,
        out_specs=out_spec,
        out_shape=jax.ShapeDtypeStruct(out_shape, BF16),
        scratch_shapes=[
            pltpu.VMEM((LANES, count), BF16),
            pltpu.VMEM((VROWS, count), BF16),
            pltpu.SMEM((1,), jnp.int32),
        ],
        compiler_params=params(63 if head else 61),
        cost_estimate=pl.CostEstimate(
            flops=4 * 4 * count * count * HD,
            bytes_accessed=6 * count * LANES,
            transcendentals=count * count,
        ),
        name="lattice_attend_" + str(head),
    )(*args)


def windows_kernel(
    anchor, weight, mid_hbm, before_hbm, after_hbm, right_ref, left_ref,
    wq_hbm, wkv_hbm, top_out, bottom_out, mid_out, right_out, left_out, held, wq_ref, wkv_ref, mid_sum, side_sum, results_t, sems,
):
    channels, inner = wq_ref.shape
    cells = WIN * WIN
    wide = inner + LANES
    tile_rows = mid_hbm.shape[0]
    end = tile_rows + HALO
    pair_lanes = 2 * LANES
    copies = [
        pltpu.make_async_copy(source, target, sems.at[i])
        for i, (source, target) in enumerate(
            (
                (mid_hbm, held.at[HALO:end, 0:WIN]),
                (before_hbm, held.at[0:HALO]),
                (after_hbm, held.at[end : end + HALO]),
            )
        )
    ]
    weight_copies = {}
    for g in range(0, inner, pair_lanes):
        for part, (source, target, at) in enumerate(
            ((wq_hbm, wq_ref, g), (wkv_hbm, wkv_ref, g), (wkv_hbm, wkv_ref, inner + g))
        ):
            cols = slice(at, at + pair_lanes)
            sem = sems.at[len(copies) + 3 * (g // pair_lanes) + part]
            weight_copies.setdefault(g, []).append(
                pltpu.make_async_copy(source.at[:, cols], target.at[:, cols], sem)
            )
    for copy in copies + sum(weight_copies.values(), []):
        copy.start()
    mid_sum[...] = jnp.zeros(mid_sum.shape, F32)
    side_sum[...] = jnp.zeros(side_sum.shape, F32)
    for row in range(0, tile_rows, HALO):
        rows = slice(row, row + HALO)
        pair = (right_ref[rows].astype(F32), left_ref[rows].astype(F32))
        held[HALO + row : 2 * HALO + row, WIN : 2 * WIN] = jnp.concatenate(pair, 1).astype(BF16)
    for copy in copies:
        copy.wait()
    slots = weight.shape[0]
    live = sum((weight[s] > 0).astype(jnp.int32) for s in range(slots))
    first = lax.broadcasted_iota(jnp.int32, (cells, LANES), 1) < HD
    ones = jnp.ones((VROWS - HD, cells), BF16)

    column = lax.broadcasted_iota(jnp.int32, (1, WIN, 1), 1)
    across = lax.broadcasted_iota(jnp.int32, (cells, cells), 0)
    along = lax.broadcasted_iota(jnp.int32, (cells, cells), 1)
    diagonal = jnp.where(across == along, 1.0, 0.0)

    def one_window(slot, arriving):
        top = anchor[0, slot] + HALO
        left = anchor[1, slot]
        factor = weight[slot].astype(F32)
        rows = pl.ds(top, WIN)
        in_mid = ((column >= left) & (column < left + WIN)).astype(F32)
        own = in_mid.astype(BF16)
        x = held[rows, 0:WIN] * own + held[rows, WIN : 2 * WIN] * (1 - own)
        x = x.reshape(cells, channels)

        def project(g):
            for copy in arriving.get(g, ()):
                copy.wait()
            q = dot(x, wq_ref[:, g : g + 2 * LANES]).astype(BF16)
            k = dot(x, wkv_ref[:, g : g + 2 * LANES]).astype(BF16)
            v = dot(x, wkv_ref[:, inner + g : inner + g + 2 * LANES])
            return q, k, v.T.astype(BF16)

        def scores(q, k, j):
            lanes = slice(j // 2 * LANES, (j // 2 + 1) * LANES)
            own = jnp.where(first if j % 2 == 0 else ~first, q[:, lanes], jnp.zeros((), BF16))
            return dot_nt(k[:, lanes], own)

        def mix(s, v_t, g, j):
            e = jnp.exp2((s - jnp.max(s, axis=0, keepdims=True)) * SCALE).astype(BF16)
            o = dot(jnp.concatenate([v_t[j * HD : (j + 1) * HD], ones], 0), e)
            at = g + j * HD
            results_t[at : at + HD] = (o[:HD] / o[HD : HD + 1]).astype(BF16)

        later = project(0)
        for g in range(0, inner, 2 * LANES):
            q, k, v_t = later
            now = [scores(q, k, j) for j in range(4)]
            if g + 2 * LANES < inner:
                later = project(g + 2 * LANES)
            for j in range(4):
                mix(now[j], v_t, g, j)
        placed = dot_nt((diagonal * factor).astype(BF16), results_t[...]).reshape(WIN, WIN, inner)
        mid_sum[rows, :, 0:inner] += placed * in_mid
        side_sum[rows, :, 0:inner] += placed * (1.0 - in_mid)
        cover = jnp.broadcast_to(in_mid * factor, (WIN, WIN, LANES))
        mid_sum[rows, :, inner:wide] += cover
        side_sum[rows, :, inner:wide] += factor - cover

    def later_window(slot, carry):
        one_window(slot, {})
        return carry

    one_window(0, weight_copies)
    lax.fori_loop(1, live, later_window, 0)
    top_out[:, 0:WIN] = mid_sum[0:HALO].astype(BF16)
    top_out[:, WIN : 2 * WIN] = side_sum[0:HALO].astype(BF16)
    bottom_out[:, 0:WIN] = mid_sum[end : end + HALO].astype(BF16)
    bottom_out[:, WIN : 2 * WIN] = side_sum[end : end + HALO].astype(BF16)
    mid_out[...] = mid_sum[HALO:end].astype(BF16)
    right_out[...] = side_sum[HALO:end, 0:HALO].astype(BF16)
    left_out[...] = side_sum[HALO:end, HALO : 2 * HALO].astype(BF16)


def windows(
    mid, before, after, from_right, from_left, w_query, w_keyval, anchor, weight
):
    tile_rows, _, channels = mid.shape
    high = tile_rows + 2 * HALO
    inner = w_query.shape[1]
    wide = inner + LANES
    vmem = pl.BlockSpec(memory_space=pltpu.VMEM)
    smem = pl.BlockSpec(memory_space=pltpu.SMEM)
    free = pl.BlockSpec(memory_space=pl.ANY)
    rim = jax.ShapeDtypeStruct((HALO, 2 * WIN, wide), BF16)
    inside = jax.ShapeDtypeStruct((tile_rows, WIN, wide), BF16)
    edge = jax.ShapeDtypeStruct((tile_rows, HALO, wide), BF16)
    slots = weight.shape[0]
    cells = WIN * WIN
    return pl.pallas_call(
        windows_kernel,
        in_specs=[smem, smem] + [free] * 3 + [vmem] * 2 + [free] * 2,
        out_specs=[vmem] * 5,
        out_shape=[rim, rim, inside, edge, edge],
        scratch_shapes=[
            pltpu.VMEM((high, 2 * WIN, channels), BF16),
            pltpu.VMEM(w_query.shape, BF16),
            pltpu.VMEM(w_keyval.shape, BF16),
            pltpu.VMEM((high, WIN, wide), F32),
            pltpu.VMEM((high, WIN, wide), F32),
            pltpu.VMEM((inner, cells), BF16),
            pltpu.SemaphoreType.DMA((3 + 3 * (inner // (2 * LANES)),)),
        ],
        compiler_params=params(61),
        cost_estimate=pl.CostEstimate(
            flops=8 * slots * 2 * cells * 3 * inner * (channels + 2 * cells),
            bytes_accessed=6 * channels * inner + 4 * high * WIN * channels,
            transcendentals=slots * cells * cells * inner // HD,
        ),
        name="windows",
    )(
        anchor, weight, mid, before, after, from_right, from_left,
        w_query, w_keyval,
    )


def fold_kernel(
    right_hbm, left_hbm, above_hbm, below_hbm, right_out, left_out, edges, sides, sems, out_sems
):
    tile_rows = right_hbm.shape[0]
    ends = (slice(0, HALO), slice(tile_rows - HALO, tile_rows))
    targets = [out.at[end] for end in ends for out in (right_out, left_out)]
    copies = [
        pltpu.make_async_copy(source, target, sems.at[i])
        for i, (source, target) in enumerate(
            [(source.at[end], edges.at[2 * i + j])
             for i, end in enumerate(ends) for j, source in enumerate((right_hbm, left_hbm))]
            + [(source.at[:, WIN : 2 * WIN], sides.at[i])
               for i, source in enumerate((above_hbm, below_hbm))]
        )
    ]
    for copy in copies:
        copy.start()
    for copy in copies:
        copy.wait()
    leaving = []
    for i in range(2):
        side = sides[i].astype(F32)
        for j in range(2):
            at = 2 * i + j
            edges[at] = (edges[at].astype(F32) + side[:, j * HALO : (j + 1) * HALO]).astype(BF16)
            leaving.append(pltpu.make_async_copy(edges.at[at], targets[at], out_sems.at[at]))
            leaving[-1].start()
    for copy in leaving:
        copy.wait()


def fold(on_right, on_left, above, below):
    wide = on_right.shape[-1]
    free = pl.BlockSpec(memory_space=pl.ANY)
    return pl.pallas_call(
        fold_kernel,
        in_specs=[free] * 4,
        out_specs=[free] * 2,
        out_shape=[jax.ShapeDtypeStruct(a.shape, a.dtype) for a in (on_right, on_left)],
        input_output_aliases={0: 0, 1: 1},
        scratch_shapes=[
            pltpu.VMEM((4, HALO, HALO, wide), BF16),
            pltpu.VMEM((2, HALO, WIN, wide), BF16),
            pltpu.SemaphoreType.DMA((6,)),
            pltpu.SemaphoreType.DMA((4,)),
        ],
        compiler_params=params(61),
        cost_estimate=pl.CostEstimate(
            flops=on_right.size, bytes_accessed=12 * on_right.size, transcendentals=0
        ),
        name="fold",
    )(on_right, on_left, above, below)


def settle_kernel(
    mid_ref, above_ref, below_ref, beside_ref, mask_ref, x_ref, known_ref, w_ref, base_ref, share_ref, own
):
    count, inner = own.shape
    tile_cols, tile_rows = mask_ref.shape
    cell = lax.broadcasted_iota(jnp.int32, (count, tile_rows), 0)
    row = lax.broadcasted_iota(jnp.int32, (count, tile_rows), 1)
    pick_row = jnp.where(cell // tile_cols == row, 1.0, 0.0).astype(BF16)
    in_row = dot_nt(pick_row, mask_ref[...].astype(F32).astype(BF16))
    cell = lax.broadcasted_iota(jnp.int32, (count, tile_cols), 0)
    col = lax.broadcasted_iota(jnp.int32, (count, tile_cols), 1)
    known_cell = jnp.sum(jnp.where(cell % tile_cols == col, in_row, 0.0), axis=1, keepdims=True) == 1

    def total(lanes):
        upper = above_ref[:, 0:WIN, lanes].astype(F32)
        lower = below_ref[:, 0:WIN, lanes].astype(F32)
        middle = mid_ref[:, :, lanes].astype(F32) + beside_ref[:, :, lanes].astype(F32)
        parts = [
            middle[:HALO] + upper,
            middle[HALO : tile_rows - HALO],
            middle[tile_rows - HALO :] + lower,
        ]
        return jnp.concatenate(parts, 0).reshape(count, LANES)

    share = 1.0 / (1.0 + total(slice(inner, inner + LANES)))
    share_ref[...] = jnp.where(known_cell, 0.0, share)
    for g in range(0, inner, LANES):
        lanes = slice(g, g + LANES)
        own[:, lanes] = (total(lanes) * share).astype(BF16)
    width = 2 * LANES
    for c in range(0, base_ref.shape[1], width):
        cols = slice(c, c + width)
        y = x_ref[:, cols].astype(F32) + dot(own[...], w_ref[:, cols])
        base_ref[:, cols] = jnp.where(known_cell, known_ref[:, cols].astype(F32), y)


def settle(mid, above, below, beside, mask, x, known, w_out):
    tile_rows, tile_cols, wide = mid.shape
    count, channels = x.shape
    vmem = pl.BlockSpec(memory_space=pltpu.VMEM)
    return pl.pallas_call(
        settle_kernel,
        in_specs=[vmem] * 8,
        out_specs=[vmem] * 2,
        out_shape=[
            jax.ShapeDtypeStruct((count, channels), F32),
            jax.ShapeDtypeStruct((count, LANES), F32),
        ],
        scratch_shapes=[pltpu.VMEM((count, wide - LANES), BF16)],
        compiler_params=params(),
        cost_estimate=pl.CostEstimate(
            flops=2**17 * count * wide, bytes_accessed=12 * count * wide, transcendentals=0
        ),
        name="settle",
    )(mid, above, below, beside, mask, x, known, w_out)


def blend_kernel(
    mixed_hbm, share_hbm, base_hbm, w_hbm, out_hbm, mixed_ref, share_ref, base_ref, w_ref, out_ref,
    blended, sems, out_sems,
):
    count, channels = base_ref.shape
    groups = mixed_ref.shape[1]
    width = 2 * LANES
    copies = [
        pltpu.make_async_copy(source, target, sems.at[i])
        for i, (source, target) in enumerate(
            ((mixed_hbm, mixed_ref), (share_hbm, share_ref), (w_hbm, w_ref), (base_hbm, base_ref))
        )
    ]
    for copy in copies:
        copy.start()
    back = lattice_order(count, False)
    for copy in copies[:2]:
        copy.wait()
    share = jnp.concatenate([share_ref[...]] * 2, 1)
    for g in range(0, groups, 2):
        lanes = slice(g * LANES, (g + 2) * LANES)
        mixed = jnp.concatenate([mixed_ref[:, g + j].reshape(count, LANES) for j in range(2)], 1)
        blended[:, lanes] = (dot(back, mixed) * share).astype(BF16)
    for copy in copies[2:]:
        copy.wait()
    outs = []
    for i, c in enumerate(range(0, channels, width)):
        cols = slice(c, c + width)
        out_ref[:, cols] = (base_ref[:, cols] + dot(blended[...], w_ref[:, cols])).astype(BF16)
        outs.append(
            pltpu.make_async_copy(out_ref.at[:, cols], out_hbm.at[:, cols], out_sems.at[i])
        )
        outs[-1].start()
    for copy in outs:
        copy.wait()


def blend(mixed, share, base, w_out):
    count, channels = base.shape
    inner = w_out.shape[0]
    arrays = (mixed, share, base, w_out)
    free = pl.BlockSpec(memory_space=pl.ANY)
    return pl.pallas_call(
        blend_kernel,
        in_specs=[free] * len(arrays),
        out_specs=free,
        out_shape=jax.ShapeDtypeStruct((count, channels), BF16),
        scratch_shapes=[pltpu.VMEM(a.shape, a.dtype) for a in arrays]
        + [
            pltpu.VMEM((count, channels), BF16),
            pltpu.VMEM((count, inner), BF16),
            pltpu.SemaphoreType.DMA((len(arrays),)),
            pltpu.SemaphoreType.DMA((channels // (2 * LANES),)),
        ],
        compiler_params=params(),
        cost_estimate=pl.CostEstimate(
            flops=2 * count * inner * (channels + count),
            bytes_accessed=2 * inner * channels + 6 * count * channels,
            transcendentals=0,
        ),
        name="blend",
    )(*arrays)


def exchange(pieces):
    return lax.all_to_all(pieces, ("row", "col"), split_axis=0, concat_axis=0, tiled=True)


def neighbours(axis):
    peers = lax.axis_size(axis)
    onward = [(i, i + 1) for i in range(peers - 1)]
    return onward, [(j, i) for i, j in onward]


def on_device(features, known, known_mask, w_query, w_keyval, w_out, win_anchor, win_weight):
    tile_rows, tile_cols, channels = features.shape
    count = tile_rows * tile_cols
    per_sub = count // SUBS
    inner = w_query.shape[1]
    devices = lax.axis_size("row") * lax.axis_size("col")
    down, up = neighbours("row")
    right, left = neighbours("col")
    x = features.reshape(count, channels)

    from_right = lax.ppermute(features[:, :HALO], "col", left)
    from_left = lax.ppermute(features[:, tile_cols - HALO :], "col", right)
    pieces = project(x, w_query, w_keyval).reshape(devices, per_sub, 3 * LANES)
    from_right, from_left, _ = lax.optimization_barrier((from_right, from_left, pieces))

    def rows_of_halo(rows):
        return jnp.concatenate([features[rows], from_right[rows], from_left[rows]], 1)

    before = lax.ppermute(rows_of_halo(slice(tile_rows - HALO, None)), "row", down)
    after = lax.ppermute(rows_of_halo(slice(0, HALO)), "row", up)

    gathered = exchange(pieces).reshape(devices * per_sub, 3 * LANES)

    top, bottom, inside, on_right, on_left = windows(
        features,
        before,
        after,
        from_right,
        from_left,
        w_query,
        w_keyval,
        win_anchor.reshape(-1, 2).T,
        win_weight.reshape(-1),
    )
    above = lax.ppermute(bottom, "row", down)
    below = lax.ppermute(top, "row", up)
    half = lattice_attend(0, gathered)
    half, above, below = lax.optimization_barrier((half, above, below))
    on_right, on_left = fold(on_right, on_left, above, below)
    gathered, half, on_right, on_left = lax.optimization_barrier((gathered, half, on_right, on_left))
    on_first = lax.ppermute(on_right, "col", right)
    on_last = lax.ppermute(on_left, "col", left)
    mixed = lattice_attend(1, gathered, half)
    mixed, on_first, on_last = lax.optimization_barrier((mixed, on_first, on_last))
    returned = exchange(mixed.reshape(devices, per_sub, LANES))
    arrived = jnp.concatenate([on_first, on_last], 1)
    base, share = settle(
        inside, above, below, arrived, known_mask.T, x, known.reshape(count, channels), w_out
    )
    returned = returned.reshape(SUBS, devices // SUBS, per_sub, LANES)
    out = blend(returned, share, base, w_out)
    return out.reshape(tile_rows, tile_cols, channels)


def solution(mesh):
    in_specs = (
        P("row", "col", None),
        P("row", "col", None),
        P("row", "col"),
        P(),
        P(),
        P(),
        P("row", "col", None, None),
        P("row", "col", None),
    )
    out_specs = P("row", "col", None)
    return jax.shard_map(
        on_device, mesh=mesh, in_specs=in_specs, out_specs=out_specs, check_vma=False
    )
```

```python
import functools
import math

import jax
import jax.numpy as jnp
from jax import lax
from jax.experimental import pallas as pl
from jax.experimental.pallas import tpu as pltpu
from jax.sharding import PartitionSpec as P

HD = 64
STRIDE = 4
WIN = 16
HALO = 8
SUBS = STRIDE * STRIDE
LANES = 128
SCALE = HD**-0.5 * math.log2(math.e)
FREE_RANGE = 100.0
VROWS = 80
QBLOCK = 2048
KBLOCK = 256
QPART = 256
AHEAD = 8
BF16 = jnp.bfloat16
F32 = jnp.float32


def dot(a, b):
    return jnp.dot(a, b, preferred_element_type=F32)


def dot_nt(a, b):
    return lax.dot_general(a, b, (((1,), (1,)), ((), ())), preferred_element_type=F32)


def whole(shape):
    return pl.BlockSpec(shape, lambda *_: (0,) * len(shape), pipeline_mode=pl.Buffered(1))


def params(mebibytes=63):
    return pltpu.CompilerParams(vmem_limit_bytes=mebibytes * 2**20)


def lattice_order(count, by_row):
    lattice = lax.broadcasted_iota(jnp.int32, (count, count), 0 if by_row else 1)
    cell = lax.broadcasted_iota(jnp.int32, (count, count), 1 if by_row else 0)
    per_sub = count // SUBS
    tile_cols = 16
    sub, place = lattice // per_sub, lattice % per_sub
    across = tile_cols // STRIDE
    row = (place // across) * STRIDE + sub // STRIDE
    col = (place % across) * STRIDE + sub % STRIDE
    return jnp.where(cell == row * tile_cols + col, 1.0, 0.0).astype(BF16)


def project_kernel(
    x_hbm, wq_hbm, wkv_hbm, out_hbm, x_ref, wq_ref, wkv_ref, ordered, queries, out_ref, sems,
    out_sems,
):
    count, channels = x_ref.shape
    inner = wq_ref.shape[1]
    width = 2 * LANES
    x_copy = pltpu.make_async_copy(x_hbm, x_ref, sems.at[0])
    x_copy.start()
    weight_copies = [
        pltpu.make_async_copy(source, target, sems.at[1 + i])
        for i, (source, target) in enumerate(((wq_hbm, wq_ref), (wkv_hbm, wkv_ref)))
    ]
    for copy in weight_copies:
        copy.start()
    order = lattice_order(count, True)
    x_copy.wait()
    ordered[...] = dot(order, x_ref[...]).astype(BF16)
    weight_copies[0].wait()
    for c in range(0, inner, width):
        queries[:, c : c + width] = dot(ordered[...], wq_ref[:, c : c + width])
    weight_copies[1].wait()
    leaving = []
    for i, c in enumerate(range(0, inner, width)):
        q = queries[:, c : c + width]
        k = dot(ordered[...], wkv_ref[:, c : c + width])
        v = dot(ordered[...], wkv_ref[:, inner + c : inner + c + width])
        for g in range(2):
            at = g * LANES
            parts = [
                jnp.concatenate([q[:, at : at + HD], k[:, at : at + HD]], 1),
                v[:, at : at + LANES],
                jnp.concatenate([q[:, at + HD : at + LANES], k[:, at + HD : at + LANES]], 1),
            ]
            for j, part in enumerate(parts):
                out_ref[:, 2 * i + g, :, j * LANES : (j + 1) * LANES] = part.astype(BF16).reshape(
                    SUBS, count // SUBS, LANES
                )
        groups = slice(2 * i, 2 * i + 2)
        leaving.append(
            pltpu.make_async_copy(out_ref.at[:, groups], out_hbm.at[:, groups], out_sems.at[i])
        )
        leaving[-1].start()
    for copy in leaving:
        copy.wait()


def project(x, w_query, w_keyval):
    count, channels = x.shape
    inner = w_query.shape[1]
    groups = inner // LANES
    shape = (SUBS, groups, count // SUBS, 3 * LANES)
    free = pl.BlockSpec(memory_space=pl.ANY)
    return pl.pallas_call(
        project_kernel,
        in_specs=[free] * 3,
        out_specs=free,
        out_shape=jax.ShapeDtypeStruct(shape, BF16),
        scratch_shapes=[
            pltpu.VMEM(x.shape, BF16),
            pltpu.VMEM(w_query.shape, BF16),
            pltpu.VMEM(w_keyval.shape, BF16),
            pltpu.VMEM(x.shape, BF16),
            pltpu.VMEM((count, inner), F32),
            pltpu.VMEM(shape, BF16),
            pltpu.SemaphoreType.DMA((3,)),
            pltpu.SemaphoreType.DMA((groups // 2,)),
        ],
        compiler_params=params(61),
        cost_estimate=pl.CostEstimate(
            flops=2 * count * channels * 3 * inner,
            bytes_accessed=2 * (3 * channels * inner + count * channels + 3 * count * inner),
            transcendentals=0,
        ),
        name="project",
    )(x, w_query, w_keyval)


def lattice_kernel(head, qk_ref, v_ref, *refs):
    if head == 0:
        o_ref, queries_t, values_t, free = refs
    else:
        other_ref, o_ref, queries_t, values_t, free = refs
    count = qk_ref.shape[0]
    block = o_ref.shape[1 - head]
    step = pl.program_id(0)

    @pl.when(step == 0)
    def _():
        row = lax.broadcasted_iota(jnp.int32, (LANES, LANES), 0)
        lane = lax.broadcasted_iota(jnp.int32, (LANES, LANES), 1)
        to_keys = jnp.where(row == lane + HD, 1.0, 0.0).astype(BF16)
        queries_t[...] = dot_nt(to_keys, qk_ref[...]).astype(BF16)
        own = (row[:HD] + head * HD == lane[:HD]).astype(F32).astype(BF16)
        values_t[0:HD] = dot_nt(own, v_ref[...]).astype(BF16)
        squares = qk_ref[...].astype(F32)
        squares = (squares * squares).astype(BF16)
        halves = ((row[:VROWS - HD] < 8) == (lane[:VROWS - HD] < HD)).astype(F32).astype(BF16)
        norms = dot_nt(halves, squares)
        bound = jnp.max(norms[:8]) * jnp.max(norms[8:]) * 1.02
        free[0] = (bound * (SCALE * SCALE) <= FREE_RANGE * FREE_RANGE).astype(jnp.int32)
        values_t[HD:VROWS] = jnp.ones((VROWS - HD, count), BF16)

    cols = pl.ds(pl.multiple_of(step * block, block), block)

    def finish(total):
        out = total[:HD] / total[HD : HD + 1]
        if head == 0:
            o_ref[...] = out.astype(BF16)
        else:
            o_ref[...] = jnp.concatenate([other_ref[...].astype(F32), out], 0).T.astype(BF16)

    @pl.when(free[0] == 1)
    def _():
        parts = block // QPART
        items = [(c, j) for c in range(0, count, KBLOCK) for j in range(parts)]
        queries = [
            queries_t[:, pl.ds(pl.multiple_of(step * block + j * QPART, QPART), QPART)]
            for j in range(parts)
        ]

        def score(i):
            c, j = items[i]
            return dot(qk_ref[c : c + KBLOCK, :], queries[j])

        totals = [None] * parts
        ahead = [score(i) for i in range(AHEAD)]
        for i, (c, j) in enumerate(items):
            now = ahead.pop(0)
            if i + AHEAD < len(items):
                ahead.append(score(i + AHEAD))
            weights = jnp.exp2(now * SCALE).astype(BF16)
            part = dot(values_t[:, c : c + KBLOCK], weights)
            totals[j] = part if totals[j] is None else totals[j] + part
        finish(jnp.concatenate(totals, 1))

    @pl.when(free[0] == 0)
    def _():
        chunks = count // KBLOCK
        q = queries_t[:, cols]

        def score(c):
            return dot(qk_ref[pl.ds(pl.multiple_of(c * KBLOCK, KBLOCK), KBLOCK), :], q)

        def top(c, m):
            return jnp.maximum(m, jnp.max(score(c), axis=0, keepdims=True))

        m = lax.fori_loop(0, chunks, top, jnp.full((1, block), -jnp.inf, F32))

        def add(c, total):
            weights = jnp.exp2((score(c) - m) * SCALE).astype(BF16)
            rows = pl.ds(pl.multiple_of(c * KBLOCK, KBLOCK), KBLOCK)
            return total + dot(values_t[:, rows], weights)

        finish(lax.fori_loop(0, chunks, add, jnp.zeros((VROWS, block), F32)))


def lattice_attend(head, x, other=None):
    count = x.shape[0]
    in_specs = [
        pl.BlockSpec((count, LANES), lambda i: (0, 2 * head), pipeline_mode=pl.Buffered(1)),
        pl.BlockSpec((count, LANES), lambda i: (0, 1), pipeline_mode=pl.Buffered(1)),
    ]
    args = [x, x]
    if head == 0:
        out_spec = pl.BlockSpec((HD, QBLOCK), lambda i: (0, i))
        out_shape = (HD, count)
    else:
        in_specs.append(pl.BlockSpec((HD, QBLOCK), lambda i: (0, i)))
        args.append(other)
        out_spec = pl.BlockSpec((QBLOCK, LANES), lambda i: (i, 0))
        out_shape = (count, LANES)
    return pl.pallas_call(
        functools.partial(lattice_kernel, head),
        grid=(count // QBLOCK,),
        in_specs=in_specs,
        out_specs=out_spec,
        out_shape=jax.ShapeDtypeStruct(out_shape, BF16),
        scratch_shapes=[
            pltpu.VMEM((LANES, count), BF16),
            pltpu.VMEM((VROWS, count), BF16),
            pltpu.SMEM((1,), jnp.int32),
        ],
        compiler_params=params(63 if head else 61),
        cost_estimate=pl.CostEstimate(
            flops=4 * 4 * count * count * HD,
            bytes_accessed=6 * count * LANES,
            transcendentals=count * count,
        ),
        name="lattice_attend_" + str(head),
    )(*args)


def windows_kernel(
    even, anchor, weight, mid_hbm, rows_1_hbm, rows_2_hbm, cols_1_ref, cols_2_ref,
    wq_hbm, wkv_hbm, rim_1_out, rim_2_out, mid_out, ends_1_out, ends_2_out,
    middle_1_out, middle_2_out, held, wq_ref, wkv_ref, mid_sum, side_sum, results_t, sems,
):
    channels, inner = wq_ref.shape
    cells = WIN * WIN
    wide = inner + LANES
    tile_rows = mid_hbm.shape[0]
    end = tile_rows + HALO
    pair_lanes = 2 * LANES
    row_even, col_even = even[0] == 1, even[1] == 1
    rows_1 = pl.ds(jnp.where(row_even, end, 0), HALO)
    rows_2 = pl.ds(jnp.where(row_even, 0, end), HALO)
    copies = [
        pltpu.make_async_copy(source, target, sems.at[i])
        for i, (source, target) in enumerate(
            (
                (mid_hbm, held.at[HALO:end, 0:WIN]),
                (rows_1_hbm, held.at[rows_1]),
                (rows_2_hbm, held.at[rows_2]),
            )
        )
    ]
    weight_copies = {}
    for g in range(0, inner, pair_lanes):
        for part, (source, target, at) in enumerate(
            ((wq_hbm, wq_ref, g), (wkv_hbm, wkv_ref, g), (wkv_hbm, wkv_ref, inner + g))
        ):
            cols = slice(at, at + pair_lanes)
            sem = sems.at[len(copies) + 3 * (g // pair_lanes) + part]
            weight_copies.setdefault(g, []).append(
                pltpu.make_async_copy(source.at[:, cols], target.at[:, cols], sem)
            )
    for copy in copies + sum(weight_copies.values(), []):
        copy.start()
    mid_sum[...] = jnp.zeros(mid_sum.shape, F32)
    side_sum[...] = jnp.zeros(side_sum.shape, F32)
    for row in range(0, tile_rows, HALO):
        rows = slice(row, row + HALO)
        pair = (cols_1_ref[rows].astype(F32), cols_2_ref[rows].astype(F32))
        pair = (jnp.where(col_even, *pair), jnp.where(col_even, *pair[::-1]))
        held[HALO + row : 2 * HALO + row, WIN : 2 * WIN] = jnp.concatenate(pair, 1).astype(BF16)
    for copy in copies:
        copy.wait()
    slots = weight.shape[0]
    live = sum((weight[s] > 0).astype(jnp.int32) for s in range(slots))
    first = lax.broadcasted_iota(jnp.int32, (cells, LANES), 1) < HD
    ones = jnp.ones((VROWS - HD, cells), BF16)

    column = lax.broadcasted_iota(jnp.int32, (1, WIN, 1), 1)
    across = lax.broadcasted_iota(jnp.int32, (cells, cells), 0)
    along = lax.broadcasted_iota(jnp.int32, (cells, cells), 1)
    diagonal = jnp.where(across == along, 1.0, 0.0)

    def one_window(slot, arriving):
        top = anchor[0, slot] + HALO
        left = anchor[1, slot]
        factor = weight[slot].astype(F32)
        rows = pl.ds(top, WIN)
        in_mid = ((column >= left) & (column < left + WIN)).astype(F32)
        own = in_mid.astype(BF16)
        x = held[rows, 0:WIN] * own + held[rows, WIN : 2 * WIN] * (1 - own)
        x = x.reshape(cells, channels)

        def project(g):
            for copy in arriving.get(g, ()):
                copy.wait()
            q = dot(x, wq_ref[:, g : g + 2 * LANES]).astype(BF16)
            k = dot(x, wkv_ref[:, g : g + 2 * LANES]).astype(BF16)
            v = dot(x, wkv_ref[:, inner + g : inner + g + 2 * LANES])
            return q, k, v.T.astype(BF16)

        def scores(q, k, j):
            lanes = slice(j // 2 * LANES, (j // 2 + 1) * LANES)
            own = jnp.where(first if j % 2 == 0 else ~first, q[:, lanes], jnp.zeros((), BF16))
            return dot_nt(k[:, lanes], own)

        def mix(s, v_t, g, j):
            e = jnp.exp2((s - jnp.max(s, axis=0, keepdims=True)) * SCALE).astype(BF16)
            o = dot(jnp.concatenate([v_t[j * HD : (j + 1) * HD], ones], 0), e)
            at = g + j * HD
            results_t[at : at + HD] = (o[:HD] / o[HD : HD + 1]).astype(BF16)

        later = project(0)
        for g in range(0, inner, 2 * LANES):
            q, k, v_t = later
            now = [scores(q, k, j) for j in range(4)]
            if g + 2 * LANES < inner:
                later = project(g + 2 * LANES)
            for j in range(4):
                mix(now[j], v_t, g, j)
        placed = dot_nt((diagonal * factor).astype(BF16), results_t[...]).reshape(WIN, WIN, inner)
        mid_sum[rows, :, 0:inner] += placed * in_mid
        side_sum[rows, :, 0:inner] += placed * (1.0 - in_mid)
        cover = jnp.broadcast_to(in_mid * factor, (WIN, WIN, LANES))
        mid_sum[rows, :, inner:wide] += cover
        side_sum[rows, :, inner:wide] += factor - cover

    def later_window(slot, carry):
        one_window(slot, {})
        return carry

    one_window(0, weight_copies)
    lax.fori_loop(1, live, later_window, 0)
    for out, rows in ((rim_1_out, rows_1), (rim_2_out, rows_2)):
        out[:, 0:WIN] = mid_sum[rows].astype(BF16)
        out[:, WIN : 2 * WIN] = side_sum[rows].astype(BF16)
    mid_out[...] = mid_sum[HALO:end].astype(BF16)

    def edges(rows):
        right, left = side_sum[rows, 0:HALO], side_sum[rows, HALO : 2 * HALO]
        return jnp.where(col_even, right, left).astype(BF16), jnp.where(col_even, left, right).astype(BF16)

    ends_1_out[0:HALO], ends_2_out[0:HALO] = edges(slice(HALO, 2 * HALO))
    ends_1_out[HALO : 2 * HALO], ends_2_out[HALO : 2 * HALO] = edges(slice(end - HALO, end))
    middle_1_out[...], middle_2_out[...] = edges(slice(2 * HALO, end - HALO))


def windows(
    even, mid, rows_1, rows_2, cols_1, cols_2, w_query, w_keyval, anchor, weight
):
    tile_rows, _, channels = mid.shape
    high = tile_rows + 2 * HALO
    inner = w_query.shape[1]
    wide = inner + LANES
    vmem = pl.BlockSpec(memory_space=pltpu.VMEM)
    smem = pl.BlockSpec(memory_space=pltpu.SMEM)
    free = pl.BlockSpec(memory_space=pl.ANY)
    rim = jax.ShapeDtypeStruct((HALO, 2 * WIN, wide), BF16)
    inside = jax.ShapeDtypeStruct((tile_rows, WIN, wide), BF16)
    ends = jax.ShapeDtypeStruct((2 * HALO, HALO, wide), BF16)
    middle = jax.ShapeDtypeStruct((tile_rows - 2 * HALO, HALO, wide), BF16)
    slots = weight.shape[0]
    cells = WIN * WIN
    return pl.pallas_call(
        windows_kernel,
        in_specs=[smem] * 3 + [free] * 3 + [vmem] * 2 + [free] * 2,
        out_specs=[vmem] * 7,
        out_shape=[rim, rim, inside, ends, ends, middle, middle],
        scratch_shapes=[
            pltpu.VMEM((high, 2 * WIN, channels), BF16),
            pltpu.VMEM(w_query.shape, BF16),
            pltpu.VMEM(w_keyval.shape, BF16),
            pltpu.VMEM((high, WIN, wide), F32),
            pltpu.VMEM((high, WIN, wide), F32),
            pltpu.VMEM((inner, cells), BF16),
            pltpu.SemaphoreType.DMA((3 + 3 * (inner // (2 * LANES)),)),
        ],
        compiler_params=params(61),
        cost_estimate=pl.CostEstimate(
            flops=8 * slots * 2 * cells * 3 * inner * (channels + 2 * cells),
            bytes_accessed=6 * channels * inner + 4 * high * WIN * channels,
            transcendentals=slots * cells * cells * inner // HD,
        ),
        name="windows",
    )(
        even, anchor, weight, mid, rows_1, rows_2, cols_1, cols_2,
        w_query, w_keyval,
    )


def settle_kernel(
    even, mid_ref, rim_1_ref, rim_2_ref, beside_ref, mask_ref, x_ref, known_ref, w_ref, base_ref, share_ref, own
):
    count, inner = own.shape
    tile_cols, tile_rows = mask_ref.shape
    cell = lax.broadcasted_iota(jnp.int32, (count, tile_rows), 0)
    row = lax.broadcasted_iota(jnp.int32, (count, tile_rows), 1)
    pick_row = jnp.where(cell // tile_cols == row, 1.0, 0.0).astype(BF16)
    in_row = dot_nt(pick_row, mask_ref[...].astype(F32).astype(BF16))
    cell = lax.broadcasted_iota(jnp.int32, (count, tile_cols), 0)
    col = lax.broadcasted_iota(jnp.int32, (count, tile_cols), 1)
    known_cell = jnp.sum(jnp.where(cell % tile_cols == col, in_row, 0.0), axis=1, keepdims=True) == 1

    def total(lanes):
        rims = [ref[:, 0:WIN, lanes].astype(F32) for ref in (rim_1_ref, rim_2_ref)]
        lower, upper = jnp.where(even[0] == 1, *rims), jnp.where(even[0] == 1, *rims[::-1])
        middle = mid_ref[:, :, lanes].astype(F32) + beside_ref[:, :, lanes].astype(F32)
        parts = [
            middle[:HALO] + upper,
            middle[HALO : tile_rows - HALO],
            middle[tile_rows - HALO :] + lower,
        ]
        return jnp.concatenate(parts, 0).reshape(count, LANES)

    share = 1.0 / (1.0 + total(slice(inner, inner + LANES)))
    share_ref[...] = jnp.where(known_cell, 0.0, share)
    for g in range(0, inner, LANES):
        lanes = slice(g, g + LANES)
        own[:, lanes] = (total(lanes) * share).astype(BF16)
    width = 2 * LANES
    for c in range(0, base_ref.shape[1], width):
        cols = slice(c, c + width)
        y = x_ref[:, cols].astype(F32) + dot(own[...], w_ref[:, cols])
        base_ref[:, cols] = jnp.where(known_cell, known_ref[:, cols].astype(F32), y)


def settle(even, mid, rim_1, rim_2, beside, mask, x, known, w_out):
    tile_rows, tile_cols, wide = mid.shape
    count, channels = x.shape
    vmem = pl.BlockSpec(memory_space=pltpu.VMEM)
    return pl.pallas_call(
        settle_kernel,
        in_specs=[pl.BlockSpec(memory_space=pltpu.SMEM)] + [vmem] * 8,
        out_specs=[vmem] * 2,
        out_shape=[
            jax.ShapeDtypeStruct((count, channels), F32),
            jax.ShapeDtypeStruct((count, LANES), F32),
        ],
        scratch_shapes=[pltpu.VMEM((count, wide - LANES), BF16)],
        compiler_params=params(),
        cost_estimate=pl.CostEstimate(
            flops=2**17 * count * wide, bytes_accessed=12 * count * wide, transcendentals=0
        ),
        name="settle",
    )(even, mid, rim_1, rim_2, beside, mask, x, known, w_out)


def blend_kernel(
    mixed_hbm, share_hbm, base_hbm, w_hbm, out_hbm, mixed_ref, share_ref, base_ref, w_ref, out_ref,
    blended, sems, out_sems,
):
    count, channels = base_ref.shape
    groups = mixed_ref.shape[1]
    width = 2 * LANES
    copies = [
        pltpu.make_async_copy(source, target, sems.at[i])
        for i, (source, target) in enumerate(
            ((mixed_hbm, mixed_ref), (share_hbm, share_ref), (w_hbm, w_ref), (base_hbm, base_ref))
        )
    ]
    for copy in copies:
        copy.start()
    back = lattice_order(count, False)
    for copy in copies[:2]:
        copy.wait()
    share = jnp.concatenate([share_ref[...]] * 2, 1)
    for g in range(0, groups, 2):
        lanes = slice(g * LANES, (g + 2) * LANES)
        mixed = jnp.concatenate([mixed_ref[:, g + j].reshape(count, LANES) for j in range(2)], 1)
        blended[:, lanes] = (dot(back, mixed) * share).astype(BF16)
    for copy in copies[2:]:
        copy.wait()
    outs = []
    for i, c in enumerate(range(0, channels, width)):
        cols = slice(c, c + width)
        out_ref[:, cols] = (base_ref[:, cols] + dot(blended[...], w_ref[:, cols])).astype(BF16)
        outs.append(
            pltpu.make_async_copy(out_ref.at[:, cols], out_hbm.at[:, cols], out_sems.at[i])
        )
        outs[-1].start()
    for copy in outs:
        copy.wait()


def blend(mixed, share, base, w_out):
    count, channels = base.shape
    inner = w_out.shape[0]
    arrays = (mixed, share, base, w_out)
    free = pl.BlockSpec(memory_space=pl.ANY)
    return pl.pallas_call(
        blend_kernel,
        in_specs=[free] * len(arrays),
        out_specs=free,
        out_shape=jax.ShapeDtypeStruct((count, channels), BF16),
        scratch_shapes=[pltpu.VMEM(a.shape, a.dtype) for a in arrays]
        + [
            pltpu.VMEM((count, channels), BF16),
            pltpu.VMEM((count, inner), BF16),
            pltpu.SemaphoreType.DMA((len(arrays),)),
            pltpu.SemaphoreType.DMA((channels // (2 * LANES),)),
        ],
        compiler_params=params(),
        cost_estimate=pl.CostEstimate(
            flops=2 * count * inner * (channels + count),
            bytes_accessed=2 * inner * channels + 6 * count * channels,
            transcendentals=0,
        ),
        name="blend",
    )(*arrays)


def exchange(pieces):
    return lax.all_to_all(pieces, ("row", "col"), split_axis=0, concat_axis=0, tiled=True)


def meet(axis, first, second):
    peers = lax.axis_size(axis)
    met = []
    for start, array in ((0, first), (1, second)):
        pairs = [(i, i + 1) for i in range(start, peers - 1, 2)]
        met.append(lax.ppermute(array, axis, pairs + [(j, i) for i, j in pairs]))
    return met


def on_device(features, known, known_mask, w_query, w_keyval, w_out, win_anchor, win_weight):
    tile_rows, tile_cols, channels = features.shape
    count = tile_rows * tile_cols
    per_sub = count // SUBS
    inner = w_query.shape[1]
    devices = lax.axis_size("row") * lax.axis_size("col")
    row_even, col_even = (lax.axis_index(axis) % 2 == 0 for axis in ("row", "col"))
    even = jnp.stack([row_even, col_even]).astype(jnp.int32)

    def swap(flag, lower, higher):
        return jnp.where(flag, higher, lower), jnp.where(flag, lower, higher)

    x = features.reshape(count, channels)

    cols = meet("col", *swap(col_even, features[:, :HALO], features[:, tile_cols - HALO :]))
    pieces = project(x, w_query, w_keyval).reshape(devices, per_sub, 3 * LANES)
    cols_1, cols_2, _ = lax.optimization_barrier((*cols, pieces))
    from_right, from_left = swap(col_even, cols_2, cols_1)

    def rows_of_halo(rows):
        return jnp.concatenate([features[rows], from_right[rows], from_left[rows]], 1)

    first_rows, last_rows = rows_of_halo(slice(0, HALO)), rows_of_halo(slice(tile_rows - HALO, None))
    rows_1, rows_2 = meet("row", *swap(row_even, first_rows, last_rows))

    gathered = exchange(pieces).reshape(devices * per_sub, 3 * LANES)

    rim_1, rim_2, inside, ends_1, ends_2, middle_1, middle_2 = windows(
        even,
        features,
        rows_1,
        rows_2,
        cols_1,
        cols_2,
        w_query,
        w_keyval,
        win_anchor.reshape(-1, 2).T,
        win_weight.reshape(-1),
    )
    rim_1, rim_2 = meet("row", rim_1, rim_2)
    middle_1, middle_2 = meet("col", middle_1, middle_2)
    half = lattice_attend(0, gathered)
    half, rim_1, rim_2, middle_1, middle_2 = lax.optimization_barrier(
        (half, rim_1, rim_2, middle_1, middle_2)
    )
    below, above = swap(row_even, rim_2, rim_1)

    def with_rims(ends, cols):
        rims = jnp.concatenate([above[:, cols], below[:, cols]], 0)
        return ends.astype(F32) + rims.astype(F32)

    right, left = slice(WIN, WIN + HALO), slice(WIN + HALO, 2 * WIN)
    ends_1 = jnp.where(col_even, with_rims(ends_1, right), with_rims(ends_1, left)).astype(BF16)
    ends_2 = jnp.where(col_even, with_rims(ends_2, left), with_rims(ends_2, right)).astype(BF16)
    gathered, half, ends_1, ends_2 = lax.optimization_barrier((gathered, half, ends_1, ends_2))
    ends_1, ends_2 = meet("col", ends_1, ends_2)
    mixed = lattice_attend(1, gathered, half)
    mixed, ends_1, ends_2 = lax.optimization_barrier((mixed, ends_1, ends_2))
    returned = exchange(mixed.reshape(devices, per_sub, LANES))
    ends = jnp.concatenate(swap(col_even, ends_1, ends_2), 1)
    middle = jnp.concatenate(swap(col_even, middle_1, middle_2), 1)
    arrived = jnp.concatenate([ends[:HALO], middle, ends[HALO:]], 0)
    base, share = settle(
        even, inside, rim_1, rim_2, arrived, known_mask.T, x, known.reshape(count, channels), w_out
    )
    returned = returned.reshape(SUBS, devices // SUBS, per_sub, LANES)
    out = blend(returned, share, base, w_out)
    return out.reshape(tile_rows, tile_cols, channels)


def solution(mesh):
    in_specs = (
        P("row", "col", None),
        P("row", "col", None),
        P("row", "col"),
        P(),
        P(),
        P(),
        P("row", "col", None, None),
        P("row", "col", None),
    )
    out_specs = P("row", "col", None)
    return jax.shard_map(
        on_device, mesh=mesh, in_specs=in_specs, out_specs=out_specs, check_vma=False
    )
```

```python
import functools
import math

import jax
import jax.numpy as jnp
from jax import lax
from jax.experimental import pallas as pl
from jax.experimental.pallas import tpu as pltpu
from jax.sharding import PartitionSpec as P

HD = 64
STRIDE = 4
WIN = 16
HALO = 8
SUBS = STRIDE * STRIDE
LANES = 128
SCALE = HD**-0.5 * math.log2(math.e)
FREE_RANGE = 100.0
VROWS = 80
QBLOCK = 2048
KBLOCK = 256
QPART = 256
AHEAD = 8
BF16 = jnp.bfloat16
F32 = jnp.float32


def dot(a, b):
    return jnp.dot(a, b, preferred_element_type=F32)


def dot_nt(a, b):
    return lax.dot_general(a, b, (((1,), (1,)), ((), ())), preferred_element_type=F32)


def whole(shape):
    return pl.BlockSpec(shape, lambda *_: (0,) * len(shape), pipeline_mode=pl.Buffered(1))


def params(mebibytes=63):
    return pltpu.CompilerParams(vmem_limit_bytes=mebibytes * 2**20)


def lattice_order(count, by_row):
    lattice = lax.broadcasted_iota(jnp.int32, (count, count), 0 if by_row else 1)
    cell = lax.broadcasted_iota(jnp.int32, (count, count), 1 if by_row else 0)
    per_sub = count // SUBS
    tile_cols = 16
    sub, place = lattice // per_sub, lattice % per_sub
    across = tile_cols // STRIDE
    row = (place // across) * STRIDE + sub // STRIDE
    col = (place % across) * STRIDE + sub % STRIDE
    return jnp.where(cell == row * tile_cols + col, 1.0, 0.0).astype(BF16)


def project_kernel(
    x_hbm, wq_hbm, wkv_hbm, out_hbm, x_ref, wq_ref, wkv_ref, ordered, queries, out_ref, sems,
    out_sems,
):
    count, channels = x_ref.shape
    inner = wq_ref.shape[1]
    width = 2 * LANES
    x_copy = pltpu.make_async_copy(x_hbm, x_ref, sems.at[0])
    x_copy.start()
    weight_copies = [
        pltpu.make_async_copy(source, target, sems.at[1 + i])
        for i, (source, target) in enumerate(((wq_hbm, wq_ref), (wkv_hbm, wkv_ref)))
    ]
    for copy in weight_copies:
        copy.start()
    order = lattice_order(count, True)
    x_copy.wait()
    ordered[...] = dot(order, x_ref[...]).astype(BF16)
    weight_copies[0].wait()
    for c in range(0, inner, width):
        queries[:, c : c + width] = dot(ordered[...], wq_ref[:, c : c + width])
    weight_copies[1].wait()
    leaving = []
    for i, c in enumerate(range(0, inner, width)):
        q = queries[:, c : c + width]
        k = dot(ordered[...], wkv_ref[:, c : c + width])
        v = dot(ordered[...], wkv_ref[:, inner + c : inner + c + width])
        for g in range(2):
            at = g * LANES
            parts = [
                jnp.concatenate([q[:, at : at + HD], k[:, at : at + HD]], 1),
                v[:, at : at + LANES],
                jnp.concatenate([q[:, at + HD : at + LANES], k[:, at + HD : at + LANES]], 1),
            ]
            for j, part in enumerate(parts):
                out_ref[:, 2 * i + g, :, j * LANES : (j + 1) * LANES] = part.astype(BF16).reshape(
                    SUBS, count // SUBS, LANES
                )
        groups = slice(2 * i, 2 * i + 2)
        leaving.append(
            pltpu.make_async_copy(out_ref.at[:, groups], out_hbm.at[:, groups], out_sems.at[i])
        )
        leaving[-1].start()
    for copy in leaving:
        copy.wait()


def project(x, w_query, w_keyval):
    count, channels = x.shape
    inner = w_query.shape[1]
    groups = inner // LANES
    shape = (SUBS, groups, count // SUBS, 3 * LANES)
    free = pl.BlockSpec(memory_space=pl.ANY)
    return pl.pallas_call(
        project_kernel,
        in_specs=[free] * 3,
        out_specs=free,
        out_shape=jax.ShapeDtypeStruct(shape, BF16),
        scratch_shapes=[
            pltpu.VMEM(x.shape, BF16),
            pltpu.VMEM(w_query.shape, BF16),
            pltpu.VMEM(w_keyval.shape, BF16),
            pltpu.VMEM(x.shape, BF16),
            pltpu.VMEM((count, inner), F32),
            pltpu.VMEM(shape, BF16),
            pltpu.SemaphoreType.DMA((3,)),
            pltpu.SemaphoreType.DMA((groups // 2,)),
        ],
        compiler_params=params(61),
        cost_estimate=pl.CostEstimate(
            flops=2 * count * channels * 3 * inner,
            bytes_accessed=2 * (3 * channels * inner + count * channels + 3 * count * inner),
            transcendentals=0,
        ),
        name="project",
    )(x, w_query, w_keyval)


def lattice_kernel(head, qk_ref, v_ref, *refs):
    if head == 0:
        o_ref, queries_t, values_t, free = refs
    else:
        other_ref, o_ref, queries_t, values_t, free = refs
    count = qk_ref.shape[0]
    block = o_ref.shape[1 - head]
    step = pl.program_id(0)

    @pl.when(step == 0)
    def _():
        row = lax.broadcasted_iota(jnp.int32, (LANES, LANES), 0)
        lane = lax.broadcasted_iota(jnp.int32, (LANES, LANES), 1)
        to_keys = jnp.where(row == lane + HD, 1.0, 0.0).astype(BF16)
        queries_t[...] = dot_nt(to_keys, qk_ref[...]).astype(BF16)
        own = (row[:HD] + head * HD == lane[:HD]).astype(F32).astype(BF16)
        values_t[0:HD] = dot_nt(own, v_ref[...]).astype(BF16)
        squares = qk_ref[...].astype(F32)
        squares = (squares * squares).astype(BF16)
        halves = ((row[:VROWS - HD] < 8) == (lane[:VROWS - HD] < HD)).astype(F32).astype(BF16)
        norms = dot_nt(halves, squares)
        bound = jnp.max(norms[:8]) * jnp.max(norms[8:]) * 1.02
        free[0] = (bound * (SCALE * SCALE) <= FREE_RANGE * FREE_RANGE).astype(jnp.int32)
        values_t[HD:VROWS] = jnp.ones((VROWS - HD, count), BF16)

    cols = pl.ds(pl.multiple_of(step * block, block), block)

    def finish(total):
        out = total[:HD] / total[HD : HD + 1]
        if head == 0:
            o_ref[...] = out.astype(BF16)
        else:
            o_ref[...] = jnp.concatenate([other_ref[...].astype(F32), out], 0).T.astype(BF16)

    @pl.when(free[0] == 1)
    def _():
        parts = block // QPART
        items = [(c, j) for c in range(0, count, KBLOCK) for j in range(parts)]
        queries = [
            queries_t[:, pl.ds(pl.multiple_of(step * block + j * QPART, QPART), QPART)]
            for j in range(parts)
        ]

        def score(i):
            c, j = items[i]
            return dot(qk_ref[c : c + KBLOCK, :], queries[j])

        totals = [None] * parts
        ahead = [score(i) for i in range(AHEAD)]
        for i, (c, j) in enumerate(items):
            now = ahead.pop(0)
            if i + AHEAD < len(items):
                ahead.append(score(i + AHEAD))
            weights = jnp.exp2(now * SCALE).astype(BF16)
            part = dot(values_t[:, c : c + KBLOCK], weights)
            totals[j] = part if totals[j] is None else totals[j] + part
        finish(jnp.concatenate(totals, 1))

    @pl.when(free[0] == 0)
    def _():
        chunks = count // KBLOCK
        q = queries_t[:, cols]

        def score(c):
            return dot(qk_ref[pl.ds(pl.multiple_of(c * KBLOCK, KBLOCK), KBLOCK), :], q)

        def top(c, m):
            return jnp.maximum(m, jnp.max(score(c), axis=0, keepdims=True))

        m = lax.fori_loop(0, chunks, top, jnp.full((1, block), -jnp.inf, F32))

        def add(c, total):
            weights = jnp.exp2((score(c) - m) * SCALE).astype(BF16)
            rows = pl.ds(pl.multiple_of(c * KBLOCK, KBLOCK), KBLOCK)
            return total + dot(values_t[:, rows], weights)

        finish(lax.fori_loop(0, chunks, add, jnp.zeros((VROWS, block), F32)))


def lattice_attend(head, x, other=None):
    count = x.shape[0]
    in_specs = [
        pl.BlockSpec((count, LANES), lambda i: (0, 2 * head), pipeline_mode=pl.Buffered(1)),
        pl.BlockSpec((count, LANES), lambda i: (0, 1), pipeline_mode=pl.Buffered(1)),
    ]
    args = [x, x]
    if head == 0:
        out_spec = pl.BlockSpec((HD, QBLOCK), lambda i: (0, i))
        out_shape = (HD, count)
    else:
        in_specs.append(pl.BlockSpec((HD, QBLOCK), lambda i: (0, i)))
        args.append(other)
        out_spec = pl.BlockSpec((QBLOCK, LANES), lambda i: (i, 0))
        out_shape = (count, LANES)
    return pl.pallas_call(
        functools.partial(lattice_kernel, head),
        grid=(count // QBLOCK,),
        in_specs=in_specs,
        out_specs=out_spec,
        out_shape=jax.ShapeDtypeStruct(out_shape, BF16),
        scratch_shapes=[
            pltpu.VMEM((LANES, count), BF16),
            pltpu.VMEM((VROWS, count), BF16),
            pltpu.SMEM((1,), jnp.int32),
        ],
        compiler_params=params(63 if head else 61),
        cost_estimate=pl.CostEstimate(
            flops=4 * 4 * count * count * HD,
            bytes_accessed=6 * count * LANES,
            transcendentals=count * count,
        ),
        name="lattice_attend_" + str(head),
    )(*args)


def windows_kernel(
    even, anchor, weight, mid_hbm, rows_1_hbm, rows_2_hbm, cols_1_ref, cols_2_ref,
    wq_hbm, wkv_hbm, rim_1_out, rim_2_out, mid_out, ends_1_out, ends_2_out,
    middle_1_out, middle_2_out, held, wq_ref, wkv_ref, mid_sum, side_sum, results_t, sems,
):
    channels, inner = wq_ref.shape
    cells = WIN * WIN
    wide = inner + LANES
    tile_rows = mid_hbm.shape[0]
    end = tile_rows + HALO
    pair_lanes = 2 * LANES
    row_even, col_even = even[0] == 1, even[1] == 1
    rows_1 = pl.ds(jnp.where(row_even, end, 0), HALO)
    rows_2 = pl.ds(jnp.where(row_even, 0, end), HALO)
    copies = [
        pltpu.make_async_copy(source, target, sems.at[i])
        for i, (source, target) in enumerate(
            (
                (mid_hbm, held.at[HALO:end, 0:WIN]),
                (rows_1_hbm, held.at[rows_1]),
                (rows_2_hbm, held.at[rows_2]),
            )
        )
    ]
    weight_copies = {}
    for g in range(0, inner, pair_lanes):
        for part, (source, target, at) in enumerate(
            ((wq_hbm, wq_ref, g), (wkv_hbm, wkv_ref, g), (wkv_hbm, wkv_ref, inner + g))
        ):
            cols = slice(at, at + pair_lanes)
            sem = sems.at[len(copies) + 3 * (g // pair_lanes) + part]
            weight_copies.setdefault(g, []).append(
                pltpu.make_async_copy(source.at[:, cols], target.at[:, cols], sem)
            )
    for copy in copies + sum(weight_copies.values(), []):
        copy.start()
    mid_sum[...] = jnp.zeros(mid_sum.shape, F32)
    side_sum[...] = jnp.zeros(side_sum.shape, F32)
    for row in range(0, tile_rows, HALO):
        rows = slice(row, row + HALO)
        pair = (cols_1_ref[rows].astype(F32), cols_2_ref[rows].astype(F32))
        pair = (jnp.where(col_even, *pair), jnp.where(col_even, *pair[::-1]))
        held[HALO + row : 2 * HALO + row, WIN : 2 * WIN] = jnp.concatenate(pair, 1).astype(BF16)
    for copy in copies:
        copy.wait()
    slots = weight.shape[0]
    live = sum((weight[s] > 0).astype(jnp.int32) for s in range(slots))
    first = lax.broadcasted_iota(jnp.int32, (cells, LANES), 1) < HD
    ones = jnp.ones((VROWS - HD, cells), BF16)

    column = lax.broadcasted_iota(jnp.int32, (1, WIN, 1), 1)
    across = lax.broadcasted_iota(jnp.int32, (cells, cells), 0)
    along = lax.broadcasted_iota(jnp.int32, (cells, cells), 1)
    diagonal = jnp.where(across == along, 1.0, 0.0)

    def one_window(slot, carry):
        top = anchor[0, slot] + HALO
        left = anchor[1, slot]
        factor = weight[slot].astype(F32)
        rows = pl.ds(top, WIN)
        in_mid = ((column >= left) & (column < left + WIN)).astype(F32)
        own = in_mid.astype(BF16)
        x = held[rows, 0:WIN] * own + held[rows, WIN : 2 * WIN] * (1 - own)
        x = x.reshape(cells, channels)

        def project(g):
            q = dot(x, wq_ref[:, g : g + 2 * LANES]).astype(BF16)
            k = dot(x, wkv_ref[:, g : g + 2 * LANES]).astype(BF16)
            v = dot(x, wkv_ref[:, inner + g : inner + g + 2 * LANES])
            return q, k, v.T.astype(BF16)

        def scores(q, k, j):
            lanes = slice(j // 2 * LANES, (j // 2 + 1) * LANES)
            own = jnp.where(first if j % 2 == 0 else ~first, q[:, lanes], jnp.zeros((), BF16))
            return dot_nt(k[:, lanes], own)

        def mix(s, v_t, g, j):
            e = jnp.exp2((s - jnp.max(s, axis=0, keepdims=True)) * SCALE).astype(BF16)
            o = dot(jnp.concatenate([v_t[j * HD : (j + 1) * HD], ones], 0), e)
            at = g + j * HD
            results_t[at : at + HD] = (o[:HD] / o[HD : HD + 1]).astype(BF16)

        later = project(0)
        for g in range(0, inner, 2 * LANES):
            q, k, v_t = later
            now = [scores(q, k, j) for j in range(4)]
            if g + 2 * LANES < inner:
                later = project(g + 2 * LANES)
            for j in range(4):
                mix(now[j], v_t, g, j)
        placed = dot_nt((diagonal * factor).astype(BF16), results_t[...]).reshape(WIN, WIN, inner)
        mid_sum[rows, :, 0:inner] += placed * in_mid
        side_sum[rows, :, 0:inner] += placed * (1.0 - in_mid)
        cover = jnp.broadcast_to(in_mid * factor, (WIN, WIN, LANES))
        mid_sum[rows, :, inner:wide] += cover
        side_sum[rows, :, inner:wide] += factor - cover
        return carry

    for copy in sum(weight_copies.values(), []):
        copy.wait()
    lax.fori_loop(0, live, one_window, 0)
    for out, rows in ((rim_1_out, rows_1), (rim_2_out, rows_2)):
        out[:, 0:WIN] = mid_sum[rows].astype(BF16)
        out[:, WIN : 2 * WIN] = side_sum[rows].astype(BF16)
    mid_out[...] = mid_sum[HALO:end].astype(BF16)

    def edges(rows):
        right, left = side_sum[rows, 0:HALO], side_sum[rows, HALO : 2 * HALO]
        return jnp.where(col_even, right, left).astype(BF16), jnp.where(col_even, left, right).astype(BF16)

    ends_1_out[0:HALO], ends_2_out[0:HALO] = edges(slice(HALO, 2 * HALO))
    ends_1_out[HALO : 2 * HALO], ends_2_out[HALO : 2 * HALO] = edges(slice(end - HALO, end))
    middle_1_out[...], middle_2_out[...] = edges(slice(2 * HALO, end - HALO))


def windows(
    even, mid, rows_1, rows_2, cols_1, cols_2, w_query, w_keyval, anchor, weight
):
    tile_rows, _, channels = mid.shape
    high = tile_rows + 2 * HALO
    inner = w_query.shape[1]
    wide = inner + LANES
    vmem = pl.BlockSpec(memory_space=pltpu.VMEM)
    smem = pl.BlockSpec(memory_space=pltpu.SMEM)
    free = pl.BlockSpec(memory_space=pl.ANY)
    rim = jax.ShapeDtypeStruct((HALO, 2 * WIN, wide), BF16)
    inside = jax.ShapeDtypeStruct((tile_rows, WIN, wide), BF16)
    ends = jax.ShapeDtypeStruct((2 * HALO, HALO, wide), BF16)
    middle = jax.ShapeDtypeStruct((tile_rows - 2 * HALO, HALO, wide), BF16)
    slots = weight.shape[0]
    cells = WIN * WIN
    return pl.pallas_call(
        windows_kernel,
        in_specs=[smem] * 3 + [free] * 3 + [vmem] * 2 + [free] * 2,
        out_specs=[vmem] * 7,
        out_shape=[rim, rim, inside, ends, ends, middle, middle],
        scratch_shapes=[
            pltpu.VMEM((high, 2 * WIN, channels), BF16),
            pltpu.VMEM(w_query.shape, BF16),
            pltpu.VMEM(w_keyval.shape, BF16),
            pltpu.VMEM((high, WIN, wide), F32),
            pltpu.VMEM((high, WIN, wide), F32),
            pltpu.VMEM((inner, cells), BF16),
            pltpu.SemaphoreType.DMA((3 + 3 * (inner // (2 * LANES)),)),
        ],
        compiler_params=params(61),
        cost_estimate=pl.CostEstimate(
            flops=8 * slots * 2 * cells * 3 * inner * (channels + 2 * cells),
            bytes_accessed=6 * channels * inner + 4 * high * WIN * channels,
            transcendentals=slots * cells * cells * inner // HD,
        ),
        name="windows",
    )(
        even, anchor, weight, mid, rows_1, rows_2, cols_1, cols_2,
        w_query, w_keyval,
    )


def settle_kernel(
    even, mid_ref, rim_1_ref, rim_2_ref, beside_ref, mask_ref, x_ref, known_ref, w_ref, base_ref, share_ref, own
):
    count, inner = own.shape
    tile_cols, tile_rows = mask_ref.shape
    cell = lax.broadcasted_iota(jnp.int32, (count, tile_rows), 0)
    row = lax.broadcasted_iota(jnp.int32, (count, tile_rows), 1)
    pick_row = jnp.where(cell // tile_cols == row, 1.0, 0.0).astype(BF16)
    in_row = dot_nt(pick_row, mask_ref[...].astype(F32).astype(BF16))
    cell = lax.broadcasted_iota(jnp.int32, (count, tile_cols), 0)
    col = lax.broadcasted_iota(jnp.int32, (count, tile_cols), 1)
    known_cell = jnp.sum(jnp.where(cell % tile_cols == col, in_row, 0.0), axis=1, keepdims=True) == 1

    def total(lanes):
        rims = [ref[:, 0:WIN, lanes].astype(F32) for ref in (rim_1_ref, rim_2_ref)]
        lower, upper = jnp.where(even[0] == 1, *rims), jnp.where(even[0] == 1, *rims[::-1])
        middle = mid_ref[:, :, lanes].astype(F32) + beside_ref[:, :, lanes].astype(F32)
        parts = [
            middle[:HALO] + upper,
            middle[HALO : tile_rows - HALO],
            middle[tile_rows - HALO :] + lower,
        ]
        return jnp.concatenate(parts, 0).reshape(count, LANES)

    share = 1.0 / (1.0 + total(slice(inner, inner + LANES)))
    share_ref[...] = jnp.where(known_cell, 0.0, share)
    for g in range(0, inner, LANES):
        lanes = slice(g, g + LANES)
        own[:, lanes] = (total(lanes) * share).astype(BF16)
    width = 2 * LANES
    for c in range(0, base_ref.shape[1], width):
        cols = slice(c, c + width)
        y = x_ref[:, cols].astype(F32) + dot(own[...], w_ref[:, cols])
        base_ref[:, cols] = jnp.where(known_cell, known_ref[:, cols].astype(F32), y)


def settle(even, mid, rim_1, rim_2, beside, mask, x, known, w_out):
    tile_rows, tile_cols, wide = mid.shape
    count, channels = x.shape
    vmem = pl.BlockSpec(memory_space=pltpu.VMEM)
    return pl.pallas_call(
        settle_kernel,
        in_specs=[pl.BlockSpec(memory_space=pltpu.SMEM)] + [vmem] * 8,
        out_specs=[vmem] * 2,
        out_shape=[
            jax.ShapeDtypeStruct((count, channels), F32),
            jax.ShapeDtypeStruct((count, LANES), F32),
        ],
        scratch_shapes=[pltpu.VMEM((count, wide - LANES), BF16)],
        compiler_params=params(),
        cost_estimate=pl.CostEstimate(
            flops=2**17 * count * wide, bytes_accessed=12 * count * wide, transcendentals=0
        ),
        name="settle",
    )(even, mid, rim_1, rim_2, beside, mask, x, known, w_out)


def blend_kernel(
    mixed_hbm, share_hbm, base_hbm, w_hbm, out_hbm, mixed_ref, share_ref, base_ref, w_ref, out_ref,
    blended, sems, out_sems,
):
    count, channels = base_ref.shape
    groups = mixed_ref.shape[1]
    width = 2 * LANES
    copies = [
        pltpu.make_async_copy(source, target, sems.at[i])
        for i, (source, target) in enumerate(
            ((mixed_hbm, mixed_ref), (share_hbm, share_ref), (w_hbm, w_ref), (base_hbm, base_ref))
        )
    ]
    for copy in copies:
        copy.start()
    back = lattice_order(count, False)
    for copy in copies[:2]:
        copy.wait()
    share = jnp.concatenate([share_ref[...]] * 2, 1)
    for g in range(0, groups, 2):
        lanes = slice(g * LANES, (g + 2) * LANES)
        mixed = jnp.concatenate([mixed_ref[:, g + j].reshape(count, LANES) for j in range(2)], 1)
        blended[:, lanes] = (dot(back, mixed) * share).astype(BF16)
    for copy in copies[2:]:
        copy.wait()
    outs = []
    for i, c in enumerate(range(0, channels, width)):
        cols = slice(c, c + width)
        out_ref[:, cols] = (base_ref[:, cols] + dot(blended[...], w_ref[:, cols])).astype(BF16)
        outs.append(
            pltpu.make_async_copy(out_ref.at[:, cols], out_hbm.at[:, cols], out_sems.at[i])
        )
        outs[-1].start()
    for copy in outs:
        copy.wait()


def blend(mixed, share, base, w_out):
    count, channels = base.shape
    inner = w_out.shape[0]
    arrays = (mixed, share, base, w_out)
    free = pl.BlockSpec(memory_space=pl.ANY)
    return pl.pallas_call(
        blend_kernel,
        in_specs=[free] * len(arrays),
        out_specs=free,
        out_shape=jax.ShapeDtypeStruct((count, channels), BF16),
        scratch_shapes=[pltpu.VMEM(a.shape, a.dtype) for a in arrays]
        + [
            pltpu.VMEM((count, channels), BF16),
            pltpu.VMEM((count, inner), BF16),
            pltpu.SemaphoreType.DMA((len(arrays),)),
            pltpu.SemaphoreType.DMA((channels // (2 * LANES),)),
        ],
        compiler_params=params(),
        cost_estimate=pl.CostEstimate(
            flops=2 * count * inner * (channels + count),
            bytes_accessed=2 * inner * channels + 6 * count * channels,
            transcendentals=0,
        ),
        name="blend",
    )(*arrays)


def exchange(pieces):
    return lax.all_to_all(pieces, ("row", "col"), split_axis=0, concat_axis=0, tiled=True)


def meet(axis, first, second):
    peers = lax.axis_size(axis)
    met = []
    for start, array in ((0, first), (1, second)):
        pairs = [(i, i + 1) for i in range(start, peers - 1, 2)]
        met.append(lax.ppermute(array, axis, pairs + [(j, i) for i, j in pairs]))
    return met


def on_device(features, known, known_mask, w_query, w_keyval, w_out, win_anchor, win_weight):
    tile_rows, tile_cols, channels = features.shape
    count = tile_rows * tile_cols
    per_sub = count // SUBS
    inner = w_query.shape[1]
    devices = lax.axis_size("row") * lax.axis_size("col")
    row_even, col_even = (lax.axis_index(axis) % 2 == 0 for axis in ("row", "col"))
    even = jnp.stack([row_even, col_even]).astype(jnp.int32)

    def swap(flag, lower, higher):
        return jnp.where(flag, higher, lower), jnp.where(flag, lower, higher)

    x = features.reshape(count, channels)

    cols = meet("col", *swap(col_even, features[:, :HALO], features[:, tile_cols - HALO :]))
    pieces = project(x, w_query, w_keyval).reshape(devices, per_sub, 3 * LANES)
    cols_1, cols_2, _ = lax.optimization_barrier((*cols, pieces))
    from_right, from_left = swap(col_even, cols_2, cols_1)

    def rows_of_halo(rows):
        return jnp.concatenate([features[rows], from_right[rows], from_left[rows]], 1)

    first_rows, last_rows = rows_of_halo(slice(0, HALO)), rows_of_halo(slice(tile_rows - HALO, None))
    rows_1, rows_2 = meet("row", *swap(row_even, first_rows, last_rows))

    gathered = exchange(pieces).reshape(devices * per_sub, 3 * LANES)

    rim_1, rim_2, inside, ends_1, ends_2, middle_1, middle_2 = windows(
        even,
        features,
        rows_1,
        rows_2,
        cols_1,
        cols_2,
        w_query,
        w_keyval,
        win_anchor.reshape(-1, 2).T,
        win_weight.reshape(-1),
    )
    rim_1, rim_2 = meet("row", rim_1, rim_2)
    middle_1, middle_2 = meet("col", middle_1, middle_2)
    half = lattice_attend(0, gathered)
    half, rim_1, rim_2, middle_1, middle_2 = lax.optimization_barrier(
        (half, rim_1, rim_2, middle_1, middle_2)
    )
    below, above = swap(row_even, rim_2, rim_1)

    def with_rims(ends, cols):
        rims = jnp.concatenate([above[:, cols], below[:, cols]], 0)
        return ends.astype(F32) + rims.astype(F32)

    right, left = slice(WIN, WIN + HALO), slice(WIN + HALO, 2 * WIN)
    ends_1 = jnp.where(col_even, with_rims(ends_1, right), with_rims(ends_1, left)).astype(BF16)
    ends_2 = jnp.where(col_even, with_rims(ends_2, left), with_rims(ends_2, right)).astype(BF16)
    gathered, half, ends_1, ends_2 = lax.optimization_barrier((gathered, half, ends_1, ends_2))
    ends_1, ends_2 = meet("col", ends_1, ends_2)
    mixed = lattice_attend(1, gathered, half)
    mixed, ends_1, ends_2 = lax.optimization_barrier((mixed, ends_1, ends_2))
    returned = exchange(mixed.reshape(devices, per_sub, LANES))
    ends = jnp.concatenate(swap(col_even, ends_1, ends_2), 1)
    middle = jnp.concatenate(swap(col_even, middle_1, middle_2), 1)
    arrived = jnp.concatenate([ends[:HALO], middle, ends[HALO:]], 0)
    base, share = settle(
        even, inside, rim_1, rim_2, arrived, known_mask.T, x, known.reshape(count, channels), w_out
    )
    returned = returned.reshape(SUBS, devices // SUBS, per_sub, LANES)
    out = blend(returned, share, base, w_out)
    return out.reshape(tile_rows, tile_cols, channels)


def solution(mesh):
    in_specs = (
        P("row", "col", None),
        P("row", "col", None),
        P("row", "col"),
        P(),
        P(),
        P(),
        P("row", "col", None, None),
        P("row", "col", None),
    )
    out_specs = P("row", "col", None)
    return jax.shard_map(
        on_device, mesh=mesh, in_specs=in_specs, out_specs=out_specs, check_vma=False
    )
```

```python
import functools
import math

import jax
import jax.numpy as jnp
from jax import lax
from jax.experimental import pallas as pl
from jax.experimental.pallas import tpu as pltpu
from jax.sharding import PartitionSpec as P

HD = 64
STRIDE = 4
WIN = 16
HALO = 8
SUBS = STRIDE * STRIDE
LANES = 128
SCALE = HD**-0.5 * math.log2(math.e)
FREE_RANGE = 100.0
VROWS = 80
QBLOCK = 2048
KBLOCK = 256
QPART = 256
AHEAD = 8
BF16 = jnp.bfloat16
F32 = jnp.float32


def dot(a, b):
    return jnp.dot(a, b, preferred_element_type=F32)


def dot_nt(a, b):
    return lax.dot_general(a, b, (((1,), (1,)), ((), ())), preferred_element_type=F32)


def whole(shape):
    return pl.BlockSpec(shape, lambda *_: (0,) * len(shape), pipeline_mode=pl.Buffered(1))


def params(mebibytes=63):
    return pltpu.CompilerParams(vmem_limit_bytes=mebibytes * 2**20)


def lattice_order(count, by_row):
    lattice = lax.broadcasted_iota(jnp.int32, (count, count), 0 if by_row else 1)
    cell = lax.broadcasted_iota(jnp.int32, (count, count), 1 if by_row else 0)
    per_sub = count // SUBS
    tile_cols = 16
    sub, place = lattice // per_sub, lattice % per_sub
    across = tile_cols // STRIDE
    row = (place // across) * STRIDE + sub // STRIDE
    col = (place % across) * STRIDE + sub % STRIDE
    return jnp.where(cell == row * tile_cols + col, 1.0, 0.0).astype(BF16)


def project_kernel(
    x_hbm, wq_hbm, wkv_hbm, out_hbm, x_ref, wq_ref, wkv_ref, ordered, queries, out_ref, sems,
    out_sems,
):
    count, channels = x_ref.shape
    inner = wq_ref.shape[1]
    width = 2 * LANES
    x_copy = pltpu.make_async_copy(x_hbm, x_ref, sems.at[0])
    x_copy.start()
    weight_copies = [
        pltpu.make_async_copy(source, target, sems.at[1 + i])
        for i, (source, target) in enumerate(((wq_hbm, wq_ref), (wkv_hbm, wkv_ref)))
    ]
    for copy in weight_copies:
        copy.start()
    order = lattice_order(count, True)
    x_copy.wait()
    ordered[...] = dot(order, x_ref[...]).astype(BF16)
    weight_copies[0].wait()
    for c in range(0, inner, width):
        queries[:, c : c + width] = dot(ordered[...], wq_ref[:, c : c + width])
    weight_copies[1].wait()
    leaving = []
    for i, c in enumerate(range(0, inner, width)):
        q = queries[:, c : c + width]
        k = dot(ordered[...], wkv_ref[:, c : c + width])
        v = dot(ordered[...], wkv_ref[:, inner + c : inner + c + width])
        for g in range(2):
            at = g * LANES
            parts = [
                jnp.concatenate([q[:, at : at + HD], k[:, at : at + HD]], 1),
                v[:, at : at + LANES],
                jnp.concatenate([q[:, at + HD : at + LANES], k[:, at + HD : at + LANES]], 1),
            ]
            for j, part in enumerate(parts):
                out_ref[:, 2 * i + g, :, j * LANES : (j + 1) * LANES] = part.astype(BF16).reshape(
                    SUBS, count // SUBS, LANES
                )
        groups = slice(2 * i, 2 * i + 2)
        leaving.append(
            pltpu.make_async_copy(out_ref.at[:, groups], out_hbm.at[:, groups], out_sems.at[i])
        )
        leaving[-1].start()
    for copy in leaving:
        copy.wait()


def project(x, w_query, w_keyval):
    count, channels = x.shape
    inner = w_query.shape[1]
    groups = inner // LANES
    shape = (SUBS, groups, count // SUBS, 3 * LANES)
    free = pl.BlockSpec(memory_space=pl.ANY)
    return pl.pallas_call(
        project_kernel,
        in_specs=[free] * 3,
        out_specs=free,
        out_shape=jax.ShapeDtypeStruct(shape, BF16),
        scratch_shapes=[
            pltpu.VMEM(x.shape, BF16),
            pltpu.VMEM(w_query.shape, BF16),
            pltpu.VMEM(w_keyval.shape, BF16),
            pltpu.VMEM(x.shape, BF16),
            pltpu.VMEM((count, inner), F32),
            pltpu.VMEM(shape, BF16),
            pltpu.SemaphoreType.DMA((3,)),
            pltpu.SemaphoreType.DMA((groups // 2,)),
        ],
        compiler_params=params(61),
        cost_estimate=pl.CostEstimate(
            flops=2 * count * channels * 3 * inner,
            bytes_accessed=2 * (3 * channels * inner + count * channels + 3 * count * inner),
            transcendentals=0,
        ),
        name="project",
    )(x, w_query, w_keyval)


def lattice_kernel(head, qk_ref, v_ref, *refs):
    if head == 0:
        o_ref, queries_t, values_t, free = refs
    else:
        other_ref, o_ref, queries_t, values_t, free = refs
    count = qk_ref.shape[0]
    block = o_ref.shape[1 - head]
    step = pl.program_id(0)

    @pl.when(step == 0)
    def _():
        row = lax.broadcasted_iota(jnp.int32, (LANES, LANES), 0)
        lane = lax.broadcasted_iota(jnp.int32, (LANES, LANES), 1)
        to_keys = jnp.where(row == lane + HD, 1.0, 0.0).astype(BF16)
        queries_t[...] = dot_nt(to_keys, qk_ref[...]).astype(BF16)
        own = (row[:HD] + head * HD == lane[:HD]).astype(F32).astype(BF16)
        values_t[0:HD] = dot_nt(own, v_ref[...]).astype(BF16)
        squares = qk_ref[...].astype(F32)
        squares = (squares * squares).astype(BF16)
        halves = ((row[:VROWS - HD] < 8) == (lane[:VROWS - HD] < HD)).astype(F32).astype(BF16)
        norms = dot_nt(halves, squares)
        bound = jnp.max(norms[:8]) * jnp.max(norms[8:]) * 1.02
        free[0] = (bound * (SCALE * SCALE) <= FREE_RANGE * FREE_RANGE).astype(jnp.int32)
        values_t[HD:VROWS] = jnp.ones((VROWS - HD, count), BF16)

    cols = pl.ds(pl.multiple_of(step * block, block), block)

    def finish(total):
        out = total[:HD] / total[HD : HD + 1]
        if head == 0:
            o_ref[...] = out.astype(BF16)
        else:
            o_ref[...] = jnp.concatenate([other_ref[...].astype(F32), out], 0).T.astype(BF16)

    @pl.when(free[0] == 1)
    def _():
        parts = block // QPART
        items = [(c, j) for c in range(0, count, KBLOCK) for j in range(parts)]
        queries = [
            queries_t[:, pl.ds(pl.multiple_of(step * block + j * QPART, QPART), QPART)]
            for j in range(parts)
        ]

        def score(i):
            c, j = items[i]
            return dot(qk_ref[c : c + KBLOCK, :], queries[j])

        totals, sums = [None] * parts, [None] * parts
        ahead = [score(i) for i in range(AHEAD)]
        for i, (c, j) in enumerate(items):
            now = ahead.pop(0)
            if i + AHEAD < len(items):
                ahead.append(score(i + AHEAD))
            weights = jnp.exp2(now * SCALE)
            part = dot(values_t[0:HD, c : c + KBLOCK], weights.astype(BF16))
            total = jnp.sum(weights.reshape(KBLOCK // 8, 8, QPART), axis=0)
            totals[j] = part if totals[j] is None else totals[j] + part
            sums[j] = total if sums[j] is None else sums[j] + total
        sums = jnp.sum(jnp.concatenate(sums, 1), axis=0, keepdims=True)
        finish(jnp.concatenate([jnp.concatenate(totals, 1), jnp.broadcast_to(sums, (VROWS - HD, block))], 0))

    @pl.when(free[0] == 0)
    def _():
        chunks = count // KBLOCK
        q = queries_t[:, cols]

        def score(c):
            return dot(qk_ref[pl.ds(pl.multiple_of(c * KBLOCK, KBLOCK), KBLOCK), :], q)

        def top(c, m):
            return jnp.maximum(m, jnp.max(score(c), axis=0, keepdims=True))

        m = lax.fori_loop(0, chunks, top, jnp.full((1, block), -jnp.inf, F32))

        def add(c, total):
            weights = jnp.exp2((score(c) - m) * SCALE).astype(BF16)
            rows = pl.ds(pl.multiple_of(c * KBLOCK, KBLOCK), KBLOCK)
            return total + dot(values_t[:, rows], weights)

        finish(lax.fori_loop(0, chunks, add, jnp.zeros((VROWS, block), F32)))


def lattice_attend(head, x, other=None):
    count = x.shape[0]
    in_specs = [
        pl.BlockSpec((count, LANES), lambda i: (0, 2 * head), pipeline_mode=pl.Buffered(1)),
        pl.BlockSpec((count, LANES), lambda i: (0, 1), pipeline_mode=pl.Buffered(1)),
    ]
    args = [x, x]
    if head == 0:
        out_spec = pl.BlockSpec((HD, QBLOCK), lambda i: (0, i))
        out_shape = (HD, count)
    else:
        in_specs.append(pl.BlockSpec((HD, QBLOCK), lambda i: (0, i)))
        args.append(other)
        out_spec = pl.BlockSpec((QBLOCK, LANES), lambda i: (i, 0))
        out_shape = (count, LANES)
    return pl.pallas_call(
        functools.partial(lattice_kernel, head),
        grid=(count // QBLOCK,),
        in_specs=in_specs,
        out_specs=out_spec,
        out_shape=jax.ShapeDtypeStruct(out_shape, BF16),
        scratch_shapes=[
            pltpu.VMEM((LANES, count), BF16),
            pltpu.VMEM((VROWS, count), BF16),
            pltpu.SMEM((1,), jnp.int32),
        ],
        compiler_params=params(61),
        cost_estimate=pl.CostEstimate(
            flops=4 * 4 * count * count * HD,
            bytes_accessed=6 * count * LANES,
            transcendentals=count * count,
        ),
        name="lattice_attend_" + str(head),
    )(*args)


def windows_kernel(
    even, anchor, weight, mid_hbm, rows_1_hbm, rows_2_hbm, cols_1_ref, cols_2_ref,
    wq_hbm, wkv_hbm, rim_1_out, rim_2_out, mid_out, ends_1_out, ends_2_out,
    middle_1_out, middle_2_out, held, wq_ref, wkv_ref, mid_sum, side_sum, results_t, sems,
):
    channels, inner = wq_ref.shape
    cells = WIN * WIN
    wide = inner + LANES
    tile_rows = mid_hbm.shape[0]
    end = tile_rows + HALO
    pair_lanes = 2 * LANES
    row_even, col_even = even[0] == 1, even[1] == 1
    rows_1 = pl.ds(jnp.where(row_even, end, 0), HALO)
    rows_2 = pl.ds(jnp.where(row_even, 0, end), HALO)
    copies = [
        pltpu.make_async_copy(source, target, sems.at[i])
        for i, (source, target) in enumerate(
            (
                (mid_hbm, held.at[HALO:end, 0:WIN]),
                (rows_1_hbm, held.at[rows_1]),
                (rows_2_hbm, held.at[rows_2]),
            )
        )
    ]
    weight_copies = {}
    for g in range(0, inner, pair_lanes):
        for part, (source, target, at) in enumerate(
            ((wq_hbm, wq_ref, g), (wkv_hbm, wkv_ref, g), (wkv_hbm, wkv_ref, inner + g))
        ):
            cols = slice(at, at + pair_lanes)
            sem = sems.at[len(copies) + 3 * (g // pair_lanes) + part]
            weight_copies.setdefault(g, []).append(
                pltpu.make_async_copy(source.at[:, cols], target.at[:, cols], sem)
            )
    for copy in copies + sum(weight_copies.values(), []):
        copy.start()
    mid_sum[...] = jnp.zeros(mid_sum.shape, F32)
    side_sum[...] = jnp.zeros(side_sum.shape, F32)
    for row in range(0, tile_rows, HALO):
        rows = slice(row, row + HALO)
        pair = (cols_1_ref[rows].astype(F32), cols_2_ref[rows].astype(F32))
        pair = (jnp.where(col_even, *pair), jnp.where(col_even, *pair[::-1]))
        held[HALO + row : 2 * HALO + row, WIN : 2 * WIN] = jnp.concatenate(pair, 1).astype(BF16)
    for copy in copies:
        copy.wait()
    slots = weight.shape[0]
    live = sum((weight[s] > 0).astype(jnp.int32) for s in range(slots))
    first = lax.broadcasted_iota(jnp.int32, (cells, LANES), 1) < HD
    ones = jnp.ones((VROWS - HD, cells), BF16)

    column = lax.broadcasted_iota(jnp.int32, (1, WIN, 1), 1)
    across = lax.broadcasted_iota(jnp.int32, (cells, cells), 0)
    along = lax.broadcasted_iota(jnp.int32, (cells, cells), 1)
    diagonal = jnp.where(across == along, 1.0, 0.0)

    def one_window(slot, carry):
        top = anchor[0, slot] + HALO
        left = anchor[1, slot]
        factor = weight[slot].astype(F32)
        rows = pl.ds(top, WIN)
        in_mid = ((column >= left) & (column < left + WIN)).astype(F32)
        own = in_mid.astype(BF16)
        x = held[rows, 0:WIN] * own + held[rows, WIN : 2 * WIN] * (1 - own)
        x = x.reshape(cells, channels)

        def project(g):
            q = dot(x, wq_ref[:, g : g + 2 * LANES]).astype(BF16)
            k = dot(x, wkv_ref[:, g : g + 2 * LANES]).astype(BF16)
            v = dot(x, wkv_ref[:, inner + g : inner + g + 2 * LANES])
            return q, k, v.T.astype(BF16)

        def scores(q, k, j):
            lanes = slice(j // 2 * LANES, (j // 2 + 1) * LANES)
            own = jnp.where(first if j % 2 == 0 else ~first, q[:, lanes], jnp.zeros((), BF16))
            return dot_nt(k[:, lanes], own)

        def mix(s, v_t, g, j):
            e = jnp.exp2((s - jnp.max(s, axis=0, keepdims=True)) * SCALE).astype(BF16)
            o = dot(jnp.concatenate([v_t[j * HD : (j + 1) * HD], ones], 0), e)
            at = g + j * HD
            results_t[at : at + HD] = (o[:HD] / o[HD : HD + 1]).astype(BF16)

        later = project(0)
        for g in range(0, inner, 2 * LANES):
            q, k, v_t = later
            now = [scores(q, k, j) for j in range(4)]
            if g + 2 * LANES < inner:
                later = project(g + 2 * LANES)
            for j in range(4):
                mix(now[j], v_t, g, j)
        placed = dot_nt((diagonal * factor).astype(BF16), results_t[...]).reshape(WIN, WIN, inner)
        mid_sum[rows, :, 0:inner] += placed * in_mid
        side_sum[rows, :, 0:inner] += placed * (1.0 - in_mid)
        cover = jnp.broadcast_to(in_mid * factor, (WIN, WIN, LANES))
        mid_sum[rows, :, inner:wide] += cover
        side_sum[rows, :, inner:wide] += factor - cover
        return carry

    for copy in sum(weight_copies.values(), []):
        copy.wait()
    lax.fori_loop(0, live, one_window, 0)
    for out, rows in ((rim_1_out, rows_1), (rim_2_out, rows_2)):
        out[:, 0:WIN] = mid_sum[rows].astype(BF16)
        out[:, WIN : 2 * WIN] = side_sum[rows].astype(BF16)
    mid_out[...] = mid_sum[HALO:end].astype(BF16)

    def edges(rows):
        right, left = side_sum[rows, 0:HALO], side_sum[rows, HALO : 2 * HALO]
        return jnp.where(col_even, right, left).astype(BF16), jnp.where(col_even, left, right).astype(BF16)

    ends_1_out[0:HALO], ends_2_out[0:HALO] = edges(slice(HALO, 2 * HALO))
    ends_1_out[HALO : 2 * HALO], ends_2_out[HALO : 2 * HALO] = edges(slice(end - HALO, end))
    middle_1_out[...], middle_2_out[...] = edges(slice(2 * HALO, end - HALO))


def windows(
    even, mid, rows_1, rows_2, cols_1, cols_2, w_query, w_keyval, anchor, weight
):
    tile_rows, _, channels = mid.shape
    high = tile_rows + 2 * HALO
    inner = w_query.shape[1]
    wide = inner + LANES
    vmem = pl.BlockSpec(memory_space=pltpu.VMEM)
    smem = pl.BlockSpec(memory_space=pltpu.SMEM)
    free = pl.BlockSpec(memory_space=pl.ANY)
    rim = jax.ShapeDtypeStruct((HALO, 2 * WIN, wide), BF16)
    inside = jax.ShapeDtypeStruct((tile_rows, WIN, wide), BF16)
    ends = jax.ShapeDtypeStruct((2 * HALO, HALO, wide), BF16)
    middle = jax.ShapeDtypeStruct((tile_rows - 2 * HALO, HALO, wide), BF16)
    slots = weight.shape[0]
    cells = WIN * WIN
    return pl.pallas_call(
        windows_kernel,
        in_specs=[smem] * 3 + [free] * 3 + [vmem] * 2 + [free] * 2,
        out_specs=[vmem] * 7,
        out_shape=[rim, rim, inside, ends, ends, middle, middle],
        scratch_shapes=[
            pltpu.VMEM((high, 2 * WIN, channels), BF16),
            pltpu.VMEM(w_query.shape, BF16),
            pltpu.VMEM(w_keyval.shape, BF16),
            pltpu.VMEM((high, WIN, wide), F32),
            pltpu.VMEM((high, WIN, wide), F32),
            pltpu.VMEM((inner, cells), BF16),
            pltpu.SemaphoreType.DMA((3 + 3 * (inner // (2 * LANES)),)),
        ],
        compiler_params=params(61),
        cost_estimate=pl.CostEstimate(
            flops=8 * slots * 2 * cells * 3 * inner * (channels + 2 * cells),
            bytes_accessed=6 * channels * inner + 4 * high * WIN * channels,
            transcendentals=slots * cells * cells * inner // HD,
        ),
        name="windows",
    )(
        even, anchor, weight, mid, rows_1, rows_2, cols_1, cols_2,
        w_query, w_keyval,
    )


def settle_kernel(
    even, mid_ref, rim_1_ref, rim_2_ref, beside_ref, mask_ref, x_ref, known_ref, w_ref, base_ref, share_ref, own
):
    count, inner = own.shape
    tile_cols, tile_rows = mask_ref.shape
    cell = lax.broadcasted_iota(jnp.int32, (count, tile_rows), 0)
    row = lax.broadcasted_iota(jnp.int32, (count, tile_rows), 1)
    pick_row = jnp.where(cell // tile_cols == row, 1.0, 0.0).astype(BF16)
    in_row = dot_nt(pick_row, mask_ref[...].astype(F32).astype(BF16))
    cell = lax.broadcasted_iota(jnp.int32, (count, tile_cols), 0)
    col = lax.broadcasted_iota(jnp.int32, (count, tile_cols), 1)
    known_cell = jnp.sum(jnp.where(cell % tile_cols == col, in_row, 0.0), axis=1, keepdims=True) == 1

    def total(lanes):
        rims = [ref[:, 0:WIN, lanes].astype(F32) for ref in (rim_1_ref, rim_2_ref)]
        lower, upper = jnp.where(even[0] == 1, *rims), jnp.where(even[0] == 1, *rims[::-1])
        middle = mid_ref[:, :, lanes].astype(F32) + beside_ref[:, :, lanes].astype(F32)
        parts = [
            middle[:HALO] + upper,
            middle[HALO : tile_rows - HALO],
            middle[tile_rows - HALO :] + lower,
        ]
        return jnp.concatenate(parts, 0).reshape(count, LANES)

    share = 1.0 / (1.0 + total(slice(inner, inner + LANES)))
    share_ref[...] = jnp.where(known_cell, 0.0, share)
    for g in range(0, inner, LANES):
        lanes = slice(g, g + LANES)
        own[:, lanes] = (total(lanes) * share).astype(BF16)
    width = 2 * LANES
    for c in range(0, base_ref.shape[1], width):
        cols = slice(c, c + width)
        y = x_ref[:, cols].astype(F32) + dot(own[...], w_ref[:, cols])
        base_ref[:, cols] = jnp.where(known_cell, known_ref[:, cols].astype(F32), y)


def settle(even, mid, rim_1, rim_2, beside, mask, x, known, w_out):
    tile_rows, tile_cols, wide = mid.shape
    count, channels = x.shape
    vmem = pl.BlockSpec(memory_space=pltpu.VMEM)
    return pl.pallas_call(
        settle_kernel,
        in_specs=[pl.BlockSpec(memory_space=pltpu.SMEM)] + [vmem] * 8,
        out_specs=[vmem] * 2,
        out_shape=[
            jax.ShapeDtypeStruct((count, channels), F32),
            jax.ShapeDtypeStruct((count, LANES), F32),
        ],
        scratch_shapes=[pltpu.VMEM((count, wide - LANES), BF16)],
        compiler_params=params(),
        cost_estimate=pl.CostEstimate(
            flops=2**17 * count * wide, bytes_accessed=12 * count * wide, transcendentals=0
        ),
        name="settle",
    )(even, mid, rim_1, rim_2, beside, mask, x, known, w_out)


def blend_kernel(
    mixed_hbm, share_hbm, base_hbm, w_hbm, out_hbm, mixed_ref, share_ref, base_ref, w_ref, out_ref,
    blended, sems, out_sems,
):
    count, channels = base_ref.shape
    groups = mixed_ref.shape[1]
    width = 2 * LANES
    copies = [
        pltpu.make_async_copy(source, target, sems.at[i])
        for i, (source, target) in enumerate(
            ((mixed_hbm, mixed_ref), (share_hbm, share_ref), (w_hbm, w_ref), (base_hbm, base_ref))
        )
    ]
    for copy in copies:
        copy.start()
    back = lattice_order(count, False)
    for copy in copies[:2]:
        copy.wait()
    share = jnp.concatenate([share_ref[...]] * 2, 1)
    for g in range(0, groups, 2):
        lanes = slice(g * LANES, (g + 2) * LANES)
        mixed = jnp.concatenate([mixed_ref[:, g + j].reshape(count, LANES) for j in range(2)], 1)
        blended[:, lanes] = (dot(back, mixed) * share).astype(BF16)
    for copy in copies[2:]:
        copy.wait()
    outs = []
    for i, c in enumerate(range(0, channels, width)):
        cols = slice(c, c + width)
        out_ref[:, cols] = (base_ref[:, cols] + dot(blended[...], w_ref[:, cols])).astype(BF16)
        outs.append(
            pltpu.make_async_copy(out_ref.at[:, cols], out_hbm.at[:, cols], out_sems.at[i])
        )
        outs[-1].start()
    for copy in outs:
        copy.wait()


def blend(mixed, share, base, w_out):
    count, channels = base.shape
    inner = w_out.shape[0]
    arrays = (mixed, share, base, w_out)
    free = pl.BlockSpec(memory_space=pl.ANY)
    return pl.pallas_call(
        blend_kernel,
        in_specs=[free] * len(arrays),
        out_specs=free,
        out_shape=jax.ShapeDtypeStruct((count, channels), BF16),
        scratch_shapes=[pltpu.VMEM(a.shape, a.dtype) for a in arrays]
        + [
            pltpu.VMEM((count, channels), BF16),
            pltpu.VMEM((count, inner), BF16),
            pltpu.SemaphoreType.DMA((len(arrays),)),
            pltpu.SemaphoreType.DMA((channels // (2 * LANES),)),
        ],
        compiler_params=params(),
        cost_estimate=pl.CostEstimate(
            flops=2 * count * inner * (channels + count),
            bytes_accessed=2 * inner * channels + 6 * count * channels,
            transcendentals=0,
        ),
        name="blend",
    )(*arrays)


def exchange(pieces):
    return lax.all_to_all(pieces, ("row", "col"), split_axis=0, concat_axis=0, tiled=True)


def meet(axis, first, second):
    peers = lax.axis_size(axis)
    met = []
    for start, array in ((0, first), (1, second)):
        pairs = [(i, i + 1) for i in range(start, peers - 1, 2)]
        met.append(lax.ppermute(array, axis, pairs + [(j, i) for i, j in pairs]))
    return met


def on_device(features, known, known_mask, w_query, w_keyval, w_out, win_anchor, win_weight):
    tile_rows, tile_cols, channels = features.shape
    count = tile_rows * tile_cols
    per_sub = count // SUBS
    inner = w_query.shape[1]
    devices = lax.axis_size("row") * lax.axis_size("col")
    row_even, col_even = (lax.axis_index(axis) % 2 == 0 for axis in ("row", "col"))
    even = jnp.stack([row_even, col_even]).astype(jnp.int32)

    def swap(flag, lower, higher):
        return jnp.where(flag, higher, lower), jnp.where(flag, lower, higher)

    x = features.reshape(count, channels)

    high = tile_cols - HALO
    cols = meet(
        "col",
        *(
            lax.dynamic_slice_in_dim(features, jnp.where(flag, high, 0), HALO, axis=1)
            for flag in (col_even, ~col_even)
        ),
    )
    pieces = project(x, w_query, w_keyval).reshape(devices, per_sub, 3 * LANES)
    cols_1, cols_2, even, _ = lax.optimization_barrier((*cols, even, pieces))
    from_right, from_left = swap(col_even, cols_2, cols_1)

    def rows_of_halo(rows):
        return jnp.concatenate([features[rows], from_right[rows], from_left[rows]], 1)

    first_rows, last_rows = rows_of_halo(slice(0, HALO)), rows_of_halo(slice(tile_rows - HALO, None))
    rows_1, rows_2 = meet("row", *swap(row_even, first_rows, last_rows))

    gathered = exchange(pieces).reshape(devices * per_sub, 3 * LANES)

    rim_1, rim_2, inside, ends_1, ends_2, middle_1, middle_2 = windows(
        even,
        features,
        rows_1,
        rows_2,
        cols_1,
        cols_2,
        w_query,
        w_keyval,
        win_anchor.reshape(-1, 2).T,
        win_weight.reshape(-1),
    )
    rim_1, rim_2 = meet("row", rim_1, rim_2)
    middle_1, middle_2 = meet("col", middle_1, middle_2)
    half = lattice_attend(0, gathered)
    half, rim_1, rim_2, middle_1, middle_2 = lax.optimization_barrier(
        (half, rim_1, rim_2, middle_1, middle_2)
    )
    below, above = swap(row_even, rim_2, rim_1)

    def with_rims(ends, cols):
        rims = jnp.concatenate([above[:, cols], below[:, cols]], 0)
        return ends.astype(F32) + rims.astype(F32)

    right, left = slice(WIN, WIN + HALO), slice(WIN + HALO, 2 * WIN)
    ends_1 = jnp.where(col_even, with_rims(ends_1, right), with_rims(ends_1, left)).astype(BF16)
    ends_2 = jnp.where(col_even, with_rims(ends_2, left), with_rims(ends_2, right)).astype(BF16)
    gathered, half, ends_1, ends_2 = lax.optimization_barrier((gathered, half, ends_1, ends_2))
    ends_1, ends_2 = meet("col", ends_1, ends_2)
    mixed = lattice_attend(1, gathered, half)
    mixed, ends_1, ends_2 = lax.optimization_barrier((mixed, ends_1, ends_2))
    returned = exchange(mixed.reshape(devices, per_sub, LANES))
    ends = jnp.concatenate(swap(col_even, ends_1, ends_2), 1)
    middle = jnp.concatenate(swap(col_even, middle_1, middle_2), 1)
    arrived = jnp.concatenate([ends[:HALO], middle, ends[HALO:]], 0)
    base, share = settle(
        even, inside, rim_1, rim_2, arrived, known_mask.T, x, known.reshape(count, channels), w_out
    )
    returned = returned.reshape(SUBS, devices // SUBS, per_sub, LANES)
    out = blend(returned, share, base, w_out)
    return out.reshape(tile_rows, tile_cols, channels)


def solution(mesh):
    in_specs = (
        P("row", "col", None),
        P("row", "col", None),
        P("row", "col"),
        P(),
        P(),
        P(),
        P("row", "col", None, None),
        P("row", "col", None),
    )
    out_specs = P("row", "col", None)
    return jax.shard_map(
        on_device, mesh=mesh, in_specs=in_specs, out_specs=out_specs, check_vma=False
    )
```

```python
import functools
import math

import jax
import jax.numpy as jnp
from jax import lax
from jax.experimental import pallas as pl
from jax.experimental.pallas import tpu as pltpu
from jax.sharding import PartitionSpec as P

HD = 64
STRIDE = 4
WIN = 16
HALO = 8
SUBS = STRIDE * STRIDE
LANES = 128
SCALE = HD**-0.5 * math.log2(math.e)
FREE_RANGE = 100.0
VROWS = 80
QBLOCK = 2048
KBLOCK = 256
QPART = 256
AHEAD = 8
BF16 = jnp.bfloat16
F32 = jnp.float32


def dot(a, b):
    return jnp.dot(a, b, preferred_element_type=F32)


def dot_nt(a, b):
    return lax.dot_general(a, b, (((1,), (1,)), ((), ())), preferred_element_type=F32)


def whole(shape):
    return pl.BlockSpec(shape, lambda *_: (0,) * len(shape), pipeline_mode=pl.Buffered(1))


def params(mebibytes=63):
    return pltpu.CompilerParams(vmem_limit_bytes=mebibytes * 2**20)


def lattice_order(count, by_row):
    lattice = lax.broadcasted_iota(jnp.int32, (count, count), 0 if by_row else 1)
    cell = lax.broadcasted_iota(jnp.int32, (count, count), 1 if by_row else 0)
    per_sub, tile_cols = count // SUBS, 16
    across = tile_cols // STRIDE

    def split(index, size):
        return index >> (size.bit_length() - 1), index & (size - 1)

    sub, place = split(lattice, per_sub)
    sub_row, sub_col = split(sub, STRIDE)
    place_row, place_col = split(place, across)
    row = place_row * STRIDE + sub_row
    col = place_col * STRIDE + sub_col
    return jnp.where(cell == row * tile_cols + col, 1.0, 0.0).astype(BF16)


def project_kernel(
    x_hbm, wq_hbm, wkv_hbm, out_hbm, x_ref, wq_ref, wkv_ref, ordered, queries, out_ref, sems,
    out_sems,
):
    count, channels = x_ref.shape
    inner = wq_ref.shape[1]
    width = 2 * LANES
    x_copy = pltpu.make_async_copy(x_hbm, x_ref, sems.at[0])
    x_copy.start()
    weight_copies = [
        pltpu.make_async_copy(source, target, sems.at[1 + i])
        for i, (source, target) in enumerate(((wq_hbm, wq_ref), (wkv_hbm, wkv_ref)))
    ]
    for copy in weight_copies:
        copy.start()
    order = lattice_order(count, True)
    x_copy.wait()
    ordered[...] = dot(order, x_ref[...]).astype(BF16)
    weight_copies[0].wait()
    for c in range(0, inner, width):
        queries[:, c : c + width] = dot(ordered[...], wq_ref[:, c : c + width])
    weight_copies[1].wait()
    leaving = []
    for i, c in enumerate(range(0, inner, width)):
        q = queries[:, c : c + width]
        k = dot(ordered[...], wkv_ref[:, c : c + width])
        v = dot(ordered[...], wkv_ref[:, inner + c : inner + c + width])
        for g in range(2):
            at = g * LANES
            parts = [
                jnp.concatenate([q[:, at : at + HD], k[:, at : at + HD]], 1),
                v[:, at : at + LANES],
                jnp.concatenate([q[:, at + HD : at + LANES], k[:, at + HD : at + LANES]], 1),
            ]
            for j, part in enumerate(parts):
                out_ref[:, 2 * i + g, :, j * LANES : (j + 1) * LANES] = part.astype(BF16).reshape(
                    SUBS, count // SUBS, LANES
                )
        groups = slice(2 * i, 2 * i + 2)
        leaving.append(
            pltpu.make_async_copy(out_ref.at[:, groups], out_hbm.at[:, groups], out_sems.at[i])
        )
        leaving[-1].start()
    for copy in leaving:
        copy.wait()


def project(x, w_query, w_keyval):
    count, channels = x.shape
    inner = w_query.shape[1]
    groups = inner // LANES
    shape = (SUBS, groups, count // SUBS, 3 * LANES)
    free = pl.BlockSpec(memory_space=pl.ANY)
    return pl.pallas_call(
        project_kernel,
        in_specs=[free] * 3,
        out_specs=free,
        out_shape=jax.ShapeDtypeStruct(shape, BF16),
        scratch_shapes=[
            pltpu.VMEM(x.shape, BF16),
            pltpu.VMEM(w_query.shape, BF16),
            pltpu.VMEM(w_keyval.shape, BF16),
            pltpu.VMEM(x.shape, BF16),
            pltpu.VMEM((count, inner), F32),
            pltpu.VMEM(shape, BF16),
            pltpu.SemaphoreType.DMA((3,)),
            pltpu.SemaphoreType.DMA((groups // 2,)),
        ],
        compiler_params=params(61),
        cost_estimate=pl.CostEstimate(
            flops=2 * count * channels * 3 * inner,
            bytes_accessed=2 * (3 * channels * inner + count * channels + 3 * count * inner),
            transcendentals=0,
        ),
        name="project",
    )(x, w_query, w_keyval)


def lattice_kernel(head, qk_ref, v_ref, *refs):
    if head == 0:
        o_ref, queries_t, values_t, free = refs
    else:
        other_ref, o_ref, queries_t, values_t, free = refs
    count = qk_ref.shape[0]
    block = o_ref.shape[1 - head]
    step = pl.program_id(0)

    @pl.when(step == 0)
    def _():
        row = lax.broadcasted_iota(jnp.int32, (LANES, LANES), 0)
        lane = lax.broadcasted_iota(jnp.int32, (LANES, LANES), 1)
        to_keys = jnp.where(row == lane + HD, 1.0, 0.0).astype(BF16)
        queries_t[...] = dot_nt(to_keys, qk_ref[...]).astype(BF16)
        own = (row[:HD] + head * HD == lane[:HD]).astype(F32).astype(BF16)
        values_t[0:HD] = dot_nt(own, v_ref[...]).astype(BF16)
        squares = qk_ref[...].astype(F32)
        squares = (squares * squares).astype(BF16)
        halves = ((row[:VROWS - HD] < 8) == (lane[:VROWS - HD] < HD)).astype(F32).astype(BF16)
        norms = dot_nt(halves, squares)
        bound = jnp.max(norms[:8]) * jnp.max(norms[8:]) * 1.02
        free[0] = (bound * (SCALE * SCALE) <= FREE_RANGE * FREE_RANGE).astype(jnp.int32)
        values_t[HD:VROWS] = jnp.ones((VROWS - HD, count), BF16)

    cols = pl.ds(pl.multiple_of(step * block, block), block)

    def finish(total):
        out = total[:HD] / total[HD : HD + 1]
        if head == 0:
            o_ref[...] = out.astype(BF16)
        else:
            o_ref[...] = jnp.concatenate([other_ref[...].astype(F32), out], 0).T.astype(BF16)

    @pl.when(free[0] == 1)
    def _():
        parts = block // QPART
        items = [(c, j) for c in range(0, count, KBLOCK) for j in range(parts)]
        queries = [
            queries_t[:, pl.ds(pl.multiple_of(step * block + j * QPART, QPART), QPART)]
            for j in range(parts)
        ]

        def score(i):
            c, j = items[i]
            return dot(qk_ref[c : c + KBLOCK, :], queries[j])

        totals, sums = [None] * parts, [None] * parts
        ahead = [score(i) for i in range(AHEAD)]
        for i, (c, j) in enumerate(items):
            now = ahead.pop(0)
            if i + AHEAD < len(items):
                ahead.append(score(i + AHEAD))
            weights = jnp.exp2(now * SCALE)
            part = dot(values_t[0:HD, c : c + KBLOCK], weights.astype(BF16))
            total = jnp.sum(weights.reshape(KBLOCK // 8, 8, QPART), axis=0)
            totals[j] = part if totals[j] is None else totals[j] + part
            sums[j] = total if sums[j] is None else sums[j] + total
        sums = jnp.sum(jnp.concatenate(sums, 1), axis=0, keepdims=True)
        finish(jnp.concatenate([jnp.concatenate(totals, 1), jnp.broadcast_to(sums, (VROWS - HD, block))], 0))

    @pl.when(free[0] == 0)
    def _():
        chunks = count // KBLOCK
        q = queries_t[:, cols]

        def score(c):
            return dot(qk_ref[pl.ds(pl.multiple_of(c * KBLOCK, KBLOCK), KBLOCK), :], q)

        def top(c, m):
            return jnp.maximum(m, jnp.max(score(c), axis=0, keepdims=True))

        m = lax.fori_loop(0, chunks, top, jnp.full((1, block), -jnp.inf, F32))

        def add(c, total):
            weights = jnp.exp2((score(c) - m) * SCALE).astype(BF16)
            rows = pl.ds(pl.multiple_of(c * KBLOCK, KBLOCK), KBLOCK)
            return total + dot(values_t[:, rows], weights)

        finish(lax.fori_loop(0, chunks, add, jnp.zeros((VROWS, block), F32)))


def lattice_attend(head, x, other=None):
    count = x.shape[0]
    in_specs = [
        pl.BlockSpec((count, LANES), lambda i: (0, 2 * head), pipeline_mode=pl.Buffered(1)),
        pl.BlockSpec((count, LANES), lambda i: (0, 1), pipeline_mode=pl.Buffered(1)),
    ]
    args = [x, x]
    if head == 0:
        out_spec = pl.BlockSpec((HD, QBLOCK), lambda i: (0, i))
        out_shape = (HD, count)
    else:
        in_specs.append(pl.BlockSpec((HD, QBLOCK), lambda i: (0, i)))
        args.append(other)
        out_spec = pl.BlockSpec((QBLOCK, LANES), lambda i: (i, 0))
        out_shape = (count, LANES)
    return pl.pallas_call(
        functools.partial(lattice_kernel, head),
        grid=(count // QBLOCK,),
        in_specs=in_specs,
        out_specs=out_spec,
        out_shape=jax.ShapeDtypeStruct(out_shape, BF16),
        scratch_shapes=[
            pltpu.VMEM((LANES, count), BF16),
            pltpu.VMEM((VROWS, count), BF16),
            pltpu.SMEM((1,), jnp.int32),
        ],
        compiler_params=params(61),
        cost_estimate=pl.CostEstimate(
            flops=4 * 4 * count * count * HD,
            bytes_accessed=6 * count * LANES,
            transcendentals=count * count,
        ),
        name="lattice_attend_" + str(head),
    )(*args)


def windows_kernel(
    even, anchor, weight, mid_hbm, rows_1_hbm, rows_2_hbm, cols_1_ref, cols_2_ref,
    wq_hbm, wkv_hbm, rim_1_out, rim_2_out, mid_out, ends_1_out, ends_2_out,
    middle_1_out, middle_2_out, held, wq_ref, wkv_ref, mid_sum, side_sum, results_t, sems,
):
    channels, inner = wq_ref.shape
    cells = WIN * WIN
    wide = inner + LANES
    tile_rows = mid_hbm.shape[0]
    end = tile_rows + HALO
    pair_lanes = 2 * LANES
    row_even, col_even = even[0] == 1, even[1] == 1
    rows_1 = pl.ds(jnp.where(row_even, end, 0), HALO)
    rows_2 = pl.ds(jnp.where(row_even, 0, end), HALO)
    copies = [
        pltpu.make_async_copy(source, target, sems.at[i])
        for i, (source, target) in enumerate(
            (
                (mid_hbm, held.at[HALO:end, 0:WIN]),
                (rows_1_hbm, held.at[rows_1]),
                (rows_2_hbm, held.at[rows_2]),
            )
        )
    ]
    weight_copies = {}
    for g in range(0, inner, pair_lanes):
        for part, (source, target, at) in enumerate(
            ((wq_hbm, wq_ref, g), (wkv_hbm, wkv_ref, g), (wkv_hbm, wkv_ref, inner + g))
        ):
            cols = slice(at, at + pair_lanes)
            sem = sems.at[len(copies) + 3 * (g // pair_lanes) + part]
            weight_copies.setdefault(g, []).append(
                pltpu.make_async_copy(source.at[:, cols], target.at[:, cols], sem)
            )
    for copy in copies + sum(weight_copies.values(), []):
        copy.start()
    mid_sum[...] = jnp.zeros(mid_sum.shape, F32)
    side_sum[...] = jnp.zeros(side_sum.shape, F32)
    for row in range(0, tile_rows, HALO):
        rows = slice(row, row + HALO)
        pair = (cols_1_ref[rows].astype(F32), cols_2_ref[rows].astype(F32))
        pair = (jnp.where(col_even, *pair), jnp.where(col_even, *pair[::-1]))
        held[HALO + row : 2 * HALO + row, WIN : 2 * WIN] = jnp.concatenate(pair, 1).astype(BF16)
    for copy in copies:
        copy.wait()
    slots = weight.shape[0]
    live = sum((weight[s] > 0).astype(jnp.int32) for s in range(slots))
    first = lax.broadcasted_iota(jnp.int32, (cells, LANES), 1) < HD
    ones = jnp.ones((VROWS - HD, cells), BF16)

    column = lax.broadcasted_iota(jnp.int32, (1, WIN, 1), 1)
    across = lax.broadcasted_iota(jnp.int32, (cells, cells), 0)
    along = lax.broadcasted_iota(jnp.int32, (cells, cells), 1)
    diagonal = jnp.where(across == along, 1.0, 0.0)

    def one_window(slot, carry):
        top = anchor[0, slot] + HALO
        left = anchor[1, slot]
        factor = weight[slot].astype(F32)
        rows = pl.ds(top, WIN)
        in_mid = ((column >= left) & (column < left + WIN)).astype(F32)
        own = in_mid.astype(BF16)
        x = held[rows, 0:WIN] * own + held[rows, WIN : 2 * WIN] * (1 - own)
        x = x.reshape(cells, channels)

        def project(g):
            q = dot(x, wq_ref[:, g : g + 2 * LANES]).astype(BF16)
            k = dot(x, wkv_ref[:, g : g + 2 * LANES]).astype(BF16)
            v = dot(x, wkv_ref[:, inner + g : inner + g + 2 * LANES])
            return q, k, v.T.astype(BF16)

        def scores(q, k, j):
            lanes = slice(j // 2 * LANES, (j // 2 + 1) * LANES)
            own = jnp.where(first if j % 2 == 0 else ~first, q[:, lanes], jnp.zeros((), BF16))
            return dot_nt(k[:, lanes], own)

        def mix(s, v_t, g, j):
            e = jnp.exp2((s - jnp.max(s, axis=0, keepdims=True)) * SCALE).astype(BF16)
            o = dot(jnp.concatenate([v_t[j * HD : (j + 1) * HD], ones], 0), e)
            at = g + j * HD
            results_t[at : at + HD] = (o[:HD] / o[HD : HD + 1]).astype(BF16)

        later = project(0)
        for g in range(0, inner, 2 * LANES):
            q, k, v_t = later
            now = [scores(q, k, j) for j in range(4)]
            if g + 2 * LANES < inner:
                later = project(g + 2 * LANES)
            for j in range(4):
                mix(now[j], v_t, g, j)
        placed = dot_nt((diagonal * factor).astype(BF16), results_t[...]).reshape(WIN, WIN, inner)
        mid_sum[rows, :, 0:inner] += placed * in_mid
        side_sum[rows, :, 0:inner] += placed * (1.0 - in_mid)
        cover = jnp.broadcast_to(in_mid * factor, (WIN, WIN, LANES))
        mid_sum[rows, :, inner:wide] += cover
        side_sum[rows, :, inner:wide] += factor - cover
        return carry

    for copy in sum(weight_copies.values(), []):
        copy.wait()
    lax.fori_loop(0, live, one_window, 0)
    for out, rows in ((rim_1_out, rows_1), (rim_2_out, rows_2)):
        out[:, 0:WIN] = mid_sum[rows].astype(BF16)
        out[:, WIN : 2 * WIN] = side_sum[rows].astype(BF16)
    mid_out[...] = mid_sum[HALO:end].astype(BF16)

    def edges(rows):
        right, left = side_sum[rows, 0:HALO], side_sum[rows, HALO : 2 * HALO]
        return jnp.where(col_even, right, left).astype(BF16), jnp.where(col_even, left, right).astype(BF16)

    ends_1_out[0:HALO], ends_2_out[0:HALO] = edges(slice(HALO, 2 * HALO))
    ends_1_out[HALO : 2 * HALO], ends_2_out[HALO : 2 * HALO] = edges(slice(end - HALO, end))
    middle_1_out[...], middle_2_out[...] = edges(slice(2 * HALO, end - HALO))


def windows(
    even, mid, rows_1, rows_2, cols_1, cols_2, w_query, w_keyval, anchor, weight
):
    tile_rows, _, channels = mid.shape
    high = tile_rows + 2 * HALO
    inner = w_query.shape[1]
    wide = inner + LANES
    vmem = pl.BlockSpec(memory_space=pltpu.VMEM)
    smem = pl.BlockSpec(memory_space=pltpu.SMEM)
    free = pl.BlockSpec(memory_space=pl.ANY)
    rim = jax.ShapeDtypeStruct((HALO, 2 * WIN, wide), BF16)
    inside = jax.ShapeDtypeStruct((tile_rows, WIN, wide), BF16)
    ends = jax.ShapeDtypeStruct((2 * HALO, HALO, wide), BF16)
    middle = jax.ShapeDtypeStruct((tile_rows - 2 * HALO, HALO, wide), BF16)
    slots = weight.shape[0]
    cells = WIN * WIN
    return pl.pallas_call(
        windows_kernel,
        in_specs=[smem] * 3 + [free] * 3 + [vmem] * 2 + [free] * 2,
        out_specs=[vmem] * 7,
        out_shape=[rim, rim, inside, ends, ends, middle, middle],
        scratch_shapes=[
            pltpu.VMEM((high, 2 * WIN, channels), BF16),
            pltpu.VMEM(w_query.shape, BF16),
            pltpu.VMEM(w_keyval.shape, BF16),
            pltpu.VMEM((high, WIN, wide), F32),
            pltpu.VMEM((high, WIN, wide), F32),
            pltpu.VMEM((inner, cells), BF16),
            pltpu.SemaphoreType.DMA((3 + 3 * (inner // (2 * LANES)),)),
        ],
        compiler_params=params(61),
        cost_estimate=pl.CostEstimate(
            flops=8 * slots * 2 * cells * 3 * inner * (channels + 2 * cells),
            bytes_accessed=6 * channels * inner + 4 * high * WIN * channels,
            transcendentals=slots * cells * cells * inner // HD,
        ),
        name="windows",
    )(
        even, anchor, weight, mid, rows_1, rows_2, cols_1, cols_2,
        w_query, w_keyval,
    )


def settle_kernel(
    even, mid_ref, rim_1_ref, rim_2_ref, beside_ref, mask_ref, x_ref, known_ref, w_ref, base_ref, share_ref, own
):
    count, inner = own.shape
    tile_cols, tile_rows = mask_ref.shape
    cell = lax.broadcasted_iota(jnp.int32, (count, tile_rows), 0)
    row = lax.broadcasted_iota(jnp.int32, (count, tile_rows), 1)
    pick_row = jnp.where(cell >> (tile_cols.bit_length() - 1) == row, 1.0, 0.0).astype(BF16)
    in_row = dot_nt(pick_row, mask_ref[...].astype(F32).astype(BF16))
    cell = lax.broadcasted_iota(jnp.int32, (count, tile_cols), 0)
    col = lax.broadcasted_iota(jnp.int32, (count, tile_cols), 1)
    known_cell = jnp.sum(jnp.where(cell & (tile_cols - 1) == col, in_row, 0.0), axis=1, keepdims=True) == 1

    def total(lanes):
        rims = [ref[:, 0:WIN, lanes].astype(F32) for ref in (rim_1_ref, rim_2_ref)]
        lower, upper = jnp.where(even[0] == 1, *rims), jnp.where(even[0] == 1, *rims[::-1])
        middle = mid_ref[:, :, lanes].astype(F32) + beside_ref[:, :, lanes].astype(F32)
        parts = [
            middle[:HALO] + upper,
            middle[HALO : tile_rows - HALO],
            middle[tile_rows - HALO :] + lower,
        ]
        return jnp.concatenate(parts, 0).reshape(count, LANES)

    share = 1.0 / (1.0 + total(slice(inner, inner + LANES)))
    share_ref[...] = jnp.where(known_cell, 0.0, share)
    for g in range(0, inner, LANES):
        lanes = slice(g, g + LANES)
        own[:, lanes] = (total(lanes) * share).astype(BF16)
    width = 2 * LANES
    for c in range(0, base_ref.shape[1], width):
        cols = slice(c, c + width)
        y = x_ref[:, cols].astype(F32) + dot(own[...], w_ref[:, cols])
        base_ref[:, cols] = jnp.where(known_cell, known_ref[:, cols].astype(F32), y)


def settle(even, mid, rim_1, rim_2, beside, mask, x, known, w_out):
    tile_rows, tile_cols, wide = mid.shape
    count, channels = x.shape
    vmem = pl.BlockSpec(memory_space=pltpu.VMEM)
    return pl.pallas_call(
        settle_kernel,
        in_specs=[pl.BlockSpec(memory_space=pltpu.SMEM)] + [vmem] * 8,
        out_specs=[vmem] * 2,
        out_shape=[
            jax.ShapeDtypeStruct((count, channels), F32),
            jax.ShapeDtypeStruct((count, LANES), F32),
        ],
        scratch_shapes=[pltpu.VMEM((count, wide - LANES), BF16)],
        compiler_params=params(),
        cost_estimate=pl.CostEstimate(
            flops=2**17 * count * wide, bytes_accessed=12 * count * wide, transcendentals=0
        ),
        name="settle",
    )(even, mid, rim_1, rim_2, beside, mask, x, known, w_out)


def blend_kernel(
    mixed_hbm, share_hbm, base_hbm, w_hbm, out_hbm, mixed_ref, share_ref, base_ref, w_ref, out_ref,
    blended, sems, out_sems,
):
    count, channels = base_ref.shape
    groups = mixed_ref.shape[1]
    width = 2 * LANES
    copies = [
        pltpu.make_async_copy(source, target, sems.at[i])
        for i, (source, target) in enumerate(
            ((mixed_hbm, mixed_ref), (share_hbm, share_ref), (w_hbm, w_ref), (base_hbm, base_ref))
        )
    ]
    for copy in copies:
        copy.start()
    back = lattice_order(count, False)
    for copy in copies[:2]:
        copy.wait()
    share = jnp.concatenate([share_ref[...]] * 2, 1)
    for g in range(0, groups, 2):
        lanes = slice(g * LANES, (g + 2) * LANES)
        mixed = jnp.concatenate([mixed_ref[:, g + j].reshape(count, LANES) for j in range(2)], 1)
        blended[:, lanes] = (dot(back, mixed) * share).astype(BF16)
    copies[2].wait()
    outs = []
    for i, c in enumerate(range(0, channels, width)):
        cols = slice(c, c + width)
        part = dot(blended[...], w_ref[:, cols])
        if i == 0:
            copies[3].wait()
        out_ref[:, cols] = (base_ref[:, cols] + part).astype(BF16)
        outs.append(
            pltpu.make_async_copy(out_ref.at[:, cols], out_hbm.at[:, cols], out_sems.at[i])
        )
        outs[-1].start()
    for copy in outs:
        copy.wait()


def blend(mixed, share, base, w_out):
    count, channels = base.shape
    inner = w_out.shape[0]
    arrays = (mixed, share, base, w_out)
    free = pl.BlockSpec(memory_space=pl.ANY)
    return pl.pallas_call(
        blend_kernel,
        in_specs=[free] * len(arrays),
        out_specs=free,
        out_shape=jax.ShapeDtypeStruct((count, channels), BF16),
        scratch_shapes=[pltpu.VMEM(a.shape, a.dtype) for a in arrays]
        + [
            pltpu.VMEM((count, channels), BF16),
            pltpu.VMEM((count, inner), BF16),
            pltpu.SemaphoreType.DMA((len(arrays),)),
            pltpu.SemaphoreType.DMA((channels // (2 * LANES),)),
        ],
        compiler_params=params(),
        cost_estimate=pl.CostEstimate(
            flops=2 * count * inner * (channels + count),
            bytes_accessed=2 * inner * channels + 6 * count * channels,
            transcendentals=0,
        ),
        name="blend",
    )(*arrays)


def exchange(pieces):
    return lax.all_to_all(pieces, ("row", "col"), split_axis=0, concat_axis=0, tiled=True)


def meet(axis, first, second):
    peers = lax.axis_size(axis)
    met = []
    for start, array in ((0, first), (1, second)):
        pairs = [(i, i + 1) for i in range(start, peers - 1, 2)]
        met.append(lax.ppermute(array, axis, pairs + [(j, i) for i, j in pairs]))
    return met


def on_device(features, known, known_mask, w_query, w_keyval, w_out, win_anchor, win_weight):
    tile_rows, tile_cols, channels = features.shape
    count = tile_rows * tile_cols
    per_sub = count // SUBS
    inner = w_query.shape[1]
    devices = lax.axis_size("row") * lax.axis_size("col")
    row_even, col_even = (lax.axis_index(axis) % 2 == 0 for axis in ("row", "col"))
    even = jnp.stack([row_even, col_even]).astype(jnp.int32)

    def swap(flag, lower, higher):
        return jnp.where(flag, higher, lower), jnp.where(flag, lower, higher)

    x = features.reshape(count, channels)

    high = tile_cols - HALO
    cols = meet(
        "col",
        *(
            lax.dynamic_slice_in_dim(features, jnp.where(flag, high, 0), HALO, axis=1)
            for flag in (col_even, ~col_even)
        ),
    )
    pieces = project(x, w_query, w_keyval).reshape(devices, per_sub, 3 * LANES)
    cols_1, cols_2, even, _ = lax.optimization_barrier((*cols, even, pieces))
    from_right, from_left = swap(col_even, cols_2, cols_1)

    def rows_of_halo(rows):
        return jnp.concatenate([features[rows], from_right[rows], from_left[rows]], 1)

    first_rows, last_rows = rows_of_halo(slice(0, HALO)), rows_of_halo(slice(tile_rows - HALO, None))
    rows_1, rows_2 = meet("row", *swap(row_even, first_rows, last_rows))

    gathered = exchange(pieces).reshape(devices * per_sub, 3 * LANES)

    rim_1, rim_2, inside, ends_1, ends_2, middle_1, middle_2 = windows(
        even,
        features,
        rows_1,
        rows_2,
        cols_1,
        cols_2,
        w_query,
        w_keyval,
        win_anchor.reshape(-1, 2).T,
        win_weight.reshape(-1),
    )
    rim_1, rim_2 = meet("row", rim_1, rim_2)
    middle_1, middle_2 = meet("col", middle_1, middle_2)
    half = lattice_attend(0, gathered)
    half, rim_1, rim_2, middle_1, middle_2 = lax.optimization_barrier(
        (half, rim_1, rim_2, middle_1, middle_2)
    )
    below, above = swap(row_even, rim_2, rim_1)

    def with_rims(ends, cols):
        rims = jnp.concatenate([above[:, cols], below[:, cols]], 0)
        return ends.astype(F32) + rims.astype(F32)

    right, left = slice(WIN, WIN + HALO), slice(WIN + HALO, 2 * WIN)
    ends_1 = jnp.where(col_even, with_rims(ends_1, right), with_rims(ends_1, left)).astype(BF16)
    ends_2 = jnp.where(col_even, with_rims(ends_2, left), with_rims(ends_2, right)).astype(BF16)
    gathered, half, ends_1, ends_2 = lax.optimization_barrier((gathered, half, ends_1, ends_2))
    ends_1, ends_2 = meet("col", ends_1, ends_2)
    mixed = lattice_attend(1, gathered, half)
    mixed, ends_1, ends_2 = lax.optimization_barrier((mixed, ends_1, ends_2))
    returned = exchange(mixed.reshape(devices, per_sub, LANES))
    ends = jnp.concatenate(swap(col_even, ends_1, ends_2), 1)
    middle = jnp.concatenate(swap(col_even, middle_1, middle_2), 1)
    arrived = jnp.concatenate([ends[:HALO], middle, ends[HALO:]], 0)
    base, share = settle(
        even, inside, rim_1, rim_2, arrived, known_mask.T, x, known.reshape(count, channels), w_out
    )
    returned = returned.reshape(SUBS, devices // SUBS, per_sub, LANES)
    out = blend(returned, share, base, w_out)
    return out.reshape(tile_rows, tile_cols, channels)


def solution(mesh):
    in_specs = (
        P("row", "col", None),
        P("row", "col", None),
        P("row", "col"),
        P(),
        P(),
        P(),
        P("row", "col", None, None),
        P("row", "col", None),
    )
    out_specs = P("row", "col", None)
    return jax.shard_map(
        on_device, mesh=mesh, in_specs=in_specs, out_specs=out_specs, check_vma=False
    )
```

```python
import functools
import math

import jax
import jax.numpy as jnp
from jax import lax
from jax.experimental import pallas as pl
from jax.experimental.pallas import tpu as pltpu
from jax.sharding import PartitionSpec as P

HD = 64
STRIDE = 4
WIN = 16
HALO = 8
SUBS = STRIDE * STRIDE
LANES = 128
SCALE = HD**-0.5 * math.log2(math.e)
FREE_RANGE = 100.0
VROWS = 80
QBLOCK = 2048
KBLOCK = 256
QPART = 256
AHEAD = 8
BF16 = jnp.bfloat16
F32 = jnp.float32


def dot(a, b):
    return jnp.dot(a, b, preferred_element_type=F32)


def dot_nt(a, b):
    return lax.dot_general(a, b, (((1,), (1,)), ((), ())), preferred_element_type=F32)


def whole(shape):
    return pl.BlockSpec(shape, lambda *_: (0,) * len(shape), pipeline_mode=pl.Buffered(1))


def params(mebibytes=63):
    return pltpu.CompilerParams(vmem_limit_bytes=mebibytes * 2**20)


def lattice_order(count, by_row):
    lattice = lax.broadcasted_iota(jnp.int32, (count, count), 0 if by_row else 1)
    cell = lax.broadcasted_iota(jnp.int32, (count, count), 1 if by_row else 0)
    per_sub, tile_cols = count // SUBS, 16
    across = tile_cols // STRIDE

    def split(index, size):
        return index >> (size.bit_length() - 1), index & (size - 1)

    sub, place = split(lattice, per_sub)
    sub_row, sub_col = split(sub, STRIDE)
    place_row, place_col = split(place, across)
    row = place_row * STRIDE + sub_row
    col = place_col * STRIDE + sub_col
    return jnp.where(cell == row * tile_cols + col, 1.0, 0.0).astype(BF16)


def project_kernel(
    x_hbm, wq_hbm, wkv_hbm, out_hbm, x_ref, wq_ref, wkv_ref, ordered, queries, out_ref, sems,
    out_sems,
):
    count, channels = x_ref.shape
    inner = wq_ref.shape[1]
    width = 2 * LANES
    x_copy = pltpu.make_async_copy(x_hbm, x_ref, sems.at[0])
    x_copy.start()
    weight_copies = [
        pltpu.make_async_copy(source, target, sems.at[1 + i])
        for i, (source, target) in enumerate(((wq_hbm, wq_ref), (wkv_hbm, wkv_ref)))
    ]
    for copy in weight_copies:
        copy.start()
    order = lattice_order(count, True)
    x_copy.wait()
    ordered[...] = dot(order, x_ref[...]).astype(BF16)
    weight_copies[0].wait()
    for c in range(0, inner, width):
        queries[:, c : c + width] = dot(ordered[...], wq_ref[:, c : c + width])
    weight_copies[1].wait()
    leaving = []
    for i, c in enumerate(range(0, inner, width)):
        q = queries[:, c : c + width]
        k = dot(ordered[...], wkv_ref[:, c : c + width])
        v = dot(ordered[...], wkv_ref[:, inner + c : inner + c + width])
        for g in range(2):
            at = g * LANES
            parts = [
                jnp.concatenate([q[:, at : at + HD], k[:, at : at + HD]], 1),
                v[:, at : at + LANES],
                jnp.concatenate([q[:, at + HD : at + LANES], k[:, at + HD : at + LANES]], 1),
            ]
            for j, part in enumerate(parts):
                out_ref[:, 2 * i + g, :, j * LANES : (j + 1) * LANES] = part.astype(BF16).reshape(
                    SUBS, count // SUBS, LANES
                )
        groups = slice(2 * i, 2 * i + 2)
        leaving.append(
            pltpu.make_async_copy(out_ref.at[:, groups], out_hbm.at[:, groups], out_sems.at[i])
        )
        leaving[-1].start()
    for copy in leaving:
        copy.wait()


def project(x, w_query, w_keyval):
    count, channels = x.shape
    inner = w_query.shape[1]
    groups = inner // LANES
    shape = (SUBS, groups, count // SUBS, 3 * LANES)
    free = pl.BlockSpec(memory_space=pl.ANY)
    return pl.pallas_call(
        project_kernel,
        in_specs=[free] * 3,
        out_specs=free,
        out_shape=jax.ShapeDtypeStruct(shape, BF16),
        scratch_shapes=[
            pltpu.VMEM(x.shape, BF16),
            pltpu.VMEM(w_query.shape, BF16),
            pltpu.VMEM(w_keyval.shape, BF16),
            pltpu.VMEM(x.shape, BF16),
            pltpu.VMEM((count, inner), F32),
            pltpu.VMEM(shape, BF16),
            pltpu.SemaphoreType.DMA((3,)),
            pltpu.SemaphoreType.DMA((groups // 2,)),
        ],
        compiler_params=params(61),
        cost_estimate=pl.CostEstimate(
            flops=2 * count * channels * 3 * inner,
            bytes_accessed=2 * (3 * channels * inner + count * channels + 3 * count * inner),
            transcendentals=0,
        ),
        name="project",
    )(x, w_query, w_keyval)


def lattice_kernel(head, qk_ref, v_ref, *refs):
    if head == 0:
        o_ref, queries_t, values_t, free = refs
    else:
        other_ref, o_ref, queries_t, values_t, free = refs
    count = qk_ref.shape[0]
    block = o_ref.shape[1 - head]
    step = pl.program_id(0)

    @pl.when(step == 0)
    def _():
        row = lax.broadcasted_iota(jnp.int32, (LANES, LANES), 0)
        lane = lax.broadcasted_iota(jnp.int32, (LANES, LANES), 1)
        to_keys = jnp.where(row == lane + HD, 1.0, 0.0).astype(BF16)
        queries_t[...] = dot_nt(to_keys, qk_ref[...]).astype(BF16)
        own = (row[:HD] + head * HD == lane[:HD]).astype(F32).astype(BF16)
        values_t[0:HD] = dot_nt(own, v_ref[...]).astype(BF16)
        squares = qk_ref[...].astype(F32)
        squares = (squares * squares).astype(BF16)
        halves = ((row[:VROWS - HD] < 8) == (lane[:VROWS - HD] < HD)).astype(F32).astype(BF16)
        norms = dot_nt(halves, squares)
        bound = jnp.max(norms[:8]) * jnp.max(norms[8:]) * 1.02
        free[0] = (bound * (SCALE * SCALE) <= FREE_RANGE * FREE_RANGE).astype(jnp.int32)
        values_t[HD:VROWS] = jnp.ones((VROWS - HD, count), BF16)

    cols = pl.ds(pl.multiple_of(step * block, block), block)

    def finish(total):
        out = total[:HD] / total[HD : HD + 1]
        if head == 0:
            o_ref[...] = out.astype(BF16)
        else:
            o_ref[...] = jnp.concatenate([other_ref[...].astype(F32), out], 0).T.astype(BF16)

    @pl.when(free[0] == 1)
    def _():
        parts = block // QPART
        items = [(c, j) for c in range(0, count, KBLOCK) for j in range(parts)]
        queries = [
            queries_t[:, pl.ds(pl.multiple_of(step * block + j * QPART, QPART), QPART)]
            for j in range(parts)
        ]

        def score(i):
            c, j = items[i]
            return dot(qk_ref[c : c + KBLOCK, :], queries[j])

        totals, sums = [None] * parts, [None] * parts
        ahead = [score(i) for i in range(AHEAD)]
        for i, (c, j) in enumerate(items):
            now = ahead.pop(0)
            if i + AHEAD < len(items):
                ahead.append(score(i + AHEAD))
            weights = jnp.exp2(now * SCALE)
            part = dot(values_t[0:HD, c : c + KBLOCK], weights.astype(BF16))
            total = jnp.sum(weights.reshape(KBLOCK // 8, 8, QPART), axis=0)
            totals[j] = part if totals[j] is None else totals[j] + part
            sums[j] = total if sums[j] is None else sums[j] + total
        sums = jnp.sum(jnp.concatenate(sums, 1), axis=0, keepdims=True)
        finish(jnp.concatenate([jnp.concatenate(totals, 1), jnp.broadcast_to(sums, (VROWS - HD, block))], 0))

    @pl.when(free[0] == 0)
    def _():
        chunks = count // KBLOCK
        q = queries_t[:, cols]

        def score(c):
            return dot(qk_ref[pl.ds(pl.multiple_of(c * KBLOCK, KBLOCK), KBLOCK), :], q)

        def top(c, m):
            return jnp.maximum(m, jnp.max(score(c), axis=0, keepdims=True))

        m = lax.fori_loop(0, chunks, top, jnp.full((1, block), -jnp.inf, F32))

        def add(c, total):
            weights = jnp.exp2((score(c) - m) * SCALE).astype(BF16)
            rows = pl.ds(pl.multiple_of(c * KBLOCK, KBLOCK), KBLOCK)
            return total + dot(values_t[:, rows], weights)

        finish(lax.fori_loop(0, chunks, add, jnp.zeros((VROWS, block), F32)))


def lattice_attend(head, x, other=None):
    count = x.shape[0]
    in_specs = [
        pl.BlockSpec((count, LANES), lambda i: (0, 2 * head), pipeline_mode=pl.Buffered(1)),
        pl.BlockSpec((count, LANES), lambda i: (0, 1), pipeline_mode=pl.Buffered(1)),
    ]
    args = [x, x]
    if head == 0:
        out_spec = pl.BlockSpec((HD, QBLOCK), lambda i: (0, i))
        out_shape = (HD, count)
    else:
        in_specs.append(pl.BlockSpec((HD, QBLOCK), lambda i: (0, i)))
        args.append(other)
        out_spec = pl.BlockSpec((QBLOCK, LANES), lambda i: (i, 0))
        out_shape = (count, LANES)
    return pl.pallas_call(
        functools.partial(lattice_kernel, head),
        grid=(count // QBLOCK,),
        in_specs=in_specs,
        out_specs=out_spec,
        out_shape=jax.ShapeDtypeStruct(out_shape, BF16),
        scratch_shapes=[
            pltpu.VMEM((LANES, count), BF16),
            pltpu.VMEM((VROWS, count), BF16),
            pltpu.SMEM((1,), jnp.int32),
        ],
        compiler_params=params(61),
        cost_estimate=pl.CostEstimate(
            flops=4 * 4 * count * count * HD,
            bytes_accessed=6 * count * LANES,
            transcendentals=count * count,
        ),
        name="lattice_attend_" + str(head),
    )(*args)


def windows_kernel(
    even, anchor, weight, mid_hbm, rows_1_hbm, rows_2_hbm, cols_1_ref, cols_2_ref,
    wq_hbm, wkv_hbm, rim_1_out, rim_2_out, mid_out, ends_1_out, ends_2_out,
    middle_1_out, middle_2_out, held, wq_ref, wkv_ref, mid_sum, side_sum, results_t, sems,
):
    channels, inner = wq_ref.shape
    cells = WIN * WIN
    wide = inner + LANES
    tile_rows = mid_hbm.shape[0]
    end = tile_rows + HALO
    pair_lanes = 2 * LANES
    row_even, col_even = even[0] == 1, even[1] == 1
    rows_1 = pl.ds(jnp.where(row_even, end, 0), HALO)
    rows_2 = pl.ds(jnp.where(row_even, 0, end), HALO)
    copies = [
        pltpu.make_async_copy(source, target, sems.at[i])
        for i, (source, target) in enumerate(
            (
                (mid_hbm, held.at[HALO:end, 0:WIN]),
                (rows_1_hbm, held.at[rows_1]),
                (rows_2_hbm, held.at[rows_2]),
            )
        )
    ]
    weight_copies = {}
    for g in range(0, inner, pair_lanes):
        for part, (source, target, at) in enumerate(
            ((wq_hbm, wq_ref, g), (wkv_hbm, wkv_ref, g), (wkv_hbm, wkv_ref, inner + g))
        ):
            cols = slice(at, at + pair_lanes)
            sem = sems.at[len(copies) + 3 * (g // pair_lanes) + part]
            weight_copies.setdefault(g, []).append(
                pltpu.make_async_copy(source.at[:, cols], target.at[:, cols], sem)
            )
    for copy in copies + sum(weight_copies.values(), []):
        copy.start()
    mid_sum[...] = jnp.zeros(mid_sum.shape, F32)
    side_sum[...] = jnp.zeros(side_sum.shape, F32)
    for row in range(0, tile_rows, HALO):
        rows = slice(row, row + HALO)
        pair = (cols_1_ref[rows].astype(F32), cols_2_ref[rows].astype(F32))
        pair = (jnp.where(col_even, *pair), jnp.where(col_even, *pair[::-1]))
        held[HALO + row : 2 * HALO + row, WIN : 2 * WIN] = jnp.concatenate(pair, 1).astype(BF16)
    for copy in copies:
        copy.wait()
    slots = weight.shape[0]
    live = sum((weight[s] > 0).astype(jnp.int32) for s in range(slots))
    first = lax.broadcasted_iota(jnp.int32, (cells, LANES), 1) < HD
    ones = jnp.ones((VROWS - HD, cells), BF16)

    column = lax.broadcasted_iota(jnp.int32, (1, WIN, 1), 1)
    across = lax.broadcasted_iota(jnp.int32, (cells, cells), 0)
    along = lax.broadcasted_iota(jnp.int32, (cells, cells), 1)
    diagonal = jnp.where(across == along, 1.0, 0.0)

    def one_window(slot, carry):
        top = anchor[0, slot] + HALO
        left = anchor[1, slot]
        factor = weight[slot].astype(F32)
        rows = pl.ds(top, WIN)
        in_mid = ((column >= left) & (column < left + WIN)).astype(F32)
        own = in_mid.astype(BF16)
        x = held[rows, 0:WIN] * own + held[rows, WIN : 2 * WIN] * (1 - own)
        x = x.reshape(cells, channels)

        def project(g):
            q = dot(x, wq_ref[:, g : g + 2 * LANES]).astype(BF16)
            k = dot(x, wkv_ref[:, g : g + 2 * LANES]).astype(BF16)
            v = dot(x, wkv_ref[:, inner + g : inner + g + 2 * LANES])
            return q, k, v.T.astype(BF16)

        def scores(q, k, j):
            lanes = slice(j // 2 * LANES, (j // 2 + 1) * LANES)
            own = jnp.where(first if j % 2 == 0 else ~first, q[:, lanes], jnp.zeros((), BF16))
            return dot_nt(k[:, lanes], own)

        def mix(s, v_t, g, j):
            e = jnp.exp2((s - jnp.max(s, axis=0, keepdims=True)) * SCALE).astype(BF16)
            o = dot(jnp.concatenate([v_t[j * HD : (j + 1) * HD], ones], 0), e)
            at = g + j * HD
            results_t[at : at + HD] = (o[:HD] / o[HD : HD + 1]).astype(BF16)

        later = project(0)
        for g in range(0, inner, 2 * LANES):
            q, k, v_t = later
            now = [scores(q, k, j) for j in range(4)]
            if g + 2 * LANES < inner:
                later = project(g + 2 * LANES)
            for j in range(4):
                mix(now[j], v_t, g, j)
        placed = dot_nt((diagonal * factor).astype(BF16), results_t[...]).reshape(WIN, WIN, inner)
        mid_sum[rows, :, 0:inner] += placed * in_mid
        side_sum[rows, :, 0:inner] += placed * (1.0 - in_mid)
        cover = jnp.broadcast_to(in_mid * factor, (WIN, WIN, LANES))
        mid_sum[rows, :, inner:wide] += cover
        side_sum[rows, :, inner:wide] += factor - cover
        return carry

    for copy in sum(weight_copies.values(), []):
        copy.wait()
    lax.fori_loop(0, live, one_window, 0)
    for out, rows in ((rim_1_out, rows_1), (rim_2_out, rows_2)):
        out[:, 0:WIN] = mid_sum[rows].astype(BF16)
        out[:, WIN : 2 * WIN] = side_sum[rows].astype(BF16)
    mid_out[...] = mid_sum[HALO:end].astype(BF16)

    def edges(rows):
        right, left = side_sum[rows, 0:HALO], side_sum[rows, HALO : 2 * HALO]
        return jnp.where(col_even, right, left).astype(BF16), jnp.where(col_even, left, right).astype(BF16)

    ends_1_out[0:HALO], ends_2_out[0:HALO] = edges(slice(HALO, 2 * HALO))
    ends_1_out[HALO : 2 * HALO], ends_2_out[HALO : 2 * HALO] = edges(slice(end - HALO, end))
    middle_1_out[...], middle_2_out[...] = edges(slice(2 * HALO, end - HALO))


def windows(
    even, mid, rows_1, rows_2, cols_1, cols_2, w_query, w_keyval, anchor, weight
):
    tile_rows, _, channels = mid.shape
    high = tile_rows + 2 * HALO
    inner = w_query.shape[1]
    wide = inner + LANES
    vmem = pl.BlockSpec(memory_space=pltpu.VMEM)
    smem = pl.BlockSpec(memory_space=pltpu.SMEM)
    free = pl.BlockSpec(memory_space=pl.ANY)
    rim = jax.ShapeDtypeStruct((HALO, 2 * WIN, wide), BF16)
    inside = jax.ShapeDtypeStruct((tile_rows, WIN, wide), BF16)
    ends = jax.ShapeDtypeStruct((2 * HALO, HALO, wide), BF16)
    middle = jax.ShapeDtypeStruct((tile_rows - 2 * HALO, HALO, wide), BF16)
    slots = weight.shape[0]
    cells = WIN * WIN
    return pl.pallas_call(
        windows_kernel,
        in_specs=[smem] * 3 + [free] * 3 + [vmem] * 2 + [free] * 2,
        out_specs=[vmem] * 7,
        out_shape=[rim, rim, inside, ends, ends, middle, middle],
        scratch_shapes=[
            pltpu.VMEM((high, 2 * WIN, channels), BF16),
            pltpu.VMEM(w_query.shape, BF16),
            pltpu.VMEM(w_keyval.shape, BF16),
            pltpu.VMEM((high, WIN, wide), F32),
            pltpu.VMEM((high, WIN, wide), F32),
            pltpu.VMEM((inner, cells), BF16),
            pltpu.SemaphoreType.DMA((3 + 3 * (inner // (2 * LANES)),)),
        ],
        compiler_params=params(61),
        cost_estimate=pl.CostEstimate(
            flops=8 * slots * 2 * cells * 3 * inner * (channels + 2 * cells),
            bytes_accessed=6 * channels * inner + 4 * high * WIN * channels,
            transcendentals=slots * cells * cells * inner // HD,
        ),
        name="windows",
    )(
        even, anchor, weight, mid, rows_1, rows_2, cols_1, cols_2,
        w_query, w_keyval,
    )


def settle_kernel(
    even, mid_ref, rim_1_ref, rim_2_ref, beside_ref, mask_ref, x_ref, known_ref, w_ref, base_ref, share_ref, own
):
    count, inner = own.shape
    tile_cols, tile_rows = mask_ref.shape
    cell = lax.broadcasted_iota(jnp.int32, (count, tile_rows), 0)
    row = lax.broadcasted_iota(jnp.int32, (count, tile_rows), 1)
    pick_row = jnp.where(cell >> (tile_cols.bit_length() - 1) == row, 1.0, 0.0).astype(BF16)
    in_row = dot_nt(pick_row, mask_ref[...].astype(F32).astype(BF16))
    cell = lax.broadcasted_iota(jnp.int32, (count, tile_cols), 0)
    col = lax.broadcasted_iota(jnp.int32, (count, tile_cols), 1)
    known_cell = jnp.sum(jnp.where(cell & (tile_cols - 1) == col, in_row, 0.0), axis=1, keepdims=True) == 1

    def total(lanes):
        rims = [ref[:, 0:WIN, lanes].astype(F32) for ref in (rim_1_ref, rim_2_ref)]
        lower, upper = jnp.where(even[0] == 1, *rims), jnp.where(even[0] == 1, *rims[::-1])
        middle = mid_ref[:, :, lanes].astype(F32) + beside_ref[:, :, lanes].astype(F32)
        parts = [
            middle[:HALO] + upper,
            middle[HALO : tile_rows - HALO],
            middle[tile_rows - HALO :] + lower,
        ]
        return jnp.concatenate(parts, 0).reshape(count, LANES)

    share = 1.0 / (1.0 + total(slice(inner, inner + LANES)))
    share_ref[...] = jnp.where(known_cell, 0.0, share)
    for g in range(0, inner, LANES):
        lanes = slice(g, g + LANES)
        own[:, lanes] = (total(lanes) * share).astype(BF16)
    width = 2 * LANES
    for c in range(0, base_ref.shape[1], width):
        cols = slice(c, c + width)
        y = x_ref[:, cols].astype(F32) + dot(own[...], w_ref[:, cols])
        base_ref[:, cols] = jnp.where(known_cell, known_ref[:, cols].astype(F32), y).astype(BF16)


def settle(even, mid, rim_1, rim_2, beside, mask, x, known, w_out):
    tile_rows, tile_cols, wide = mid.shape
    count, channels = x.shape
    vmem = pl.BlockSpec(memory_space=pltpu.VMEM)
    return pl.pallas_call(
        settle_kernel,
        in_specs=[pl.BlockSpec(memory_space=pltpu.SMEM)] + [vmem] * 8,
        out_specs=[vmem] * 2,
        out_shape=[
            jax.ShapeDtypeStruct((count, channels), BF16),
            jax.ShapeDtypeStruct((count, LANES), F32),
        ],
        scratch_shapes=[pltpu.VMEM((count, wide - LANES), BF16)],
        compiler_params=params(),
        cost_estimate=pl.CostEstimate(
            flops=2**17 * count * wide, bytes_accessed=12 * count * wide, transcendentals=0
        ),
        name="settle",
    )(even, mid, rim_1, rim_2, beside, mask, x, known, w_out)


def blend_kernel(
    mixed_hbm, share_hbm, base_hbm, w_hbm, out_hbm, mixed_ref, share_ref, base_ref, w_ref, out_ref,
    blended, sems, out_sems,
):
    count, channels = base_ref.shape
    groups = mixed_ref.shape[1]
    width = 2 * LANES
    copies = [
        pltpu.make_async_copy(source, target, sems.at[i])
        for i, (source, target) in enumerate(
            ((mixed_hbm, mixed_ref), (share_hbm, share_ref), (w_hbm, w_ref), (base_hbm, base_ref))
        )
    ]
    for copy in copies:
        copy.start()
    back = lattice_order(count, False)
    for copy in copies[:2]:
        copy.wait()
    share = jnp.concatenate([share_ref[...]] * 2, 1)
    for g in range(0, groups, 2):
        lanes = slice(g * LANES, (g + 2) * LANES)
        mixed = jnp.concatenate([mixed_ref[:, g + j].reshape(count, LANES) for j in range(2)], 1)
        blended[:, lanes] = (dot(back, mixed) * share).astype(BF16)
    copies[2].wait()
    outs = []
    for i, c in enumerate(range(0, channels, width)):
        cols = slice(c, c + width)
        part = dot(blended[...], w_ref[:, cols])
        if i == 0:
            copies[3].wait()
        out_ref[:, cols] = (base_ref[:, cols].astype(F32) + part).astype(BF16)
        outs.append(
            pltpu.make_async_copy(out_ref.at[:, cols], out_hbm.at[:, cols], out_sems.at[i])
        )
        outs[-1].start()
    for copy in outs:
        copy.wait()


def blend(mixed, share, base, w_out):
    count, channels = base.shape
    inner = w_out.shape[0]
    arrays = (mixed, share, base, w_out)
    free = pl.BlockSpec(memory_space=pl.ANY)
    return pl.pallas_call(
        blend_kernel,
        in_specs=[free] * len(arrays),
        out_specs=free,
        out_shape=jax.ShapeDtypeStruct((count, channels), BF16),
        scratch_shapes=[pltpu.VMEM(a.shape, a.dtype) for a in arrays]
        + [
            pltpu.VMEM((count, channels), BF16),
            pltpu.VMEM((count, inner), BF16),
            pltpu.SemaphoreType.DMA((len(arrays),)),
            pltpu.SemaphoreType.DMA((channels // (2 * LANES),)),
        ],
        compiler_params=params(),
        cost_estimate=pl.CostEstimate(
            flops=2 * count * inner * (channels + count),
            bytes_accessed=2 * inner * channels + 6 * count * channels,
            transcendentals=0,
        ),
        name="blend",
    )(*arrays)


def exchange(pieces):
    return lax.all_to_all(pieces, ("row", "col"), split_axis=0, concat_axis=0, tiled=True)


def meet(axis, first, second):
    peers = lax.axis_size(axis)
    met = []
    for start, array in ((0, first), (1, second)):
        pairs = [(i, i + 1) for i in range(start, peers - 1, 2)]
        met.append(lax.ppermute(array, axis, pairs + [(j, i) for i, j in pairs]))
    return met


def on_device(features, known, known_mask, w_query, w_keyval, w_out, win_anchor, win_weight):
    tile_rows, tile_cols, channels = features.shape
    count = tile_rows * tile_cols
    per_sub = count // SUBS
    inner = w_query.shape[1]
    devices = lax.axis_size("row") * lax.axis_size("col")
    row_even, col_even = (lax.axis_index(axis) % 2 == 0 for axis in ("row", "col"))
    even = jnp.stack([row_even, col_even]).astype(jnp.int32)

    def swap(flag, lower, higher):
        return jnp.where(flag, higher, lower), jnp.where(flag, lower, higher)

    x = features.reshape(count, channels)

    high = tile_cols - HALO
    cols = meet(
        "col",
        *(
            lax.dynamic_slice_in_dim(features, jnp.where(flag, high, 0), HALO, axis=1)
            for flag in (col_even, ~col_even)
        ),
    )
    pieces = project(x, w_query, w_keyval).reshape(devices, per_sub, 3 * LANES)
    cols_1, cols_2, even, _ = lax.optimization_barrier((*cols, even, pieces))
    from_right, from_left = swap(col_even, cols_2, cols_1)

    def rows_of_halo(rows):
        return jnp.concatenate([features[rows], from_right[rows], from_left[rows]], 1)

    first_rows, last_rows = rows_of_halo(slice(0, HALO)), rows_of_halo(slice(tile_rows - HALO, None))
    rows_1, rows_2 = meet("row", *swap(row_even, first_rows, last_rows))

    gathered = exchange(pieces).reshape(devices * per_sub, 3 * LANES)

    rim_1, rim_2, inside, ends_1, ends_2, middle_1, middle_2 = windows(
        even,
        features,
        rows_1,
        rows_2,
        cols_1,
        cols_2,
        w_query,
        w_keyval,
        win_anchor.reshape(-1, 2).T,
        win_weight.reshape(-1),
    )
    rim_1, rim_2 = meet("row", rim_1, rim_2)
    middle_1, middle_2 = meet("col", middle_1, middle_2)
    half = lattice_attend(0, gathered)
    half, rim_1, rim_2, middle_1, middle_2 = lax.optimization_barrier(
        (half, rim_1, rim_2, middle_1, middle_2)
    )
    below, above = swap(row_even, rim_2, rim_1)

    def with_rims(ends, cols):
        rims = jnp.concatenate([above[:, cols], below[:, cols]], 0)
        return ends.astype(F32) + rims.astype(F32)

    right, left = slice(WIN, WIN + HALO), slice(WIN + HALO, 2 * WIN)
    ends_1 = jnp.where(col_even, with_rims(ends_1, right), with_rims(ends_1, left)).astype(BF16)
    ends_2 = jnp.where(col_even, with_rims(ends_2, left), with_rims(ends_2, right)).astype(BF16)
    gathered, half, ends_1, ends_2 = lax.optimization_barrier((gathered, half, ends_1, ends_2))
    ends_1, ends_2 = meet("col", ends_1, ends_2)
    mixed = lattice_attend(1, gathered, half)
    mixed, ends_1, ends_2 = lax.optimization_barrier((mixed, ends_1, ends_2))
    returned = exchange(mixed.reshape(devices, per_sub, LANES))
    ends = jnp.concatenate(swap(col_even, ends_1, ends_2), 1)
    middle = jnp.concatenate(swap(col_even, middle_1, middle_2), 1)
    arrived = jnp.concatenate([ends[:HALO], middle, ends[HALO:]], 0)
    base, share = settle(
        even, inside, rim_1, rim_2, arrived, known_mask.T, x, known.reshape(count, channels), w_out
    )
    returned = returned.reshape(SUBS, devices // SUBS, per_sub, LANES)
    out = blend(returned, share, base, w_out)
    return out.reshape(tile_rows, tile_cols, channels)


def solution(mesh):
    in_specs = (
        P("row", "col", None),
        P("row", "col", None),
        P("row", "col"),
        P(),
        P(),
        P(),
        P("row", "col", None, None),
        P("row", "col", None),
    )
    out_specs = P("row", "col", None)
    return jax.shard_map(
        on_device, mesh=mesh, in_specs=in_specs, out_specs=out_specs, check_vma=False
    )
```
